128 devices in a mesh: ia: 8 (over z, y_hi), ja: 8 (over x, y_lo), sa: 2 (over core).
Axes of the slice: x: 4, y: 4 (y_hi: 2, y_lo: 2; y = y_hi * 2 + y_lo), z: 4, core: 2. Of those that a mesh axis runs over, the one named last changes fastest.
Arguments:
- alignment_features: bfloat16 [128, 1024, 256], P('sa', 'ia'), may hold values from -90 to 90
- norm_gain_vector: float32 [256], replicated, may hold values from 0.25 to 1.75
- norm_offset_vector: float32 [256], replicated, may hold values from -1.8 to 1.8
- projection_weight: bfloat16 [256, 64], replicated, may hold values from -0.75 to 0.75
- output_weight: bfloat16 [1024, 128], replicated, may hold values from -0.1875 to 0.1875
- output_bias: float32 [128], replicated, may hold values from -1.8 to 1.8
- pair_update_cotangent: bfloat16 [1024, 1024, 128], P(('ia', 'sa'), 'ja'), may hold values from -6 to 6
Outputs:
- pair_update_result: bfloat16 [1024, 1024, 128], P(('ia', 'sa'), 'ja')
- alignment_gradient: bfloat16 [128, 1024, 256], P('sa', 'ia')
- projection_weight_gradient: float32 [256, 64], replicated
- out_weight_grad: float32 [1024, 128], replicated
- out_bias_grad: float32 [128], replicated
The draws below stay inside these ranges and needn't reach their ends.
All inputs are finite; a program needn't handle non-finite values.
Results may differ from the reference program's by a relative error of at most 0.025.
Values may be sent and summed in bfloat16 or wider, within the bound.
No kernel may reach another device: no remote copies, remote signals or barrier semaphores. Data moves between devices by JAX's collectives and lax.ppermute only.
A program may use at most 128 MiB of HBM per device.

```python
import math
import jax
import jax.numpy as jnp
from jax import lax

CM = 256
PROJECT_CHANNELS = 32
PAIR_WIDTH = 128
S = 128
RESIDUE_COUNT = 1024


def draw_alignment_features(key, part):
    key = jax.random.fold_in(key, 7)
    subkeys = jax.random.split(key, 4)
    channel_scale = jnp.exp(jax.random.uniform(subkeys[1], (1, 1, CM), jnp.float32, jnp.log(0.5), jnp.log(5.0)))
    row_shift = jnp.clip(0.5 * jax.random.normal(subkeys[2], (S, RESIDUE_COUNT, 1), jnp.float32), -1.5, 1.5)
    row_scale = jnp.exp(jax.random.uniform(subkeys[0], (S, RESIDUE_COUNT, 1), jnp.float32, jnp.log(0.4), jnp.log(4.0)))
    base_values = jnp.clip(jax.random.normal(subkeys[3], (S, RESIDUE_COUNT, CM), jnp.float32), -4.0, 4.0)
    return (row_scale * (base_values * channel_scale + row_shift)).astype(jnp.bfloat16)


def level_of(stream_key, dims, pieces, low, top_value):
    gain, own = 1.0, jax.random.fold_in(stream_key, 6)
    for position, shards_of in pieces:
        heights = jnp.exp(jax.random.uniform(jax.random.fold_in(own, position), (shards_of,), jnp.float32, low / len(pieces), top_value / len(pieces)))
        gain = gain * jnp.repeat(heights, dims[position] // shards_of).reshape([-1 if axis == position else 1 for axis in range(len(dims))])
    return gain


def noise(rng, shape, width, most, pieces=(), kind=jnp.bfloat16):
    drawn = jax.random.normal(rng, shape, jnp.float32) * width
    if len(pieces) > 0:
        drawn = level_of(rng, shape, pieces, -0.22, 0.18) * drawn
    return jnp.clip(drawn, min=-most, max=most).astype(kind)


def setup_inputs(seed: int = 0) -> dict:
    keys = jax.random.split(jax.random.key(seed), 8)
    return {
        "alignment_features": draw_alignment_features(jax.random.fold_in(keys[7], 71), 0),
        "norm_gain_vector": jnp.clip(1.0 + 0.15 * jax.random.normal(keys[1], (CM,), jnp.float32), 0.25, 1.75),
        "norm_offset_vector": noise(keys[2], (CM,), 0.3, 1.8, (), jnp.float32),
        "projection_weight": noise(keys[3], (CM, 2 * PROJECT_CHANNELS), 0.125, 0.75),
        "output_weight": noise(keys[4], (PROJECT_CHANNELS * PROJECT_CHANNELS, PAIR_WIDTH), (PROJECT_CHANNELS * PROJECT_CHANNELS) ** -0.5, 0.1875),
        "output_bias": noise(keys[5], (PAIR_WIDTH,), 0.3, 1.8, (), jnp.float32),
        "pair_update_cotangent": noise(keys[6], (RESIDUE_COUNT, RESIDUE_COUNT, PAIR_WIDTH), 1.0, 6.0, ((0, 16), (1, 8))),
    }


epsilon = 1e-05

def layer_pieces(alignment_features, norm_gain_vector, norm_offset_vector):
    value_entries = alignment_features.astype(jnp.float32)
    average = lax.optimization_barrier(jnp.mean(value_entries, axis=-1, keepdims=True))
    centred = value_entries - average
    variance = lax.optimization_barrier(jnp.mean(centred * centred, axis=-1, keepdims=True))
    inverse_deviation = lax.rsqrt(variance + epsilon)
    rescaled_rows = centred * inverse_deviation
    normalized_rows = (rescaled_rows * norm_gain_vector + norm_offset_vector).astype(jnp.bfloat16)
    return (normalized_rows, rescaled_rows, inverse_deviation)

def norm_reverse_pass(normalized_gradient, rescaled_rows, inverse_deviation):
    first_mean = lax.optimization_barrier(jnp.mean(normalized_gradient, axis=-1, keepdims=True))
    cross_mean = lax.optimization_barrier(jnp.mean(normalized_gradient * rescaled_rows, axis=-1, keepdims=True))
    return (inverse_deviation * (normalized_gradient - first_mean - rescaled_rows * cross_mean)).astype(jnp.bfloat16)

def reference(alignment_features, norm_gain_vector, norm_offset_vector, projection_weight, output_weight, output_bias, pair_update_cotangent):
    highest = lax.Precision.HIGHEST
    normalized_rows, rescaled_rows, inverse_deviation = layer_pieces(alignment_features, norm_gain_vector, norm_offset_vector)
    projected = jnp.einsum('srm,mk->skr', normalized_rows.astype(jnp.float32), projection_weight.astype(jnp.float32), precision=highest).astype(jnp.bfloat16)
    left = projected[:, :PROJECT_CHANNELS]
    right_wide = projected[:, PROJECT_CHANNELS:].astype(jnp.float32)
    weight_cube = output_weight.astype(jnp.float32).reshape(PROJECT_CHANNELS, PROJECT_CHANNELS, PAIR_WIDTH)
    inv_seqs = 1.0 / S
    block_rows = math.gcd(RESIDUE_COUNT, 16)

    def block_step(totals, block_index):
        weight_accumulated, bias_accumulated, column_total = totals
        offset = (block_index * block_rows).astype(jnp.int32)
        left_block = lax.dynamic_slice_in_dim(left, offset, block_rows, 2).astype(jnp.float32)
        cotangent = lax.dynamic_slice_in_dim(pair_update_cotangent, offset, block_rows, 0).astype(jnp.float32)
        outer_sum = jnp.einsum('sci,sdj->icdj', left_block, right_wide, precision=highest) * inv_seqs
        outer_wide = lax.optimization_barrier(outer_sum.astype(jnp.bfloat16)).astype(jnp.float32)
        pair_rows = (jnp.einsum('icdj,cde->ije', outer_wide, weight_cube, precision=highest) + output_bias).astype(jnp.bfloat16)
        weight_accumulated = weight_accumulated + jnp.einsum('icdj,ije->cde', outer_wide, cotangent, precision=highest)
        bias_accumulated = bias_accumulated + lax.optimization_barrier(jnp.sum(cotangent, axis=(0, 1)))
        grad_sum = jnp.einsum('ije,cde->icdj', cotangent, weight_cube, precision=highest)
        outer_grad = lax.optimization_barrier(grad_sum.astype(jnp.bfloat16)).astype(jnp.float32)
        left_part = jnp.einsum('icdj,sdj->sci', outer_grad, right_wide, precision=highest)
        column_total = column_total + jnp.einsum('icdj,sci->sdj', outer_grad, left_block, precision=highest)
        return ((weight_accumulated, bias_accumulated, column_total), (pair_rows, left_part))
    initial = (jnp.zeros((PROJECT_CHANNELS, PROJECT_CHANNELS, PAIR_WIDTH), jnp.float32), jnp.zeros((PAIR_WIDTH,), jnp.float32), jnp.zeros((S, PROJECT_CHANNELS, RESIDUE_COUNT), jnp.float32))
    totals, stacked = lax.scan(block_step, initial, jnp.arange(RESIDUE_COUNT // block_rows, dtype=jnp.int32))
    weight_accumulated, bias_accumulated, column_total = totals
    pair_stack, left_parts = stacked
    pair_update_result = pair_stack.reshape(RESIDUE_COUNT, RESIDUE_COUNT, PAIR_WIDTH)
    left_grad = (jnp.transpose(left_parts, (1, 2, 0, 3)).reshape(S, PROJECT_CHANNELS, RESIDUE_COUNT) * inv_seqs).astype(jnp.bfloat16)
    right_grad = (column_total * inv_seqs).astype(jnp.bfloat16)
    projected_grad = jnp.concatenate([left_grad, right_grad], axis=1)
    grad_wide = projected_grad.astype(jnp.float32)
    projection_weight_gradient = jnp.einsum('srm,skr->mk', normalized_rows.astype(jnp.float32), grad_wide, precision=highest) / RESIDUE_COUNT
    normalized_gradient = jnp.einsum('skr,mk->srm', grad_wide, projection_weight.astype(jnp.float32), precision=highest) * norm_gain_vector
    alignment_gradient = norm_reverse_pass(normalized_gradient, rescaled_rows, inverse_deviation)
    return (pair_update_result, alignment_gradient, projection_weight_gradient, weight_accumulated.reshape(PROJECT_CHANNELS * PROJECT_CHANNELS, PAIR_WIDTH) / RESIDUE_COUNT, bias_accumulated / RESIDUE_COUNT)
```

```python
import jax
import jax.numpy as jnp
from jax import lax
from jax.sharding import PartitionSpec as P

epsilon = 1e-05
AXES = ("ia", "ja", "sa")
RING = 4
SWAP_Y = (0, 2, 1, 3)


def torus_permute(value, move):
    pairs = []
    for z in range(RING):
        for y in range(RING):
            for x in range(RING):
                for s in range(2):
                    tx, ty, tz, ts = move(x, y, z, s)
                    tx, ty, tz = tx % RING, ty % RING, tz % RING
                    source = ((z * 2 + y // 2) * 8 + x * 2 + y % 2) * 2 + s
                    target = ((tz * 2 + ty // 2) * 8 + tx * 2 + ty % 2) * 2 + ts
                    pairs.append((source, target))
    return lax.ppermute(value, AXES, pairs)


def swap_cores(value):
    return torus_permute(value, lambda x, y, z, s: (x, y, z, 1 - s))


def swap_low_y(value):
    return torus_permute(value, lambda x, y, z, s: (x, y ^ 1, z, s))


def shift_z(value, steps):
    return torus_permute(value, lambda x, y, z, s: (x, y, z + steps, s))


def shift_x(value, steps):
    return torus_permute(value, lambda x, y, z, s: (x + steps, y, z, s))


def transpose_xz(value):
    return torus_permute(value, lambda x, y, z, s: (z, SWAP_Y[y], x, s))


def layer_pieces(alignment_features, norm_gain_vector, norm_offset_vector):
    value_entries = alignment_features.astype(jnp.float32)
    average = jnp.mean(value_entries, axis=-1, keepdims=True)
    centred = value_entries - average
    variance = jnp.mean(centred * centred, axis=-1, keepdims=True)
    inverse_deviation = lax.rsqrt(variance + epsilon)
    rescaled_rows = centred * inverse_deviation
    normalized_rows = (rescaled_rows * norm_gain_vector + norm_offset_vector).astype(jnp.bfloat16)
    return (normalized_rows, rescaled_rows, inverse_deviation)


def norm_reverse_pass(normalized_gradient, rescaled_rows, inverse_deviation):
    first_mean = jnp.mean(normalized_gradient, axis=-1, keepdims=True)
    cross_mean = jnp.mean(normalized_gradient * rescaled_rows, axis=-1, keepdims=True)
    return (
        inverse_deviation * (normalized_gradient - first_mean - rescaled_rows * cross_mean)
    ).astype(jnp.bfloat16)


def project(normalized_rows, weight):
    return jnp.einsum(
        "srm,mk->skr", normalized_rows, weight, preferred_element_type=jnp.float32
    ).astype(jnp.bfloat16)


def add_up(parts):
    total = parts[0].astype(jnp.float32)
    for part in parts[1:]:
        total = total + part.astype(jnp.float32)
    return total


def body(
    alignment_features,
    norm_gain_vector,
    norm_offset_vector,
    projection_weight,
    output_weight,
    output_bias,
    pair_update_cotangent,
):
    half, residues, channels = alignment_features.shape
    width = projection_weight.shape[1] // 2
    pair_channels = output_weight.shape[1]
    rows = pair_update_cotangent.shape[0]
    seqs_total = half * 2
    rows_total = residues * lax.axis_size("ia")
    quarter = half // RING
    inv_seqs = 1.0 / seqs_total
    x = lax.axis_index("ja") // 2
    low_y = lax.axis_index("ja") % 2
    z = lax.axis_index("ia") // 2
    core = lax.axis_index("sa")
    bf = jnp.bfloat16

    own_quarter = lax.dynamic_slice_in_dim(alignment_features, x * quarter, quarter, 0)
    quarter_rows, _, _ = layer_pieces(own_quarter, norm_gain_vector, norm_offset_vector)
    right_piece = project(quarter_rows, projection_weight[:, width:])
    arrived = transpose_xz(right_piece)
    right_half = jnp.concatenate([arrived] + [shift_z(arrived, -t) for t in range(1, RING)], axis=0)
    right_cols = jnp.concatenate([right_half, swap_cores(right_half)], axis=0)

    normalized_rows, rescaled_rows, inverse_deviation = layer_pieces(
        alignment_features, norm_gain_vector, norm_offset_vector
    )
    left = project(normalized_rows, projection_weight[:, :width])
    left = jnp.roll(left, -z * quarter, axis=0)
    left_kept = lax.dynamic_slice_in_dim(left, core * rows, rows, 2)
    left_sent = lax.dynamic_slice_in_dim(left, (1 - core) * rows, rows, 2)
    own_left = jnp.concatenate([left_kept, swap_cores(left_sent)], axis=0)

    cube = output_weight.reshape(width, width, pair_channels)
    outer_grad = jnp.einsum(
        "ije,cde->icdj", pair_update_cotangent, cube, preferred_element_type=jnp.float32
    ).astype(bf)
    right_partial = jnp.einsum(
        "icdj,sci->sdj", outer_grad, own_left, preferred_element_type=jnp.float32
    )
    bias_partial = jnp.sum(pair_update_cotangent, axis=(0, 1), dtype=jnp.float32)

    right_sum = add_up([right_partial[:half], swap_cores(right_partial[half:].astype(bf))])
    pieces = [right_sum[t * quarter : (t + 1) * quarter].astype(bf) for t in range(RING)]
    right_sum = add_up([pieces[0]] + [shift_z(pieces[t], t) for t in range(1, RING)])
    right_sum = transpose_xz(right_sum.astype(bf))
    right_sum = add_up([right_sum, swap_low_y(right_sum)])
    right_grad = (right_sum * inv_seqs).astype(bf)
    right_pieces = [right_grad] + [shift_x(right_grad, -t) for t in range(1, RING)]

    left_partial = jnp.einsum(
        "icdj,sdj->sci", outer_grad, right_cols, preferred_element_type=jnp.float32
    ).astype(bf)
    left_all = jnp.concatenate([left_partial[:half], swap_cores(left_partial[half:])], axis=2)

    def left_quarter(t):
        place = lax.rem(x + t - z + RING, RING)
        return lax.dynamic_slice_in_dim(left_all, place * quarter, quarter, 0)

    left_sum = add_up([left_quarter(0)] + [shift_x(left_quarter(t), t) for t in range(1, RING)])
    left_sum = left_sum.astype(bf)
    left_sum = add_up([left_sum, swap_low_y(left_sum)])
    left_sum = jnp.where(core == 0, left_sum, jnp.roll(left_sum, rows, axis=2))
    left_grad = (left_sum * inv_seqs).astype(bf)
    left_pieces = [left_grad] + [shift_x(left_grad, -t) for t in range(1, RING)]

    outer = (
        jnp.einsum("sci,sdj->icdj", own_left, right_cols, preferred_element_type=jnp.float32)
        * inv_seqs
    ).astype(bf)
    weight_partial = jnp.einsum(
        "icdj,ije->cde", outer, pair_update_cotangent, preferred_element_type=jnp.float32
    )
    pair_update_result = (
        jnp.einsum("icdj,cde->ije", outer, cube, preferred_element_type=jnp.float32) + output_bias
    ).astype(bf)
    devices = 128
    weight_share = jnp.sum(
        lax.all_to_all(
            weight_partial.astype(bf).reshape(devices, -1, pair_channels), AXES, 0, 0, tiled=True
        ).astype(jnp.float32),
        axis=0,
    )

    eighth = quarter // 2
    grad_quarter = jnp.concatenate([left_grad, right_grad], axis=1)
    grad_eighth = lax.dynamic_slice_in_dim(grad_quarter, low_y * eighth, eighth, 0)
    rows_eighth = lax.dynamic_slice_in_dim(quarter_rows, low_y * eighth, eighth, 0)
    projection_part = jnp.einsum(
        "srm,skr->mk", rows_eighth, grad_eighth, preferred_element_type=jnp.float32
    )
    small = jnp.concatenate(
        [
            projection_part.reshape(devices, -1),
            jnp.broadcast_to(bias_partial, (devices, pair_channels)),
        ],
        axis=1,
    ).reshape(devices, 2, pair_channels)
    small_share = jnp.sum(lax.all_to_all(small, AXES, 0, 0, tiled=True), axis=0)
    share = jnp.concatenate([weight_share, small_share], axis=0)
    whole = lax.all_to_all(
        jnp.broadcast_to(share, (devices, *share.shape)), AXES, 0, 0, tiled=True
    )
    weight_sum = whole[:, :-2].reshape(width * width, pair_channels)
    projection_sum = whole[:, -2].reshape(channels, 2 * width)
    bias_sum = whole[0, -1]

    grads = jnp.concatenate(
        [jnp.concatenate(left_pieces, axis=0), jnp.concatenate(right_pieces, axis=0)], axis=1
    )
    projected_grad = jnp.roll(grads, x * quarter, axis=0)
    normalized_gradient = (
        jnp.einsum(
            "skr,mk->srm", projected_grad, projection_weight, preferred_element_type=jnp.float32
        )
        * norm_gain_vector
    )
    alignment_gradient = norm_reverse_pass(normalized_gradient, rescaled_rows, inverse_deviation)
    return (
        pair_update_result,
        alignment_gradient,
        projection_sum / rows_total,
        weight_sum / rows_total,
        bias_sum / rows_total,
    )


def solution(mesh):
    in_specs = (P("sa", "ia", None), P(), P(), P(), P(), P(), P(("ia", "sa"), "ja", None))
    out_specs = (P(("ia", "sa"), "ja", None), P("sa", "ia", None), P(), P(), P())
    return jax.shard_map(body, mesh=mesh, in_specs=in_specs, out_specs=out_specs, check_vma=False)
```

```python
import jax
import jax.numpy as jnp
from jax import lax
from jax.experimental import pallas as pl
from jax.experimental.pallas import tpu as pltpu
from jax.sharding import PartitionSpec as P

epsilon = 1e-05
AXES = ("ia", "ja", "sa")
RING = 4
SWAP_Y = (0, 2, 1, 3)
ROWS_AT_ONCE = 8
BF16 = jnp.bfloat16
F32 = jnp.float32
VMEM_LIMIT = 48 * 1024 * 1024


def dot(a, b, contract):
    return lax.dot_general(a, b, (contract, ((), ())), preferred_element_type=F32)


def params():
    return pltpu.CompilerParams(
        dimension_semantics=("arbitrary",), vmem_limit_bytes=VMEM_LIMIT
    )


def whole(shape):
    return pl.BlockSpec(shape, lambda *_: (0,) * len(shape))


def norm_rows(features):
    values = features.astype(F32)
    scale = 1.0 / values.shape[-1]
    centred = values - jnp.sum(values, axis=-1, keepdims=True) * scale
    variance = jnp.sum(centred * centred, axis=-1, keepdims=True) * scale
    inverse_deviation = lax.rsqrt(variance + epsilon)
    return centred * inverse_deviation, inverse_deviation


def project_kernel(features_ref, gain_ref, offset_ref, weight_ref, out_ref):
    seqs, residues, channels = features_ref.shape
    width = weight_ref.shape[0]
    for s in range(0, seqs, 2):
        rescaled, _ = norm_rows(features_ref[s : s + 2].reshape(2 * residues, channels))
        normed = (rescaled * gain_ref[...] + offset_ref[...]).astype(BF16)
        both = dot(weight_ref[...], normed, ((1,), (1,))).astype(BF16)
        out_ref[s] = both[:, :residues]
        out_ref[s + 1] = both[:, residues:]


def project(features, gain, offset, weight, seqs):
    count, residues, channels = features.shape
    width = weight.shape[0]
    return pl.pallas_call(
        project_kernel,
        grid=(count // seqs,),
        in_specs=[
            pl.BlockSpec((seqs, residues, channels), lambda n: (n, 0, 0)),
            whole((1, channels)),
            whole((1, channels)),
            whole((width, channels)),
        ],
        out_specs=pl.BlockSpec((seqs, width, residues), lambda n: (n, 0, 0)),
        out_shape=jax.ShapeDtypeStruct((count, width, residues), BF16),
        compiler_params=params(),
        cost_estimate=pl.CostEstimate(
            flops=2 * count * residues * channels * width,
            bytes_accessed=2 * count * residues * (channels + width),
            transcendentals=count * residues,
        ),
        name="project",
    )(features, gain.reshape(1, -1), offset.reshape(1, -1), weight)


def outer_grad_kernel(cot_ref, weight_ref, left_ref, grad_ref, right_ref, bias_ref, total_ref):
    step = pl.program_id(0)
    rows, cols, pair_channels = cot_ref.shape
    width = grad_ref.shape[1]

    @pl.when(step == 0)
    def _():
        total_ref[...] = jnp.zeros_like(total_ref)
        bias_ref[...] = jnp.zeros_like(bias_ref)

    bias_ref[...] += jnp.sum(
        cot_ref[...].astype(F32).reshape(rows * cols // 8, 8, pair_channels), axis=0
    )
    for i in range(0, rows, 2):
        cot = cot_ref[i : i + 2].reshape(2 * cols, pair_channels)
        grad = dot(weight_ref[...], cot, ((1,), (1,))).astype(BF16)
        grad = grad.reshape(width, width, 2 * cols)
        grad_ref[0, :, i * width : (i + 1) * width, :] = grad[:, :, :cols]
        grad_ref[0, :, (i + 1) * width : (i + 2) * width, :] = grad[:, :, cols:]
    left = left_ref[...].T
    for d in range(0, width, 2):
        both = jnp.concatenate([grad_ref[0, d], grad_ref[0, d + 1]], axis=1)
        total_ref[:, d * cols : (d + 2) * cols] += dot(left, both, ((1,), (0,)))

    @pl.when(step == pl.num_programs(0) - 1)
    def _():
        right_ref[...] = total_ref[...].astype(BF16)


def outer_grad_and_right(cotangent, weight, left):
    rows, cols, pair_channels = cotangent.shape
    seqs = left.shape[1]
    width = left.shape[0] // rows
    blocks = rows // ROWS_AT_ONCE
    block = ROWS_AT_ONCE * width
    return pl.pallas_call(
        outer_grad_kernel,
        grid=(blocks,),
        in_specs=[
            pl.BlockSpec((ROWS_AT_ONCE, cols, pair_channels), lambda n: (n, 0, 0)),
            whole((width * width, pair_channels)),
            pl.BlockSpec((block, seqs), lambda n: (n, 0)),
        ],
        out_specs=[
            pl.BlockSpec((1, width, block, cols), lambda n: (n, 0, 0, 0)),
            whole((seqs, width * cols)),
            whole((8, pair_channels)),
        ],
        out_shape=[
            jax.ShapeDtypeStruct((blocks, width, block, cols), BF16),
            jax.ShapeDtypeStruct((seqs, width * cols), BF16),
            jax.ShapeDtypeStruct((8, pair_channels), F32),
        ],
        scratch_shapes=[pltpu.VMEM((seqs, width * cols), F32)],
        compiler_params=params(),
        cost_estimate=pl.CostEstimate(
            flops=4 * rows * cols * width * width * pair_channels,
            bytes_accessed=2 * rows * cols * (pair_channels + width * width),
            transcendentals=0,
        ),
        name="outer_grad",
    )(cotangent, weight, left)


def fill(whole_ref, piece_refs):
    first = 0
    for piece in piece_refs:
        count = piece.shape[0]
        whole_ref[first : first + count, :] = piece[...]
        first += count


def left_grad_kernel(*refs):
    piece_refs, (grad_ref, out_ref, cols_ref) = refs[:-3], refs[-3:]
    _, width, _, cols = grad_ref.shape

    @pl.when(pl.program_id(0) == 0)
    def _():
        for d in range(width):
            here = slice(d * cols, (d + 1) * cols)
            part = jnp.concatenate([piece[:, here] for piece in piece_refs], axis=0)
            cols_ref[here, :] = part.T

    total = None
    for d in range(0, width, 2):
        both = jnp.concatenate([grad_ref[0, d], grad_ref[0, d + 1]], axis=1)
        term = dot(both, cols_ref[d * cols : (d + 2) * cols, :], ((1,), (0,)))
        total = term if total is None else total + term
    out_ref[...] = total.T.astype(BF16)


def left_grad_part(pieces, outer_grad):
    blocks, width, block, cols = outer_grad.shape
    seqs = sum(piece.shape[0] for piece in pieces)
    return pl.pallas_call(
        left_grad_kernel,
        grid=(blocks,),
        in_specs=[whole(piece.shape) for piece in pieces]
        + [pl.BlockSpec((1, width, block, cols), lambda n: (n, 0, 0, 0))],
        out_specs=pl.BlockSpec((seqs, block), lambda n: (0, n)),
        out_shape=jax.ShapeDtypeStruct((seqs, blocks * block), BF16),
        scratch_shapes=[pltpu.VMEM((width * cols, seqs), BF16)],
        compiler_params=params(),
        cost_estimate=pl.CostEstimate(
            flops=2 * blocks * width * block * cols * seqs,
            bytes_accessed=2 * blocks * width * block * cols,
            transcendentals=0,
        ),
        name="left_grad",
    )(*pieces, outer_grad)


def pair_kernel(*refs):
    piece_refs, refs = refs[:-9], refs[-9:]
    left_ref, weight_ref, bias_ref, cot_ref, pair_ref, grad_ref = refs[:6]
    cols_ref, outer_ref, total_ref = refs[6:]
    step = pl.program_id(0)
    rows, cols, pair_channels = cot_ref.shape
    width = outer_ref.shape[0]
    inv_seqs = 1.0 / cols_ref.shape[0]

    @pl.when(step == 0)
    def _():
        fill(cols_ref, piece_refs)
        total_ref[...] = jnp.zeros_like(total_ref)

    for d in range(0, width, 2):
        both = dot(left_ref[...], cols_ref[:, d * cols : (d + 2) * cols], ((1,), (0,)))
        both = (both * inv_seqs).astype(BF16)
        outer_ref[d] = both[:, :cols]
        outer_ref[d + 1] = both[:, cols:]
    for i in range(0, rows, 2):
        outer = jnp.concatenate(
            [
                outer_ref[:, n * width : (n + 1) * width, :].reshape(width * width, cols)
                for n in (i, i + 1)
            ],
            axis=1,
        )
        cot = cot_ref[i : i + 2].reshape(2 * cols, pair_channels)
        total_ref[...] += dot(outer, cot, ((1,), (0,)))
        pair = dot(weight_ref[...], outer, ((1,), (0,))).T + bias_ref[...]
        pair_ref[i : i + 2] = pair.astype(BF16).reshape(2, cols, pair_channels)

    @pl.when(step == pl.num_programs(0) - 1)
    def _():
        grad_ref[...] = total_ref[...].astype(BF16)


def pair_and_weight_grad(pieces, left, weight, bias, cotangent):
    rows, cols, pair_channels = cotangent.shape
    seqs = left.shape[1]
    width = left.shape[0] // rows
    blocks = rows // ROWS_AT_ONCE
    block = ROWS_AT_ONCE * width
    return pl.pallas_call(
        pair_kernel,
        grid=(blocks,),
        in_specs=[whole(piece.shape) for piece in pieces]
        + [
            pl.BlockSpec((block, seqs), lambda n: (n, 0)),
            whole((pair_channels, width * width)),
            whole((1, pair_channels)),
            pl.BlockSpec((ROWS_AT_ONCE, cols, pair_channels), lambda n: (n, 0, 0)),
        ],
        out_specs=[
            pl.BlockSpec((ROWS_AT_ONCE, cols, pair_channels), lambda n: (n, 0, 0)),
            whole((width * width, pair_channels)),
        ],
        out_shape=[
            jax.ShapeDtypeStruct((rows, cols, pair_channels), BF16),
            jax.ShapeDtypeStruct((width * width, pair_channels), BF16),
        ],
        scratch_shapes=[
            pltpu.VMEM((seqs, width * cols), BF16),
            pltpu.VMEM((width, block, cols), BF16),
            pltpu.VMEM((width * width, pair_channels), F32),
        ],
        compiler_params=params(),
        cost_estimate=pl.CostEstimate(
            flops=2 * rows * cols * width * width * (2 * pair_channels + seqs),
            bytes_accessed=4 * rows * cols * pair_channels,
            transcendentals=0,
        ),
        name="pair_update",
    )(*pieces, left, weight, bias.reshape(1, -1), cotangent)


def projection_grad_kernel(features_ref, gain_ref, offset_ref, left_ref, right_ref, out_ref):
    seqs = features_ref.shape[0]
    total = None
    for s in range(seqs):
        rescaled, _ = norm_rows(features_ref[s])
        normed = (rescaled * gain_ref[...] + offset_ref[...]).astype(BF16)
        grads = jnp.concatenate([left_ref[s], right_ref[s]], axis=0)
        term = dot(grads, normed, ((1,), (0,)))
        total = term if total is None else total + term
    out_ref[...] = total


def projection_grad_part(features, gain, offset, left, right):
    channels = features.shape[2]
    return pl.pallas_call(
        projection_grad_kernel,
        out_shape=jax.ShapeDtypeStruct((2 * left.shape[1], channels), F32),
        compiler_params=pltpu.CompilerParams(vmem_limit_bytes=VMEM_LIMIT),
        name="projection_grad",
    )(features, gain.reshape(1, -1), offset.reshape(1, -1), left, right)


def norm_grad_kernel(x_ref, *refs):
    left_refs, right_refs = refs[:RING], refs[RING : 2 * RING]
    features_ref, gain_ref, weight_ref, out_ref, grads_ref = refs[2 * RING :]
    step = pl.program_id(0)
    seqs = features_ref.shape[0]
    width = left_refs[0].shape[1]
    steps = left_refs[0].shape[0] // seqs
    for t in range(RING):

        @pl.when(step // steps == t)
        def _(t=t):
            here = pl.ds(lax.rem(step, steps) * seqs, seqs)
            grads_ref[:, :width, :] = left_refs[t][here]
            grads_ref[:, width:, :] = right_refs[t][here]

    channels = features_ref.shape[2]
    for s in range(seqs):
        rescaled, inverse_deviation = norm_rows(features_ref[s])
        grad = dot(grads_ref[s], weight_ref[...], ((0,), (0,))) * gain_ref[...]
        first = jnp.sum(grad, axis=-1, keepdims=True) * (1.0 / channels)
        cross = jnp.sum(grad * rescaled, axis=-1, keepdims=True) * (1.0 / channels)
        out_ref[s] = (inverse_deviation * (grad - first - rescaled * cross)).astype(BF16)


def norm_grad(x, left_pieces, right_pieces, features, gain, weight, seqs=8):
    count, residues, channels = features.shape
    quarter, width, _ = left_pieces[0].shape
    steps = quarter // seqs

    def place(n, x_ref):
        return (lax.rem(n // steps + x_ref[0], RING) * steps + lax.rem(n, steps), 0, 0)

    def all_of(shape):
        return pl.BlockSpec(shape, lambda n, x_ref: (0,) * len(shape))

    return pl.pallas_call(
        norm_grad_kernel,
        grid_spec=pltpu.PrefetchScalarGridSpec(
            num_scalar_prefetch=1,
            grid=(count // seqs,),
            in_specs=[all_of(left_pieces[0].shape)] * (2 * RING)
            + [
                pl.BlockSpec((seqs, residues, channels), place),
                all_of((1, channels)),
                all_of(weight.shape),
            ],
            out_specs=pl.BlockSpec((seqs, residues, channels), place),
            scratch_shapes=[pltpu.VMEM((seqs, 2 * width, residues), BF16)],
        ),
        out_shape=jax.ShapeDtypeStruct(features.shape, BF16),
        compiler_params=params(),
        cost_estimate=pl.CostEstimate(
            flops=4 * count * residues * channels * width,
            bytes_accessed=4 * count * residues * channels,
            transcendentals=count * residues,
        ),
        name="norm_grad",
    )(x.reshape(1), *left_pieces, *right_pieces, features, gain.reshape(1, -1), weight)


def torus_permute(value, move):
    pairs = []
    for z in range(RING):
        for y in range(RING):
            for x in range(RING):
                for s in range(2):
                    tx, ty, tz, ts = move(x, y, z, s)
                    tx, ty, tz = tx % RING, ty % RING, tz % RING
                    source = ((z * 2 + y // 2) * 8 + x * 2 + y % 2) * 2 + s
                    target = ((tz * 2 + ty // 2) * 8 + tx * 2 + ty % 2) * 2 + ts
                    pairs.append((source, target))
    return lax.ppermute(value, AXES, pairs)


def swap_cores(value):
    return torus_permute(value, lambda x, y, z, s: (x, y, z, 1 - s))


def swap_low_y(value):
    return torus_permute(value, lambda x, y, z, s: (x, y ^ 1, z, s))


def shift_z(value, steps):
    return torus_permute(value, lambda x, y, z, s: (x, y, z + steps, s))


def shift_x(value, steps):
    return torus_permute(value, lambda x, y, z, s: (x + steps, y, z, s))


def transpose_xz(value):
    return torus_permute(value, lambda x, y, z, s: (z, SWAP_Y[y], x, s))


def add_up(parts):
    total = parts[0].astype(F32)
    for part in parts[1:]:
        total = total + part.astype(F32)
    return total


def body(
    alignment_features,
    norm_gain_vector,
    norm_offset_vector,
    projection_weight,
    output_weight,
    output_bias,
    pair_update_cotangent,
):
    half, residues, channels = alignment_features.shape
    width = projection_weight.shape[1] // 2
    pair_channels = output_weight.shape[1]
    rows, cols, _ = pair_update_cotangent.shape
    rows_total = residues * lax.axis_size("ia")
    quarter = half // RING
    inv_seqs = 1.0 / (half * 2)
    x = lax.axis_index("ja") // 2
    low_y = lax.axis_index("ja") % 2
    z = lax.axis_index("ia") // 2
    core = lax.axis_index("sa")
    gain, offset = norm_gain_vector, norm_offset_vector
    weight_rows = projection_weight.T

    own_quarter = lax.dynamic_slice_in_dim(alignment_features, x * quarter, quarter, 0)
    right_piece = project(own_quarter, gain, offset, weight_rows[width:], quarter // 2)
    arrived = transpose_xz(right_piece.reshape(quarter, width * residues))
    right_pieces = [arrived] + [shift_z(arrived, -t) for t in range(1, RING)]
    right_cols = right_pieces + [swap_cores(piece) for piece in right_pieces]

    left = project(alignment_features, gain, offset, weight_rows[:width], 8)
    left = jnp.roll(left, -z * quarter, axis=0)
    left_kept = lax.dynamic_slice_in_dim(left, core * rows, rows, 2).transpose(2, 1, 0)
    left_sent = lax.dynamic_slice_in_dim(left, (1 - core) * rows, rows, 2)
    left_came = swap_cores(left_sent).transpose(2, 1, 0)
    own_left = jnp.concatenate([left_kept, left_came], axis=2).reshape(rows * width, 2 * half)

    weight_dc = (
        output_weight.reshape(width, width, pair_channels)
        .transpose(1, 0, 2)
        .reshape(width * width, pair_channels)
    )
    outer_grad, right_partial, bias_partial = outer_grad_and_right(
        pair_update_cotangent, weight_dc, own_left
    )

    right_sum = add_up([right_partial[:half], swap_cores(right_partial[half:])])
    pieces = [right_sum[t * quarter : (t + 1) * quarter].astype(BF16) for t in range(RING)]
    right_sum = add_up([pieces[0]] + [shift_z(pieces[t], t) for t in range(1, RING)])
    right_sum = transpose_xz(right_sum.astype(BF16))
    right_sum = add_up([right_sum, swap_low_y(right_sum)])
    right_grad = (right_sum * inv_seqs).astype(BF16).reshape(quarter, width, residues)
    right_grads = [right_grad] + [shift_x(right_grad, -t) for t in range(1, RING)]

    left_partial = left_grad_part(right_cols, outer_grad)
    left_all = jnp.concatenate([left_partial[:half], swap_cores(left_partial[half:])], axis=1)

    def left_quarter(t):
        place = lax.rem(x + t - z + RING, RING)
        return lax.dynamic_slice_in_dim(left_all, place * quarter, quarter, 0)

    left_sum = add_up([left_quarter(0)] + [shift_x(left_quarter(t), t) for t in range(1, RING)])
    left_sum = left_sum.astype(BF16)
    left_sum = add_up([left_sum, swap_low_y(left_sum)])
    left_sum = (left_sum * inv_seqs).astype(BF16).reshape(quarter, 2, rows, width)
    left_sum = jnp.where(core == 0, left_sum, left_sum[:, ::-1])
    left_grad = left_sum.reshape(quarter, residues, width).transpose(0, 2, 1)
    left_grads = [left_grad] + [shift_x(left_grad, -t) for t in range(1, RING)]

    pair_update_result, weight_partial = pair_and_weight_grad(
        right_cols, own_left, weight_dc.T, output_bias, pair_update_cotangent
    )
    devices = 128
    weight_share = jnp.sum(
        lax.all_to_all(
            weight_partial.reshape(devices, -1, pair_channels), AXES, 0, 0, tiled=True
        ).astype(F32),
        axis=0,
    )

    eighth = quarter // 2
    features_eighth = lax.dynamic_slice_in_dim(
        alignment_features, x * quarter + low_y * eighth, eighth, 0
    )
    projection_part = projection_grad_part(
        features_eighth,
        gain,
        offset,
        lax.dynamic_slice_in_dim(left_grad, low_y * eighth, eighth, 0),
        lax.dynamic_slice_in_dim(right_grad, low_y * eighth, eighth, 0),
    )
    small = jnp.concatenate(
        [
            projection_part.reshape(devices, -1),
            jnp.broadcast_to(jnp.sum(bias_partial, axis=0), (devices, pair_channels)),
        ],
        axis=1,
    ).reshape(devices, 2, pair_channels)
    small_share = jnp.sum(lax.all_to_all(small, AXES, 0, 0, tiled=True), axis=0)
    share = jnp.concatenate([weight_share, small_share], axis=0)
    everything = lax.all_to_all(
        jnp.broadcast_to(share, (devices, *share.shape)), AXES, 0, 0, tiled=True
    )
    weight_sum = (
        everything[:, :-2]
        .reshape(width, width, pair_channels)
        .transpose(1, 0, 2)
        .reshape(width * width, pair_channels)
    )
    projection_sum = everything[:, -2].reshape(2 * width, channels).T
    bias_sum = everything[0, -1]

    alignment_gradient = norm_grad(
        x, left_grads, right_grads, alignment_features, gain, weight_rows
    )
    return (
        pair_update_result,
        alignment_gradient,
        projection_sum / rows_total,
        weight_sum / rows_total,
        bias_sum / rows_total,
    )


def solution(mesh):
    in_specs = (P("sa", "ia", None), P(), P(), P(), P(), P(), P(("ia", "sa"), "ja", None))
    out_specs = (P(("ia", "sa"), "ja", None), P("sa", "ia", None), P(), P(), P())
    return jax.shard_map(body, mesh=mesh, in_specs=in_specs, out_specs=out_specs, check_vma=False)
```

```python
import functools

import jax
import jax.numpy as jnp
from jax import lax
from jax.experimental import pallas as pl
from jax.experimental.pallas import tpu as pltpu
from jax.sharding import PartitionSpec as P

epsilon = 1e-05
AXES = ("ia", "ja", "sa")
RING = 4
SWAP_Y = (0, 2, 1, 3)
ROWS_AT_ONCE = 8
BF16 = jnp.bfloat16
F32 = jnp.float32
VMEM_LIMIT = 12 * 1024 * 1024


def dot(a, b, contract):
    return lax.dot_general(a, b, (contract, ((), ())), preferred_element_type=F32)


def params(limit=VMEM_LIMIT):
    return pltpu.CompilerParams(dimension_semantics=("arbitrary",), vmem_limit_bytes=limit)


ANYWHERE = pl.BlockSpec(memory_space=pl.ANY)


def cost(flops, bytes_accessed, transcendentals):
    return pl.CostEstimate(
        flops=flops, bytes_accessed=bytes_accessed, transcendentals=transcendentals
    )


def whole(shape):
    return pl.BlockSpec(shape, lambda *_: (0,) * len(shape))


def row_mean(values):
    channels = values.shape[-1]
    ones = jnp.full((channels, 128), 1.0 / channels, BF16)
    mean = dot(values.astype(BF16), ones, ((1,), (0,)))
    return jnp.concatenate([mean] * (channels // 128), axis=1)


def norm_block(features):
    centred = features.astype(F32) - row_mean(features)
    inverse_deviation = lax.rsqrt(row_mean(centred * centred) + epsilon)
    return centred * inverse_deviation, inverse_deviation


def norm_rows(features):
    values = features.astype(F32)
    scale = 1.0 / values.shape[-1]
    centred = values - jnp.sum(values, axis=-1, keepdims=True) * scale
    variance = jnp.sum(centred * centred, axis=-1, keepdims=True) * scale
    return centred * lax.rsqrt(variance + epsilon)


def project_kernel(place_ref, features_ref, gain_ref, offset_ref, weight_ref, *refs):
    out_ref = refs[-1]
    seqs, residues, channels = features_ref.shape
    at_once = 256 // residues
    for s in range(0, seqs, at_once):
        rescaled = norm_rows(
            features_ref[s : s + at_once].reshape(at_once * residues, channels)
        )
        normed = (rescaled * gain_ref[...] + offset_ref[...]).astype(BF16)
        several = dot(weight_ref[...], normed, ((1,), (1,))).astype(BF16)
        for n in range(at_once):
            out_ref[s + n] = several[:, n * residues : (n + 1) * residues]


def project(first, count, part, residues, features, gain, offset, weight, after=()):
    total, _, channels = features.shape
    width = weight.shape[0]
    seqs = 1024 // residues
    steps = total // seqs

    def place(n, place_ref):
        return (lax.rem(place_ref[0] + n, steps), place_ref[1], 0)

    return pl.pallas_call(
        project_kernel,
        grid_spec=pltpu.PrefetchScalarGridSpec(
            num_scalar_prefetch=1,
            grid=(count // seqs,),
            in_specs=[
                pl.BlockSpec((seqs, residues, channels), place),
                whole((1, channels)),
                whole((1, channels)),
                whole((width, channels)),
            ]
            + [ANYWHERE] * len(after),
            out_specs=pl.BlockSpec((seqs, width, residues), lambda n, place_ref: (n, 0, 0)),
        ),
        out_shape=jax.ShapeDtypeStruct((count, width, residues), BF16),
        compiler_params=params(),
        cost_estimate=cost(
            flops=4 * count * residues * channels * width,
            bytes_accessed=2 * count * residues * (channels + width),
            transcendentals=count * residues,
        ),
        name="project",
    )(jnp.stack([first, part]), features, gain, offset, weight, *after)


def outer_grad_block(cot_ref, weight_ref, grad_ref):
    rows, cols, pair_channels = cot_ref.shape
    width = grad_ref.shape[0]
    for i in range(0, rows, 2):
        cot = cot_ref[i : i + 2].reshape(2 * cols, pair_channels)
        grad = dot(weight_ref[...], cot, ((1,), (1,))).astype(BF16)
        grad = grad.reshape(width, width, 2 * cols)
        grad_ref[:, i * width : (i + 1) * width, :] = grad[:, :, :cols]
        grad_ref[:, (i + 1) * width : (i + 2) * width, :] = grad[:, :, cols:]


def right_grad_kernel(fresh, cot_ref, weight_ref, left_ref, total_in_ref, bias_in_ref, *refs):
    right_ref, total_ref, bias_ref, grad_ref = refs[-4:]
    step = pl.program_id(0)
    rows, cols, pair_channels = cot_ref.shape
    width = grad_ref.shape[0]

    @pl.when(step == 0)
    def _():
        if fresh:
            total_ref[...] = jnp.zeros_like(total_ref)
            bias_ref[...] = jnp.zeros_like(bias_ref)
        else:
            total_ref[...] = total_in_ref[...]
            bias_ref[...] = bias_in_ref[...]

    bias_ref[...] += jnp.sum(
        cot_ref[...].astype(F32).reshape(rows * cols // 8, 8, pair_channels), axis=0
    )
    outer_grad_block(cot_ref, weight_ref, grad_ref)
    left = left_ref[...].T
    for d in range(0, width, 2):
        both = jnp.concatenate([grad_ref[d], grad_ref[d + 1]], axis=1)
        total_ref[:, d * cols : (d + 2) * cols] += dot(left, both, ((1,), (0,)))

    if not fresh:

        @pl.when(step == pl.num_programs(0) - 1)
        def _():
            right_ref[...] = total_ref[...].astype(BF16)


def right_grad_part(first, count, cotangent, weight, left, before, after=()):
    rows, cols, pair_channels = cotangent.shape
    seqs = left.shape[1]
    width = left.shape[0] // rows
    block = ROWS_AT_ONCE * width
    fresh = before is None
    if fresh:
        before = (None, jnp.zeros((8, pair_channels), F32), jnp.zeros((8, pair_channels), F32))
    right_shape = (8, pair_channels) if fresh else (seqs, width * cols)
    return pl.pallas_call(
        functools.partial(right_grad_kernel, fresh),
        grid=(count,),
        in_specs=[
            pl.BlockSpec((ROWS_AT_ONCE, cols, pair_channels), lambda n: (first + n, 0, 0)),
            whole((width * width, pair_channels)),
            pl.BlockSpec((block, seqs), lambda n: (first + n, 0)),
            whole(before[1].shape),
            whole(before[2].shape),
        ]
        + [ANYWHERE] * len(after),
        out_specs=[
            whole(right_shape),
            whole((seqs, width * cols)),
            whole((8, pair_channels)),
        ],
        out_shape=[
            jax.ShapeDtypeStruct(right_shape, BF16),
            jax.ShapeDtypeStruct((seqs, width * cols), F32),
            jax.ShapeDtypeStruct((8, pair_channels), F32),
        ],
        scratch_shapes=[pltpu.VMEM((width, block, cols), BF16)],
        compiler_params=params(),
        cost_estimate=cost(
            flops=4 * count * ROWS_AT_ONCE * cols * width * width * pair_channels,
            bytes_accessed=2 * count * ROWS_AT_ONCE * cols * pair_channels,
            transcendentals=0,
        ),
        name="right_grad",
    )(cotangent, weight, left, before[1], before[2], *after)


def left_grad_kernel(turn_ref, *refs):
    piece_refs, (cot_ref, weight_ref, out_ref, cols_ref, grad_ref) = refs[: 2 * RING], refs[-5:]
    width, _, cols = grad_ref.shape
    quarter = piece_refs[0].shape[0]

    @pl.when(pl.program_id(0) == 0)
    def _():
        for d in range(width):
            here = slice(d * cols, (d + 1) * cols)
            part = jnp.concatenate([piece[:, here] for piece in piece_refs], axis=0)
            cols_ref[here, :] = part.T

    outer_grad_block(cot_ref, weight_ref, grad_ref)
    total = None
    for d in range(0, width, 2):
        both = jnp.concatenate([grad_ref[d], grad_ref[d + 1]], axis=1)
        term = dot(both, cols_ref[d * cols : (d + 2) * cols, :], ((1,), (0,)))
        total = term if total is None else total + term
    total = total.T.astype(BF16)
    for p in range(RING):
        place = lax.rem(turn_ref[0] + p, RING)
        for h in range(2):
            first = (h * RING + p) * quarter
            out_ref[place, h * quarter : (h + 1) * quarter, :] = total[first : first + quarter]


def left_grad_part(turn, pieces, cotangent, weight, after=()):
    rows, cols, pair_channels = cotangent.shape
    quarter = pieces[0].shape[0]
    width = pieces[0].shape[1] // cols
    blocks, block = rows // ROWS_AT_ONCE, ROWS_AT_ONCE * width
    seqs = 2 * RING * quarter
    return pl.pallas_call(
        left_grad_kernel,
        grid_spec=pltpu.PrefetchScalarGridSpec(
            num_scalar_prefetch=1,
            grid=(blocks,),
            in_specs=[whole(piece.shape) for piece in pieces]
            + [ANYWHERE] * len(after)
            + [
                pl.BlockSpec((ROWS_AT_ONCE, cols, pair_channels), lambda n, turn_ref: (n, 0, 0)),
                whole((width * width, pair_channels)),
            ],
            out_specs=pl.BlockSpec((RING, 2 * quarter, block), lambda n, turn_ref: (0, 0, n)),
            scratch_shapes=[
                pltpu.VMEM((width * cols, seqs), BF16),
                pltpu.VMEM((width, block, cols), BF16),
            ],
        ),
        out_shape=jax.ShapeDtypeStruct((RING, 2 * quarter, blocks * block), BF16),
        compiler_params=params(),
        cost_estimate=cost(
            flops=4 * blocks * width * block * cols * (seqs + pair_channels),
            bytes_accessed=4 * seqs * width * cols,
            transcendentals=0,
        ),
        name="left_grad",
    )(
        turn.reshape(1),
        *pieces,
        *after,
        cotangent,
        weight,
    )


def add_kernel(count, scale, *refs):
    total = refs[0][...].astype(F32)
    for ref in refs[1:count]:
        total = total + ref[...].astype(F32)
    refs[-1][...] = (total * scale).astype(BF16)


def add_up(parts, scale=1.0, after=()):
    return pl.pallas_call(
        lambda *refs: add_kernel(len(parts), scale, *refs),
        in_specs=[pl.BlockSpec(memory_space=pltpu.VMEM)] * len(parts) + [ANYWHERE] * len(after),
        out_specs=pl.BlockSpec(memory_space=pltpu.VMEM),
        out_shape=jax.ShapeDtypeStruct(parts[0].shape, BF16),
        compiler_params=pltpu.CompilerParams(vmem_limit_bytes=VMEM_LIMIT),
        name="add_up",
    )(*parts, *after)


def pair_kernel(fresh, *refs):
    piece_refs, refs = refs[: 2 * RING], refs[2 * RING :]
    left_ref, weight_ref, bias_ref, cot_ref, before_ref = refs[:5]
    pair_ref, total_ref, cols_ref, outer_ref = refs[-4:]
    rows, cols, pair_channels = cot_ref.shape
    width = outer_ref.shape[0]
    inv_seqs = 1.0 / cols_ref.shape[0]

    @pl.when(pl.program_id(0) == 0)
    def _():
        first = 0
        for piece in piece_refs:
            cols_ref[first : first + piece.shape[0], :] = piece[...]
            first += piece.shape[0]
        total_ref[...] = jnp.zeros_like(total_ref) if fresh else before_ref[...]

    for d in range(0, width, 2):
        both = dot(left_ref[...], cols_ref[:, d * cols : (d + 2) * cols], ((1,), (0,)))
        both = (both * inv_seqs).astype(BF16)
        outer_ref[d] = both[:, :cols]
        outer_ref[d + 1] = both[:, cols:]
    for i in range(0, rows, 2):
        outer = jnp.concatenate(
            [
                outer_ref[:, n * width : (n + 1) * width, :].reshape(width * width, cols)
                for n in (i, i + 1)
            ],
            axis=1,
        )
        cot = cot_ref[i : i + 2].reshape(2 * cols, pair_channels)
        total_ref[...] += dot(outer, cot, ((1,), (0,)))
        pair = dot(weight_ref[...], outer, ((1,), (0,))).T + bias_ref[...]
        pair_ref[i : i + 2] = pair.astype(BF16).reshape(2, cols, pair_channels)


def pair_and_weight_grad(first, count, pieces, left, weight, bias, cotangent, before, after=()):
    rows, cols, pair_channels = cotangent.shape
    seqs = left.shape[1]
    width = left.shape[0] // rows
    block = ROWS_AT_ONCE * width
    fresh = before is None
    if fresh:
        before = (None, jnp.zeros((8, pair_channels), F32))
    operands = [*pieces, left, weight, bias.reshape(1, -1), cotangent, before[1], *after]
    in_specs = [whole(piece.shape) for piece in pieces] + [
        pl.BlockSpec((block, seqs), lambda n: (first + n, 0)),
        whole((pair_channels, width * width)),
        whole((1, pair_channels)),
        pl.BlockSpec((ROWS_AT_ONCE, cols, pair_channels), lambda n: (first + n, 0, 0)),
        whole(before[1].shape),
    ]
    in_specs += [ANYWHERE] * len(after)
    aliases = {}
    if not fresh:
        aliases = {len(operands): 0}
        operands.append(before[0])
        in_specs.append(ANYWHERE)
    return pl.pallas_call(
        functools.partial(pair_kernel, fresh),
        grid=(count,),
        in_specs=in_specs,
        out_specs=[
            pl.BlockSpec((ROWS_AT_ONCE, cols, pair_channels), lambda n: (first + n, 0, 0)),
            whole((width * width, pair_channels)),
        ],
        out_shape=[
            jax.ShapeDtypeStruct((rows, cols, pair_channels), BF16),
            jax.ShapeDtypeStruct((width * width, pair_channels), F32),
        ],
        scratch_shapes=[
            pltpu.VMEM((seqs, width * cols), BF16),
            pltpu.VMEM((width, block, cols), BF16),
        ],
        input_output_aliases=aliases,
        compiler_params=params(),
        cost_estimate=cost(
            flops=4 * count * ROWS_AT_ONCE * cols * width * width * (2 * pair_channels + seqs),
            bytes_accessed=4 * count * ROWS_AT_ONCE * cols * pair_channels,
            transcendentals=0,
        ),
        name="pair_update",
    )(*operands)


def projection_grad_kernel(place_ref, features_ref, gain_ref, offset_ref, grads_ref, out_ref):
    seqs = features_ref.shape[0]
    total = None
    for s in range(seqs):
        rescaled = norm_rows(features_ref[s])
        normed = (rescaled * gain_ref[...] + offset_ref[...]).astype(BF16)
        term = dot(grads_ref[s], normed, ((1,), (0,)))
        total = term if total is None else total + term
    out_ref[...] = total


def projection_grad_part(x, low_y, features, gain, offset, grads):
    _, residues, channels = features.shape
    quarter, both_widths, _ = grads.shape
    eighth = quarter // 2
    place = jnp.stack([x * 2 + low_y, low_y])
    return pl.pallas_call(
        projection_grad_kernel,
        grid_spec=pltpu.PrefetchScalarGridSpec(
            num_scalar_prefetch=1,
            grid=(1,),
            in_specs=[
                pl.BlockSpec((eighth, residues, channels), lambda n, ref: (ref[0], 0, 0)),
                whole((1, channels)),
                whole((1, channels)),
                pl.BlockSpec((eighth, both_widths, residues), lambda n, ref: (ref[1], 0, 0)),
            ],
            out_specs=whole((both_widths, channels)),
        ),
        out_shape=jax.ShapeDtypeStruct((both_widths, channels), F32),
        compiler_params=params(),
        name="projection_grad",
    )(place, features, gain, offset, grads)


def norm_grad_kernel(count, first_ref, features_ref, gain_ref, weight_ref, *refs):
    piece_refs, (out_ref, token_ref, grads_ref) = refs[:count], refs[-3:]
    token_ref[...] = jnp.zeros_like(token_ref)
    step = pl.program_id(0)
    seqs, residues, channels = features_ref.shape
    steps = piece_refs[0].shape[0] // seqs
    for t in range(len(piece_refs)):

        @pl.when(step // steps == t)
        def _(t=t):
            grads_ref[...] = piece_refs[t][pl.ds(lax.rem(step, steps) * seqs, seqs)]

    at_once = 4
    for s in range(0, seqs, at_once):
        features = features_ref[s : s + at_once].reshape(at_once * residues, channels)
        rescaled, inverse_deviation = norm_block(features)
        grad = [dot(grads_ref[s + n], weight_ref[...], ((0,), (0,))) for n in range(at_once)]
        grad = jnp.concatenate(grad, axis=0) * gain_ref[...]
        grad = inverse_deviation * (grad - row_mean(grad) - rescaled * row_mean(grad * rescaled))
        out_ref[s : s + at_once] = grad.astype(BF16).reshape(at_once, residues, channels)


def norm_grad(first, pieces, features, gain, weight, before=None, after=()):
    _, residues, channels = features.shape
    quarter, both_widths, _ = pieces[0].shape
    seqs = 8
    steps = quarter // seqs

    def place(n, first_ref):
        return (lax.rem(n // steps + first_ref[0], RING) * steps + lax.rem(n, steps), 0, 0)

    operands = [first.reshape(1), features, gain, weight, *pieces, *after]
    in_specs = [
        pl.BlockSpec((seqs, residues, channels), place),
        whole((1, channels)),
        whole(weight.shape),
    ]
    in_specs += [whole(piece.shape) for piece in pieces] + [ANYWHERE] * len(after)
    aliases = {}
    if before is not None:
        aliases = {len(operands): 0}
        operands.append(before)
        in_specs.append(ANYWHERE)
    return pl.pallas_call(
        functools.partial(norm_grad_kernel, len(pieces)),
        grid_spec=pltpu.PrefetchScalarGridSpec(
            num_scalar_prefetch=1,
            grid=(len(pieces) * steps,),
            in_specs=in_specs,
            out_specs=[pl.BlockSpec((seqs, residues, channels), place), whole((8, 128))],
            scratch_shapes=[pltpu.VMEM((seqs, both_widths, residues), BF16)],
        ),
        out_shape=[
            jax.ShapeDtypeStruct(features.shape, BF16),
            jax.ShapeDtypeStruct((8, 128), F32),
        ],
        input_output_aliases=aliases,
        compiler_params=params(),
        cost_estimate=cost(
            flops=4 * len(pieces) * quarter * residues * channels * both_widths,
            bytes_accessed=4 * len(pieces) * quarter * residues * channels,
            transcendentals=0,
        ),
        name="norm_grad",
    )(*operands)


def share_kernel(scale, terms_ref, *refs):
    share_ref, spread_ref = refs[-2:]
    total = terms_ref[0].astype(F32)
    for n in range(1, terms_ref.shape[0]):
        total = total + terms_ref[n].astype(F32)
    total = total * scale
    share_ref[...] = total
    spread_ref[...] = jnp.broadcast_to(total.astype(BF16), spread_ref.shape)


def add_terms(terms, scale, after=()):
    return pl.pallas_call(
        functools.partial(share_kernel, scale),
        in_specs=[pl.BlockSpec(memory_space=pltpu.VMEM)] + [ANYWHERE] * len(after),
        out_specs=[pl.BlockSpec(memory_space=pltpu.VMEM)] * 2,
        out_shape=[
            jax.ShapeDtypeStruct(terms.shape[1:], F32),
            jax.ShapeDtypeStruct(terms.shape, BF16),
        ],
        compiler_params=pltpu.CompilerParams(vmem_limit_bytes=VMEM_LIMIT),
        name="add_terms",
    )(terms, *after)


def terms_kernel(weight_ref, projection_ref, bias_ref, *refs):
    out_ref, token_ref = refs[-2:]
    token_ref[...] = jnp.zeros_like(token_ref)
    devices, rows, lanes = out_ref.shape
    weight_rows = weight_ref.shape[0] // devices
    bias = jnp.sum(bias_ref[...], axis=0, keepdims=True)
    bias_high = bias.astype(BF16).astype(F32)
    tail = jnp.concatenate(
        [bias_high, bias - bias_high, jnp.zeros((rows - weight_rows - 3, lanes), F32)], axis=0
    )
    for n in range(devices):
        block = [
            weight_ref[n * weight_rows : (n + 1) * weight_rows, :],
            projection_ref[n : n + 1, :],
            tail,
        ]
        out_ref[n] = jnp.concatenate(block, axis=0).astype(BF16)


def gather_terms(devices, weight_part, projection_part, bias_part, after=()):
    lanes = weight_part.shape[1]
    return pl.pallas_call(
        terms_kernel,
        in_specs=[pl.BlockSpec(memory_space=pltpu.VMEM)] * 3 + [ANYWHERE] * len(after),
        out_specs=[pl.BlockSpec(memory_space=pltpu.VMEM)] * 2,
        out_shape=[
            jax.ShapeDtypeStruct((devices, 16, lanes), BF16),
            jax.ShapeDtypeStruct((8, lanes), F32),
        ],
        compiler_params=pltpu.CompilerParams(vmem_limit_bytes=VMEM_LIMIT),
        name="gather_terms",
    )(weight_part, projection_part.reshape(devices, lanes), bias_part, *after)


def torus_permute(value, move):
    pairs = []
    for z in range(RING):
        for y in range(RING):
            for x in range(RING):
                for s in range(2):
                    tx, ty, tz, ts = move(x, y, z, s)
                    tx, ty, tz = tx % RING, ty % RING, tz % RING
                    source = ((z * 2 + y // 2) * 8 + x * 2 + y % 2) * 2 + s
                    target = ((tz * 2 + ty // 2) * 8 + tx * 2 + ty % 2) * 2 + ts
                    pairs.append((source, target))
    return lax.ppermute(value, AXES, pairs)


def swap_cores(value):
    return torus_permute(value, lambda x, y, z, s: (x, y, z, 1 - s))


def swap_low_y(value):
    return torus_permute(value, lambda x, y, z, s: (x, y ^ 1, z, s))


def shift_z(value, steps):
    return torus_permute(value, lambda x, y, z, s: (x, y, z + steps, s))


def shift_x(value, steps):
    return torus_permute(value, lambda x, y, z, s: (x + steps, y, z, s))


def transpose_xz(value):
    return torus_permute(value, lambda x, y, z, s: (z, SWAP_Y[y], x, s))


def body(
    alignment_features,
    norm_gain_vector,
    norm_offset_vector,
    projection_weight,
    output_weight,
    output_bias,
    pair_update_cotangent,
):
    half, residues, channels = alignment_features.shape
    width = projection_weight.shape[1] // 2
    pair_channels = output_weight.shape[1]
    rows, cols, _ = pair_update_cotangent.shape
    rows_total = residues * lax.axis_size("ia")
    quarter = half // RING
    inv_seqs = 1.0 / (half * 2)
    x = lax.axis_index("ja") // 2
    low_y = lax.axis_index("ja") % 2
    z = lax.axis_index("ia") // 2
    core = lax.axis_index("sa")
    features = pltpu.with_memory_space_constraint(alignment_features, pltpu.HBM)
    cotangent = pair_update_cotangent
    gain_row = norm_gain_vector.reshape(1, -1)
    offset_row = norm_offset_vector.reshape(1, -1)
    weight_rows = projection_weight.T

    right_piece = project(
        x * 2,
        quarter,
        x * 0,
        residues,
        features,
        pltpu.with_memory_space_constraint(gain_row, pltpu.HBM),
        pltpu.with_memory_space_constraint(offset_row, pltpu.HBM),
        weight_rows[width:],
    )
    arrived = transpose_xz(right_piece.reshape(quarter, width * residues))

    def left_rows(part):
        return project(
            z,
            half,
            part,
            rows,
            alignment_features,
            gain_row,
            offset_row,
            weight_rows[:width],
            after=(right_piece,),
        )

    left_came = swap_cores(left_rows(1 - core)).transpose(2, 1, 0)
    left_kept = left_rows(core).transpose(2, 1, 0)
    own_left = jnp.concatenate([left_kept, left_came], axis=2).reshape(rows * width, 2 * half)

    arrived = add_up([arrived], after=(own_left,))
    right_pieces = [arrived] + [shift_z(arrived, -t) for t in range(1, RING)]
    right_cols = right_pieces + [swap_cores(piece) for piece in right_pieces]

    weight_dc = (
        output_weight.reshape(width, width, pair_channels)
        .transpose(1, 0, 2)
        .reshape(width * width, pair_channels)
    )
    blocks = rows // ROWS_AT_ONCE
    part = right_grad_part(
        0, blocks // 2, cotangent, weight_dc, own_left, None, after=(arrived,)
    )
    right_partial, _, bias_partial = right_grad_part(
        blocks // 2,
        blocks // 2,
        cotangent,
        weight_dc,
        own_left,
        part,
        after=tuple(right_pieces[1:]),
    )

    right_sum = add_up([right_partial[:half], swap_cores(right_partial[half:])])
    pieces = [right_sum[t * quarter : (t + 1) * quarter] for t in range(RING)]
    right_came = [shift_z(pieces[t], t) for t in range(1, RING)]
    left_partial = left_grad_part(
        lax.rem(z - x + RING, RING),
        right_cols,
        cotangent,
        weight_dc,
        after=(right_sum,),
    )

    left_came = [shift_x(left_partial[t], t) for t in range(1, RING)]
    right_sum = transpose_xz(add_up([pieces[0], *right_came], after=(left_partial,)))

    def pair_part(first, count, before, after):
        return pair_and_weight_grad(
            first,
            count,
            right_cols,
            own_left,
            weight_dc.T,
            output_bias,
            cotangent,
            before,
            after,
        )

    pair = pair_part(0, 4, None, (left_partial,))
    left_sum = add_up([left_partial[0], *left_came], after=(pair[1],))

    left_other, right_other = swap_low_y(left_sum), swap_low_y(right_sum)
    pair = pair_part(4, 2, pair, (left_sum,))
    left_sum = add_up([left_sum, left_other], inv_seqs, after=(pair[1],))
    right_grad = add_up([right_sum, right_other], inv_seqs, after=(pair[1],))

    left_own, left_came = left_sum[:quarter], swap_cores(left_sum[quarter:])
    left_low = jnp.where(core == 0, left_own, left_came).reshape(quarter, rows, width)
    left_high = jnp.where(core == 0, left_came, left_own).reshape(quarter, rows, width)
    left_grad = jnp.concatenate(
        [left_low.transpose(0, 2, 1), left_high.transpose(0, 2, 1)], axis=2
    )
    grads = jnp.concatenate([left_grad, right_grad.reshape(quarter, width, residues)], axis=1)
    grad_pieces = [grads] + [shift_x(grads, -t) for t in range(1, RING)]

    pair_update_result, weight_partial = pair_part(6, blocks - 6, pair, (grads,))
    projection_part = projection_grad_part(x, low_y, features, gain_row, offset_row, grads)
    devices = 128
    terms, token = gather_terms(
        devices, weight_partial, projection_part, bias_partial, after=tuple(grad_pieces[1:])
    )

    came = lax.all_to_all(terms, AXES, 0, 0, tiled=True)

    def norm_part(first, before, after):
        pieces = grad_pieces[first : first + 2]
        place = lax.rem(x + first, RING)
        return norm_grad(
            place, pieces, alignment_features, gain_row, weight_rows, before, after
        )

    alignment_gradient, token = norm_part(0, None, (token,))
    share, spread = add_terms(came, 1.0 / rows_total, after=(token,))
    bias_sum = share[9] + share[10]
    everything = lax.all_to_all(spread, AXES, 0, 0, tiled=True).astype(F32)
    alignment_gradient, _ = norm_part(2, alignment_gradient, (share,))
    weight_sum = (
        everything[:, :8]
        .reshape(width, width, pair_channels)
        .transpose(1, 0, 2)
        .reshape(width * width, pair_channels)
    )
    projection_sum = everything[:, 8].reshape(2 * width, channels).T

    return (
        pair_update_result,
        alignment_gradient,
        projection_sum,
        weight_sum,
        bias_sum,
    )


def solution(mesh):
    in_specs = (P("sa", "ia", None), P(), P(), P(), P(), P(), P(("ia", "sa"), "ja", None))
    out_specs = (P(("ia", "sa"), "ja", None), P("sa", "ia", None), P(), P(), P())
    return jax.shard_map(body, mesh=mesh, in_specs=in_specs, out_specs=out_specs, check_vma=False)
```

```python
import functools

import jax
import jax.numpy as jnp
from jax import lax
from jax.experimental import pallas as pl
from jax.experimental.pallas import tpu as pltpu
from jax.sharding import PartitionSpec as P

epsilon = 1e-05
AXES = ("ia", "ja", "sa")
RING = 4
SWAP_Y = (0, 2, 1, 3)
ROWS_AT_ONCE = 8
BF16 = jnp.bfloat16
F32 = jnp.float32
VMEM_LIMIT = 12 * 1024 * 1024


def dot(a, b, contract):
    return lax.dot_general(a, b, (contract, ((), ())), preferred_element_type=F32)


def params(limit=VMEM_LIMIT):
    return pltpu.CompilerParams(dimension_semantics=("arbitrary",), vmem_limit_bytes=limit)


ANYWHERE = pl.BlockSpec(memory_space=pl.ANY)


def cost(flops, bytes_accessed, transcendentals):
    return pl.CostEstimate(
        flops=flops, bytes_accessed=bytes_accessed, transcendentals=transcendentals
    )


def whole(shape):
    return pl.BlockSpec(shape, lambda *_: (0,) * len(shape))


def row_mean(values):
    channels = values.shape[-1]
    ones = jnp.full((channels, 128), 1.0 / channels, BF16)
    mean = dot(values.astype(BF16), ones, ((1,), (0,)))
    return jnp.concatenate([mean] * (channels // 128), axis=1)


def norm_block(features):
    centred = features.astype(F32) - row_mean(features)
    inverse_deviation = lax.rsqrt(row_mean(centred * centred) + epsilon)
    return centred * inverse_deviation, inverse_deviation


def norm_rows(features):
    values = features.astype(F32)
    scale = 1.0 / values.shape[-1]
    centred = values - jnp.sum(values, axis=-1, keepdims=True) * scale
    variance = jnp.sum(centred * centred, axis=-1, keepdims=True) * scale
    return centred * lax.rsqrt(variance + epsilon)


def project_kernel(place_ref, features_ref, gain_ref, offset_ref, weight_ref, *refs):
    out_ref = refs[-1]
    seqs, residues, channels = features_ref.shape
    at_once = 256 // residues
    for s in range(0, seqs, at_once):
        rescaled = norm_rows(
            features_ref[s : s + at_once].reshape(at_once * residues, channels)
        )
        normed = (rescaled * gain_ref[...] + offset_ref[...]).astype(BF16)
        several = dot(weight_ref[...], normed, ((1,), (1,))).astype(BF16)
        for n in range(at_once):
            out_ref[s + n] = several[:, n * residues : (n + 1) * residues]


def project(first, count, part, residues, features, gain, offset, weight, after=()):
    total, _, channels = features.shape
    width = weight.shape[0]
    seqs = 1024 // residues
    steps = total // seqs

    def place(n, place_ref):
        return (lax.rem(place_ref[0] + n, steps), place_ref[1], 0)

    return pl.pallas_call(
        project_kernel,
        grid_spec=pltpu.PrefetchScalarGridSpec(
            num_scalar_prefetch=1,
            grid=(count // seqs,),
            in_specs=[
                pl.BlockSpec((seqs, residues, channels), place),
                whole((1, channels)),
                whole((1, channels)),
                whole((width, channels)),
            ]
            + [ANYWHERE] * len(after),
            out_specs=pl.BlockSpec((seqs, width, residues), lambda n, place_ref: (n, 0, 0)),
        ),
        out_shape=jax.ShapeDtypeStruct((count, width, residues), BF16),
        compiler_params=params(),
        cost_estimate=cost(
            flops=4 * count * residues * channels * width,
            bytes_accessed=2 * count * residues * (channels + width),
            transcendentals=count * residues,
        ),
        name="project",
    )(jnp.stack([first, part]), features, gain, offset, weight, *after)


def outer_grad_block(cot_ref, weight_ref, grad_ref):
    rows, cols, pair_channels = cot_ref.shape
    width = grad_ref.shape[0]
    for i in range(0, rows, 2):
        cot = cot_ref[i : i + 2].reshape(2 * cols, pair_channels)
        grad = dot(weight_ref[...], cot, ((1,), (1,))).astype(BF16)
        grad = grad.reshape(width, width, 2 * cols)
        grad_ref[:, i * width : (i + 1) * width, :] = grad[:, :, :cols]
        grad_ref[:, (i + 1) * width : (i + 2) * width, :] = grad[:, :, cols:]


def right_grad_kernel(fresh, cot_ref, weight_ref, left_ref, total_in_ref, bias_in_ref, *refs):
    right_ref, total_ref, bias_ref, grad_ref = refs[-4:]
    step = pl.program_id(0)
    rows, cols, pair_channels = cot_ref.shape
    width = grad_ref.shape[0]

    @pl.when(step == 0)
    def _():
        if fresh:
            total_ref[...] = jnp.zeros_like(total_ref)
            bias_ref[...] = jnp.zeros_like(bias_ref)
        else:
            total_ref[...] = total_in_ref[...]
            bias_ref[...] = bias_in_ref[...]

    bias_ref[...] += jnp.sum(
        cot_ref[...].astype(F32).reshape(rows * cols // 8, 8, pair_channels), axis=0
    )
    outer_grad_block(cot_ref, weight_ref, grad_ref)
    left = left_ref[...].T
    for d in range(0, width, 2):
        both = jnp.concatenate([grad_ref[d], grad_ref[d + 1]], axis=1)
        total_ref[:, d * cols : (d + 2) * cols] += dot(left, both, ((1,), (0,)))

    if not fresh:

        @pl.when(step == pl.num_programs(0) - 1)
        def _():
            right_ref[...] = total_ref[...].astype(BF16)


def right_grad_part(first, count, cotangent, weight, left, before, after=()):
    rows, cols, pair_channels = cotangent.shape
    seqs = left.shape[1]
    width = left.shape[0] // rows
    block = ROWS_AT_ONCE * width
    fresh = before is None
    if fresh:
        before = (None, jnp.zeros((8, pair_channels), F32), jnp.zeros((8, pair_channels), F32))
    right_shape = (8, pair_channels) if fresh else (seqs, width * cols)
    return pl.pallas_call(
        functools.partial(right_grad_kernel, fresh),
        grid=(count,),
        in_specs=[
            pl.BlockSpec((ROWS_AT_ONCE, cols, pair_channels), lambda n: (first + n, 0, 0)),
            whole((width * width, pair_channels)),
            pl.BlockSpec((block, seqs), lambda n: (first + n, 0)),
            whole(before[1].shape),
            whole(before[2].shape),
        ]
        + [ANYWHERE] * len(after),
        out_specs=[
            whole(right_shape),
            whole((seqs, width * cols)),
            whole((8, pair_channels)),
        ],
        out_shape=[
            jax.ShapeDtypeStruct(right_shape, BF16),
            jax.ShapeDtypeStruct((seqs, width * cols), F32),
            jax.ShapeDtypeStruct((8, pair_channels), F32),
        ],
        scratch_shapes=[pltpu.VMEM((width, block, cols), BF16)],
        compiler_params=params(),
        cost_estimate=cost(
            flops=4 * count * ROWS_AT_ONCE * cols * width * width * pair_channels,
            bytes_accessed=2 * count * ROWS_AT_ONCE * cols * pair_channels,
            transcendentals=0,
        ),
        name="right_grad",
    )(cotangent, weight, left, before[1], before[2], *after)


def left_grad_kernel(turn_ref, *refs):
    piece_refs, (cot_ref, weight_ref, out_ref, cols_ref, grad_ref) = refs[: 2 * RING], refs[-5:]
    width, _, cols = grad_ref.shape
    quarter = piece_refs[0].shape[0]

    @pl.when(pl.program_id(0) == 0)
    def _():
        for d in range(width):
            here = slice(d * cols, (d + 1) * cols)
            part = jnp.concatenate([piece[:, here] for piece in piece_refs], axis=0)
            cols_ref[here, :] = part.T

    outer_grad_block(cot_ref, weight_ref, grad_ref)
    total = None
    for d in range(0, width, 2):
        both = jnp.concatenate([grad_ref[d], grad_ref[d + 1]], axis=1)
        term = dot(both, cols_ref[d * cols : (d + 2) * cols, :], ((1,), (0,)))
        total = term if total is None else total + term
    total = total.T.astype(BF16)
    for p in range(RING):
        place = lax.rem(turn_ref[0] + p, RING)
        for h in range(2):
            first = (h * RING + p) * quarter
            out_ref[place, h * quarter : (h + 1) * quarter, :] = total[first : first + quarter]


def left_grad_part(turn, pieces, cotangent, weight, after=()):
    rows, cols, pair_channels = cotangent.shape
    quarter = pieces[0].shape[0]
    width = pieces[0].shape[1] // cols
    blocks, block = rows // ROWS_AT_ONCE, ROWS_AT_ONCE * width
    seqs = 2 * RING * quarter
    return pl.pallas_call(
        left_grad_kernel,
        grid_spec=pltpu.PrefetchScalarGridSpec(
            num_scalar_prefetch=1,
            grid=(blocks,),
            in_specs=[whole(piece.shape) for piece in pieces]
            + [ANYWHERE] * len(after)
            + [
                pl.BlockSpec((ROWS_AT_ONCE, cols, pair_channels), lambda n, turn_ref: (n, 0, 0)),
                whole((width * width, pair_channels)),
            ],
            out_specs=pl.BlockSpec((RING, 2 * quarter, block), lambda n, turn_ref: (0, 0, n)),
            scratch_shapes=[
                pltpu.VMEM((width * cols, seqs), BF16),
                pltpu.VMEM((width, block, cols), BF16),
            ],
        ),
        out_shape=jax.ShapeDtypeStruct((RING, 2 * quarter, blocks * block), BF16),
        compiler_params=params(),
        cost_estimate=cost(
            flops=4 * blocks * width * block * cols * (seqs + pair_channels),
            bytes_accessed=4 * seqs * width * cols,
            transcendentals=0,
        ),
        name="left_grad",
    )(
        turn.reshape(1),
        *pieces,
        *after,
        cotangent,
        weight,
    )


def add_kernel(count, scale, *refs):
    total = refs[0][...].astype(F32)
    for ref in refs[1:count]:
        total = total + ref[...].astype(F32)
    refs[-1][...] = (total * scale).astype(BF16)


def add_up(parts, scale=1.0, after=()):
    return pl.pallas_call(
        lambda *refs: add_kernel(len(parts), scale, *refs),
        in_specs=[pl.BlockSpec(memory_space=pltpu.VMEM)] * len(parts) + [ANYWHERE] * len(after),
        out_specs=pl.BlockSpec(memory_space=pltpu.VMEM),
        out_shape=jax.ShapeDtypeStruct(parts[0].shape, BF16),
        compiler_params=pltpu.CompilerParams(vmem_limit_bytes=VMEM_LIMIT),
        name="add_up",
    )(*parts, *after)


def pair_kernel(fresh, *refs):
    piece_refs, refs = refs[: 2 * RING], refs[2 * RING :]
    left_ref, weight_ref, bias_ref, cot_ref, before_ref = refs[:5]
    pair_ref, total_ref, cols_ref, outer_ref = refs[-4:]
    rows, cols, pair_channels = cot_ref.shape
    width = outer_ref.shape[0]
    inv_seqs = 1.0 / cols_ref.shape[0]

    @pl.when(pl.program_id(0) == 0)
    def _():
        first = 0
        for piece in piece_refs:
            cols_ref[first : first + piece.shape[0], :] = piece[...]
            first += piece.shape[0]
        total_ref[...] = jnp.zeros_like(total_ref) if fresh else before_ref[...]

    for d in range(0, width, 2):
        both = dot(left_ref[...], cols_ref[:, d * cols : (d + 2) * cols], ((1,), (0,)))
        both = (both * inv_seqs).astype(BF16)
        outer_ref[d] = both[:, :cols]
        outer_ref[d + 1] = both[:, cols:]
    for i in range(0, rows, 2):
        outer = jnp.concatenate(
            [
                outer_ref[:, n * width : (n + 1) * width, :].reshape(width * width, cols)
                for n in (i, i + 1)
            ],
            axis=1,
        )
        cot = cot_ref[i : i + 2].reshape(2 * cols, pair_channels)
        total_ref[...] += dot(outer, cot, ((1,), (0,)))
        pair = dot(weight_ref[...], outer, ((1,), (0,))).T + bias_ref[...]
        pair_ref[i : i + 2] = pair.astype(BF16).reshape(2, cols, pair_channels)


def pair_and_weight_grad(first, count, pieces, left, weight, bias, cotangent, before, after=()):
    rows, cols, pair_channels = cotangent.shape
    seqs = left.shape[1]
    width = left.shape[0] // rows
    block = ROWS_AT_ONCE * width
    fresh = before is None
    if fresh:
        before = (None, jnp.zeros((8, pair_channels), F32))
    operands = [*pieces, left, weight, bias.reshape(1, -1), cotangent, before[1], *after]
    in_specs = [whole(piece.shape) for piece in pieces] + [
        pl.BlockSpec((block, seqs), lambda n: (first + n, 0)),
        whole((pair_channels, width * width)),
        whole((1, pair_channels)),
        pl.BlockSpec((ROWS_AT_ONCE, cols, pair_channels), lambda n: (first + n, 0, 0)),
        whole(before[1].shape),
    ]
    in_specs += [ANYWHERE] * len(after)
    aliases = {}
    if not fresh:
        aliases = {len(operands): 0}
        operands.append(before[0])
        in_specs.append(ANYWHERE)
    return pl.pallas_call(
        functools.partial(pair_kernel, fresh),
        grid=(count,),
        in_specs=in_specs,
        out_specs=[
            pl.BlockSpec((ROWS_AT_ONCE, cols, pair_channels), lambda n: (first + n, 0, 0)),
            whole((width * width, pair_channels)),
        ],
        out_shape=[
            jax.ShapeDtypeStruct((rows, cols, pair_channels), BF16),
            jax.ShapeDtypeStruct((width * width, pair_channels), F32),
        ],
        scratch_shapes=[
            pltpu.VMEM((seqs, width * cols), BF16),
            pltpu.VMEM((width, block, cols), BF16),
        ],
        input_output_aliases=aliases,
        compiler_params=params(),
        cost_estimate=cost(
            flops=4 * count * ROWS_AT_ONCE * cols * width * width * (2 * pair_channels + seqs),
            bytes_accessed=4 * count * ROWS_AT_ONCE * cols * pair_channels,
            transcendentals=0,
        ),
        name="pair_update",
    )(*operands)


def projection_grad_kernel(place_ref, features_ref, gain_ref, offset_ref, grads_ref, out_ref):
    seqs = features_ref.shape[0]
    total = None
    for s in range(seqs):
        rescaled = norm_rows(features_ref[s])
        normed = (rescaled * gain_ref[...] + offset_ref[...]).astype(BF16)
        term = dot(grads_ref[s], normed, ((1,), (0,)))
        total = term if total is None else total + term
    out_ref[...] = total


def projection_grad_part(x, low_y, features, gain, offset, grads):
    _, residues, channels = features.shape
    quarter, both_widths, _ = grads.shape
    eighth = quarter // 2
    place = jnp.stack([x * 2 + low_y, low_y])
    return pl.pallas_call(
        projection_grad_kernel,
        grid_spec=pltpu.PrefetchScalarGridSpec(
            num_scalar_prefetch=1,
            grid=(1,),
            in_specs=[
                pl.BlockSpec((eighth, residues, channels), lambda n, ref: (ref[0], 0, 0)),
                whole((1, channels)),
                whole((1, channels)),
                pl.BlockSpec((eighth, both_widths, residues), lambda n, ref: (ref[1], 0, 0)),
            ],
            out_specs=whole((both_widths, channels)),
        ),
        out_shape=jax.ShapeDtypeStruct((both_widths, channels), F32),
        compiler_params=params(),
        name="projection_grad",
    )(place, features, gain, offset, grads)


def norm_grad_kernel(count, first_ref, features_ref, gain_ref, weight_ref, *refs):
    piece_refs, (out_ref, token_ref, grads_ref) = refs[:count], refs[-3:]
    token_ref[...] = jnp.zeros_like(token_ref)
    step = pl.program_id(0)
    seqs, residues, channels = features_ref.shape
    steps = piece_refs[0].shape[0] // seqs
    for t in range(len(piece_refs)):

        @pl.when(step // steps == t)
        def _(t=t):
            grads_ref[...] = piece_refs[t][pl.ds(lax.rem(step, steps) * seqs, seqs)]

    at_once = 4
    for s in range(0, seqs, at_once):
        features = features_ref[s : s + at_once].reshape(at_once * residues, channels)
        rescaled, inverse_deviation = norm_block(features)
        grad = [dot(grads_ref[s + n], weight_ref[...], ((0,), (0,))) for n in range(at_once)]
        grad = jnp.concatenate(grad, axis=0) * gain_ref[...]
        grad = inverse_deviation * (grad - row_mean(grad) - rescaled * row_mean(grad * rescaled))
        out_ref[s : s + at_once] = grad.astype(BF16).reshape(at_once, residues, channels)


def norm_grad(first, pieces, features, gain, weight, before=None, after=()):
    _, residues, channels = features.shape
    quarter, both_widths, _ = pieces[0].shape
    seqs = 8
    steps = quarter // seqs

    def place(n, first_ref):
        return (lax.rem(n // steps + first_ref[0], RING) * steps + lax.rem(n, steps), 0, 0)

    operands = [first.reshape(1), features, gain, weight, *pieces, *after]
    in_specs = [
        pl.BlockSpec((seqs, residues, channels), place),
        whole((1, channels)),
        whole(weight.shape),
    ]
    in_specs += [whole(piece.shape) for piece in pieces] + [ANYWHERE] * len(after)
    aliases = {}
    if before is not None:
        aliases = {len(operands): 0}
        operands.append(before)
        in_specs.append(ANYWHERE)
    return pl.pallas_call(
        functools.partial(norm_grad_kernel, len(pieces)),
        grid_spec=pltpu.PrefetchScalarGridSpec(
            num_scalar_prefetch=1,
            grid=(len(pieces) * steps,),
            in_specs=in_specs,
            out_specs=[pl.BlockSpec((seqs, residues, channels), place), whole((8, 128))],
            scratch_shapes=[pltpu.VMEM((seqs, both_widths, residues), BF16)],
        ),
        out_shape=[
            jax.ShapeDtypeStruct(features.shape, BF16),
            jax.ShapeDtypeStruct((8, 128), F32),
        ],
        input_output_aliases=aliases,
        compiler_params=params(),
        cost_estimate=cost(
            flops=4 * len(pieces) * quarter * residues * channels * both_widths,
            bytes_accessed=4 * len(pieces) * quarter * residues * channels,
            transcendentals=0,
        ),
        name="norm_grad",
    )(*operands)


def share_kernel(scale, terms_ref, *refs):
    share_ref, spread_ref = refs[-2:]
    total = terms_ref[0].astype(F32)
    for n in range(1, terms_ref.shape[0]):
        total = total + terms_ref[n].astype(F32)
    total = total * scale
    share_ref[...] = total
    spread_ref[...] = jnp.broadcast_to(total.astype(BF16), spread_ref.shape)


def add_terms(terms, scale, after=()):
    return pl.pallas_call(
        functools.partial(share_kernel, scale),
        in_specs=[pl.BlockSpec(memory_space=pltpu.VMEM)] + [ANYWHERE] * len(after),
        out_specs=[pl.BlockSpec(memory_space=pltpu.VMEM)] * 2,
        out_shape=[
            jax.ShapeDtypeStruct(terms.shape[1:], F32),
            jax.ShapeDtypeStruct(terms.shape, BF16),
        ],
        compiler_params=pltpu.CompilerParams(vmem_limit_bytes=VMEM_LIMIT),
        name="add_terms",
    )(terms, *after)


def terms_kernel(weight_ref, projection_ref, bias_ref, *refs):
    out_ref, token_ref = refs[-2:]
    token_ref[...] = jnp.zeros_like(token_ref)
    devices, rows, lanes = out_ref.shape
    weight_rows = weight_ref.shape[0] // devices
    bias = jnp.sum(bias_ref[...], axis=0, keepdims=True)
    bias_high = bias.astype(BF16).astype(F32)
    tail = jnp.concatenate(
        [bias_high, bias - bias_high, jnp.zeros((rows - weight_rows - 3, lanes), F32)], axis=0
    )
    for n in range(devices):
        block = [
            weight_ref[n * weight_rows : (n + 1) * weight_rows, :],
            projection_ref[n : n + 1, :],
            tail,
        ]
        out_ref[n] = jnp.concatenate(block, axis=0).astype(BF16)


def gather_terms(devices, weight_part, projection_part, bias_part, after=()):
    lanes = weight_part.shape[1]
    return pl.pallas_call(
        terms_kernel,
        in_specs=[pl.BlockSpec(memory_space=pltpu.VMEM)] * 3 + [ANYWHERE] * len(after),
        out_specs=[pl.BlockSpec(memory_space=pltpu.VMEM)] * 2,
        out_shape=[
            jax.ShapeDtypeStruct((devices, 16, lanes), BF16),
            jax.ShapeDtypeStruct((8, lanes), F32),
        ],
        compiler_params=pltpu.CompilerParams(vmem_limit_bytes=VMEM_LIMIT),
        name="gather_terms",
    )(weight_part, projection_part.reshape(devices, lanes), bias_part, *after)


def torus_permute(value, move):
    pairs = []
    for z in range(RING):
        for y in range(RING):
            for x in range(RING):
                for s in range(2):
                    tx, ty, tz, ts = move(x, y, z, s)
                    tx, ty, tz = tx % RING, ty % RING, tz % RING
                    source = ((z * 2 + y // 2) * 8 + x * 2 + y % 2) * 2 + s
                    target = ((tz * 2 + ty // 2) * 8 + tx * 2 + ty % 2) * 2 + ts
                    pairs.append((source, target))
    return lax.ppermute(value, AXES, pairs)


def swap_cores(value):
    return torus_permute(value, lambda x, y, z, s: (x, y, z, 1 - s))


def swap_low_y(value):
    return torus_permute(value, lambda x, y, z, s: (x, y ^ 1, z, s))


def swap_both(value):
    return torus_permute(value, lambda x, y, z, s: (x, y ^ 1, z, 1 - s))


def shift_z(value, steps):
    return torus_permute(value, lambda x, y, z, s: (x, y, z + steps, s))


def shift_x(value, steps):
    return torus_permute(value, lambda x, y, z, s: (x + steps, y, z, s))


def transpose_xz(value):
    return torus_permute(value, lambda x, y, z, s: (z, SWAP_Y[y], x, s))


def body(
    alignment_features,
    norm_gain_vector,
    norm_offset_vector,
    projection_weight,
    output_weight,
    output_bias,
    pair_update_cotangent,
):
    half, residues, channels = alignment_features.shape
    width = projection_weight.shape[1] // 2
    pair_channels = output_weight.shape[1]
    rows, cols, _ = pair_update_cotangent.shape
    rows_total = residues * lax.axis_size("ia")
    quarter = half // RING
    inv_seqs = 1.0 / (half * 2)
    x = lax.axis_index("ja") // 2
    low_y = lax.axis_index("ja") % 2
    z = lax.axis_index("ia") // 2
    core = lax.axis_index("sa")
    features = pltpu.with_memory_space_constraint(alignment_features, pltpu.HBM)
    cotangent = pair_update_cotangent
    gain_row = norm_gain_vector.reshape(1, -1)
    offset_row = norm_offset_vector.reshape(1, -1)
    weight_rows = projection_weight.T

    right_piece = project(
        x * 2,
        quarter,
        x * 0,
        residues,
        features,
        pltpu.with_memory_space_constraint(gain_row, pltpu.HBM),
        pltpu.with_memory_space_constraint(offset_row, pltpu.HBM),
        weight_rows[width:],
    )
    arrived = transpose_xz(right_piece.reshape(quarter, width * residues))

    def left_rows(part):
        return project(
            z,
            half,
            part,
            rows,
            alignment_features,
            gain_row,
            offset_row,
            weight_rows[:width],
            after=(right_piece,),
        )

    left_came = swap_cores(left_rows(1 - core)).transpose(2, 1, 0)
    left_kept = left_rows(core).transpose(2, 1, 0)
    own_left = jnp.concatenate([left_kept, left_came], axis=2).reshape(rows * width, 2 * half)

    arrived = add_up([arrived], after=(own_left,))
    right_pieces = [arrived] + [shift_z(arrived, -t) for t in range(1, RING)]
    right_cols = right_pieces + [swap_cores(piece) for piece in right_pieces]

    weight_dc = (
        output_weight.reshape(width, width, pair_channels)
        .transpose(1, 0, 2)
        .reshape(width * width, pair_channels)
    )
    blocks = rows // ROWS_AT_ONCE
    part = right_grad_part(
        0, blocks // 2, cotangent, weight_dc, own_left, None, after=(arrived,)
    )
    right_partial, _, bias_partial = right_grad_part(
        blocks // 2,
        blocks // 2,
        cotangent,
        weight_dc,
        own_left,
        part,
        after=tuple(right_pieces[1:]),
    )

    right_sum = add_up([right_partial[:half], swap_cores(right_partial[half:])])
    pieces = [right_sum[t * quarter : (t + 1) * quarter] for t in range(RING)]
    right_came = [shift_z(pieces[t], t) for t in range(1, RING)]
    left_partial = left_grad_part(
        lax.rem(z - x + RING, RING),
        right_cols,
        cotangent,
        weight_dc,
        after=(right_sum,),
    )

    left_came = [shift_x(left_partial[t], t) for t in range(1, RING)]
    right_sum = transpose_xz(add_up([pieces[0], *right_came], after=(left_partial,)))

    def pair_part(first, count, before, after):
        return pair_and_weight_grad(
            first,
            count,
            right_cols,
            own_left,
            weight_dc.T,
            output_bias,
            cotangent,
            before,
            after,
        )

    pair = pair_part(0, 4, None, (left_partial,))
    left_sum = add_up([left_partial[0], *left_came], after=(pair[1], right_sum))

    left_own, left_other = left_sum[:quarter], left_sum[quarter:]
    own_beside, right_beside = swap_low_y(left_own), swap_low_y(right_sum)
    other_here, other_beside = swap_cores(left_other), swap_both(left_other)
    pair = pair_part(4, 2, pair, (left_sum,))
    left_own = add_up([left_own, own_beside], inv_seqs, after=(pair[1],))
    left_came = add_up([other_here, other_beside], inv_seqs, after=(pair[1],))
    right_grad = add_up([right_sum, right_beside], inv_seqs, after=(pair[1],))

    left_low = jnp.where(core == 0, left_own, left_came).reshape(quarter, rows, width)
    left_high = jnp.where(core == 0, left_came, left_own).reshape(quarter, rows, width)
    left_grad = jnp.concatenate(
        [left_low.transpose(0, 2, 1), left_high.transpose(0, 2, 1)], axis=2
    )
    grads = jnp.concatenate([left_grad, right_grad.reshape(quarter, width, residues)], axis=1)
    grad_pieces = [grads] + [shift_x(grads, -t) for t in range(1, RING)]

    pair_update_result, weight_partial = pair_part(6, blocks - 6, pair, (grads,))
    projection_part = projection_grad_part(x, low_y, features, gain_row, offset_row, grads)
    devices = 128
    terms, token = gather_terms(
        devices, weight_partial, projection_part, bias_partial, after=tuple(grad_pieces[1:])
    )

    came = lax.all_to_all(terms, AXES, 0, 0, tiled=True)

    def norm_part(first, before, after):
        pieces = grad_pieces[first : first + 2]
        place = lax.rem(x + first, RING)
        return norm_grad(
            place, pieces, features, gain_row, weight_rows, before, after
        )

    alignment_gradient, token = norm_part(0, None, (token,))
    share, spread = add_terms(came, 1.0 / rows_total, after=(token,))
    bias_sum = share[9] + share[10]
    everything = lax.all_to_all(spread, AXES, 0, 0, tiled=True).astype(F32)
    alignment_gradient, _ = norm_part(2, alignment_gradient, (share,))
    weight_sum = (
        everything[:, :8]
        .reshape(width, width, pair_channels)
        .transpose(1, 0, 2)
        .reshape(width * width, pair_channels)
    )
    projection_sum = everything[:, 8].reshape(2 * width, channels).T

    return (
        pair_update_result,
        alignment_gradient,
        projection_sum,
        weight_sum,
        bias_sum,
    )


def solution(mesh):
    in_specs = (P("sa", "ia", None), P(), P(), P(), P(), P(), P(("ia", "sa"), "ja", None))
    out_specs = (P(("ia", "sa"), "ja", None), P("sa", "ia", None), P(), P(), P())
    return jax.shard_map(body, mesh=mesh, in_specs=in_specs, out_specs=out_specs, check_vma=False)
```

```python
import functools

import jax
import jax.numpy as jnp
from jax import lax
from jax.experimental import pallas as pl
from jax.experimental.pallas import tpu as pltpu
from jax.sharding import PartitionSpec as P

epsilon = 1e-05
AXES = ("ia", "ja", "sa")
RING = 4
SWAP_Y = (0, 2, 1, 3)
ROWS_AT_ONCE = 16
BF16 = jnp.bfloat16
F32 = jnp.float32
VMEM_LIMIT = 20 * 1024 * 1024


def dot(a, b, contract):
    return lax.dot_general(a, b, (contract, ((), ())), preferred_element_type=F32)


def params(limit=VMEM_LIMIT):
    return pltpu.CompilerParams(dimension_semantics=("arbitrary",), vmem_limit_bytes=limit)


ANYWHERE = pl.BlockSpec(memory_space=pl.ANY)


def cost(flops, bytes_accessed, transcendentals):
    return pl.CostEstimate(
        flops=flops, bytes_accessed=bytes_accessed, transcendentals=transcendentals
    )


def whole(shape):
    return pl.BlockSpec(shape, lambda *_: (0,) * len(shape))


def row_mean(values):
    channels = values.shape[-1]
    ones = jnp.full((channels, 128), 1.0 / channels, BF16)
    mean = dot(values.astype(BF16), ones, ((1,), (0,)))
    return jnp.concatenate([mean] * (channels // 128), axis=1)


def norm_block(features):
    centred = features.astype(F32) - row_mean(features)
    inverse_deviation = lax.rsqrt(row_mean(centred * centred) + epsilon)
    return centred * inverse_deviation, inverse_deviation


def norm_rows(features):
    values = features.astype(F32)
    scale = 1.0 / values.shape[-1]
    centred = values - jnp.sum(values, axis=-1, keepdims=True) * scale
    variance = jnp.sum(centred * centred, axis=-1, keepdims=True) * scale
    return centred * lax.rsqrt(variance + epsilon)


def project_kernel(place_ref, features_ref, gain_ref, offset_ref, weight_ref, *refs):
    out_ref = refs[-1]
    seqs, residues, channels = features_ref.shape
    at_once = 256 // residues
    for s in range(0, seqs, at_once):
        rescaled = norm_rows(
            features_ref[s : s + at_once].reshape(at_once * residues, channels)
        )
        normed = (rescaled * gain_ref[...] + offset_ref[...]).astype(BF16)
        several = dot(weight_ref[...], normed, ((1,), (1,))).astype(BF16)
        for n in range(at_once):
            out_ref[s + n] = several[:, n * residues : (n + 1) * residues]


def project(first, count, part, residues, features, gain, offset, weight, after=()):
    total, _, channels = features.shape
    width = weight.shape[0]
    seqs = min(2048 // residues, 16)
    steps = total // seqs

    def place(n, place_ref):
        return (lax.rem(place_ref[0] + n, steps), place_ref[1], 0)

    return pl.pallas_call(
        project_kernel,
        grid_spec=pltpu.PrefetchScalarGridSpec(
            num_scalar_prefetch=1,
            grid=(count // seqs,),
            in_specs=[
                pl.BlockSpec((seqs, residues, channels), place),
                whole((1, channels)),
                whole((1, channels)),
                whole((width, channels)),
            ]
            + [ANYWHERE] * len(after),
            out_specs=pl.BlockSpec((seqs, width, residues), lambda n, place_ref: (n, 0, 0)),
        ),
        out_shape=jax.ShapeDtypeStruct((count, width, residues), BF16),
        compiler_params=params(),
        cost_estimate=cost(
            flops=4 * count * residues * channels * width,
            bytes_accessed=2 * count * residues * (channels + width),
            transcendentals=count * residues,
        ),
        name="project",
    )(jnp.stack([first, part]), features, gain, offset, weight, *after)


def outer_grad_block(cot_ref, weight_ref, grad_ref):
    rows, cols, pair_channels = cot_ref.shape
    width = grad_ref.shape[0]
    for i in range(0, rows, 2):
        cot = cot_ref[i : i + 2].reshape(2 * cols, pair_channels)
        grad = dot(weight_ref[...], cot, ((1,), (1,))).astype(BF16)
        grad = grad.reshape(width, width, 2 * cols)
        grad_ref[:, i * width : (i + 1) * width, :] = grad[:, :, :cols]
        grad_ref[:, (i + 1) * width : (i + 2) * width, :] = grad[:, :, cols:]


def right_grad_kernel(fresh, cot_ref, weight_ref, left_ref, total_in_ref, bias_in_ref, *refs):
    right_ref, total_ref, bias_ref, grad_ref = refs[-4:]
    step = pl.program_id(0)
    rows, cols, pair_channels = cot_ref.shape
    width = grad_ref.shape[0]

    @pl.when(step == 0)
    def _():
        if fresh:
            total_ref[...] = jnp.zeros_like(total_ref)
            bias_ref[...] = jnp.zeros_like(bias_ref)
        else:
            total_ref[...] = total_in_ref[...]
            bias_ref[...] = bias_in_ref[...]

    bias_ref[...] += jnp.sum(
        cot_ref[...].astype(F32).reshape(rows * cols // 8, 8, pair_channels), axis=0
    )
    outer_grad_block(cot_ref, weight_ref, grad_ref)
    left = left_ref[...].T
    for d in range(0, width, 2):
        both = jnp.concatenate([grad_ref[d], grad_ref[d + 1]], axis=1)
        total_ref[:, d * cols : (d + 2) * cols] += dot(left, both, ((1,), (0,)))

    if not fresh:

        @pl.when(step == pl.num_programs(0) - 1)
        def _():
            right_ref[...] = total_ref[...].astype(BF16)


def right_grad_part(first, count, cotangent, weight, left, before, after=()):
    rows, cols, pair_channels = cotangent.shape
    seqs = left.shape[1]
    width = left.shape[0] // rows
    block = ROWS_AT_ONCE * width
    fresh = before is None
    if fresh:
        before = (None, jnp.zeros((8, pair_channels), F32), jnp.zeros((8, pair_channels), F32))
    right_shape = (8, pair_channels) if fresh else (seqs, width * cols)
    return pl.pallas_call(
        functools.partial(right_grad_kernel, fresh),
        grid=(count,),
        in_specs=[
            pl.BlockSpec((ROWS_AT_ONCE, cols, pair_channels), lambda n: (first + n, 0, 0)),
            whole((width * width, pair_channels)),
            pl.BlockSpec((block, seqs), lambda n: (first + n, 0)),
            whole(before[1].shape),
            whole(before[2].shape),
        ]
        + [ANYWHERE] * len(after),
        out_specs=[
            whole(right_shape),
            whole((seqs, width * cols)),
            whole((8, pair_channels)),
        ],
        out_shape=[
            jax.ShapeDtypeStruct(right_shape, BF16),
            jax.ShapeDtypeStruct((seqs, width * cols), F32),
            jax.ShapeDtypeStruct((8, pair_channels), F32),
        ],
        scratch_shapes=[pltpu.VMEM((width, block, cols), BF16)],
        compiler_params=params(),
        cost_estimate=cost(
            flops=4 * count * ROWS_AT_ONCE * cols * width * width * pair_channels,
            bytes_accessed=2 * count * ROWS_AT_ONCE * cols * pair_channels,
            transcendentals=0,
        ),
        name="right_grad",
    )(cotangent, weight, left, before[1], before[2], *after)


def left_grad_kernel(turn_ref, *refs):
    piece_refs, (cot_ref, weight_ref, out_ref, cols_ref, grad_ref) = refs[: 2 * RING], refs[-5:]
    width, _, cols = grad_ref.shape
    quarter = piece_refs[0].shape[0]

    @pl.when(pl.program_id(0) == 0)
    def _():
        for d in range(width):
            here = slice(d * cols, (d + 1) * cols)
            part = jnp.concatenate([piece[:, here] for piece in piece_refs], axis=0)
            cols_ref[here, :] = part.T

    outer_grad_block(cot_ref, weight_ref, grad_ref)
    total = None
    for d in range(0, width, 2):
        both = jnp.concatenate([grad_ref[d], grad_ref[d + 1]], axis=1)
        term = dot(both, cols_ref[d * cols : (d + 2) * cols, :], ((1,), (0,)))
        total = term if total is None else total + term
    total = total.T.astype(BF16)
    for p in range(RING):
        place = lax.rem(turn_ref[0] + p, RING)
        for h in range(2):
            first = (h * RING + p) * quarter
            out_ref[place, h * quarter : (h + 1) * quarter, :] = total[first : first + quarter]


def left_grad_part(turn, pieces, cotangent, weight, after=()):
    rows, cols, pair_channels = cotangent.shape
    quarter = pieces[0].shape[0]
    width = pieces[0].shape[1] // cols
    blocks, block = rows // ROWS_AT_ONCE, ROWS_AT_ONCE * width
    seqs = 2 * RING * quarter
    return pl.pallas_call(
        left_grad_kernel,
        grid_spec=pltpu.PrefetchScalarGridSpec(
            num_scalar_prefetch=1,
            grid=(blocks,),
            in_specs=[whole(piece.shape) for piece in pieces]
            + [ANYWHERE] * len(after)
            + [
                pl.BlockSpec((ROWS_AT_ONCE, cols, pair_channels), lambda n, turn_ref: (n, 0, 0)),
                whole((width * width, pair_channels)),
            ],
            out_specs=pl.BlockSpec((RING, 2 * quarter, block), lambda n, turn_ref: (0, 0, n)),
            scratch_shapes=[
                pltpu.VMEM((width * cols, seqs), BF16),
                pltpu.VMEM((width, block, cols), BF16),
            ],
        ),
        out_shape=jax.ShapeDtypeStruct((RING, 2 * quarter, blocks * block), BF16),
        compiler_params=params(),
        cost_estimate=cost(
            flops=4 * blocks * width * block * cols * (seqs + pair_channels),
            bytes_accessed=4 * seqs * width * cols,
            transcendentals=0,
        ),
        name="left_grad",
    )(
        turn.reshape(1),
        *pieces,
        *after,
        cotangent,
        weight,
    )


def add_kernel(count, scale, *refs):
    total = refs[0][...].astype(F32)
    for ref in refs[1:count]:
        total = total + ref[...].astype(F32)
    refs[-1][...] = (total * scale).astype(BF16)


def add_up(parts, scale=1.0, after=()):
    return pl.pallas_call(
        lambda *refs: add_kernel(len(parts), scale, *refs),
        in_specs=[pl.BlockSpec(memory_space=pltpu.VMEM)] * len(parts) + [ANYWHERE] * len(after),
        out_specs=pl.BlockSpec(memory_space=pltpu.VMEM),
        out_shape=jax.ShapeDtypeStruct(parts[0].shape, BF16),
        compiler_params=pltpu.CompilerParams(vmem_limit_bytes=VMEM_LIMIT),
        name="add_up",
    )(*parts, *after)


def pair_kernel(fresh, *refs):
    piece_refs, refs = refs[: 2 * RING], refs[2 * RING :]
    left_ref, weight_ref, bias_ref, cot_ref, before_ref = refs[:5]
    pair_ref, total_ref, cols_ref, outer_ref = refs[-4:]
    rows, cols, pair_channels = cot_ref.shape
    width = outer_ref.shape[0]
    inv_seqs = 1.0 / cols_ref.shape[0]

    @pl.when(pl.program_id(0) == 0)
    def _():
        first = 0
        for piece in piece_refs:
            cols_ref[first : first + piece.shape[0], :] = piece[...]
            first += piece.shape[0]
        total_ref[...] = jnp.zeros_like(total_ref) if fresh else before_ref[...]

    for d in range(0, width, 2):
        both = dot(left_ref[...], cols_ref[:, d * cols : (d + 2) * cols], ((1,), (0,)))
        both = (both * inv_seqs).astype(BF16)
        outer_ref[d] = both[:, :cols]
        outer_ref[d + 1] = both[:, cols:]
    for i in range(0, rows, 2):
        outer = jnp.concatenate(
            [
                outer_ref[:, n * width : (n + 1) * width, :].reshape(width * width, cols)
                for n in (i, i + 1)
            ],
            axis=1,
        )
        cot = cot_ref[i : i + 2].reshape(2 * cols, pair_channels)
        total_ref[...] += dot(outer, cot, ((1,), (0,)))
        pair = dot(weight_ref[...], outer, ((1,), (0,))).T + bias_ref[...]
        pair_ref[i : i + 2] = pair.astype(BF16).reshape(2, cols, pair_channels)


def pair_and_weight_grad(first, count, pieces, left, weight, bias, cotangent, before, after=()):
    rows, cols, pair_channels = cotangent.shape
    seqs = left.shape[1]
    width = left.shape[0] // rows
    block = ROWS_AT_ONCE * width
    fresh = before is None
    if fresh:
        before = (None, jnp.zeros((8, pair_channels), F32))
    operands = [*pieces, left, weight, bias.reshape(1, -1), cotangent, before[1], *after]
    in_specs = [whole(piece.shape) for piece in pieces] + [
        pl.BlockSpec((block, seqs), lambda n: (first + n, 0)),
        whole((pair_channels, width * width)),
        whole((1, pair_channels)),
        pl.BlockSpec((ROWS_AT_ONCE, cols, pair_channels), lambda n: (first + n, 0, 0)),
        whole(before[1].shape),
    ]
    in_specs += [ANYWHERE] * len(after)
    aliases = {}
    if not fresh:
        aliases = {len(operands): 0}
        operands.append(before[0])
        in_specs.append(ANYWHERE)
    return pl.pallas_call(
        functools.partial(pair_kernel, fresh),
        grid=(count,),
        in_specs=in_specs,
        out_specs=[
            pl.BlockSpec((ROWS_AT_ONCE, cols, pair_channels), lambda n: (first + n, 0, 0)),
            whole((width * width, pair_channels)),
        ],
        out_shape=[
            jax.ShapeDtypeStruct((rows, cols, pair_channels), BF16),
            jax.ShapeDtypeStruct((width * width, pair_channels), F32),
        ],
        scratch_shapes=[
            pltpu.VMEM((seqs, width * cols), BF16),
            pltpu.VMEM((width, block, cols), BF16),
        ],
        input_output_aliases=aliases,
        compiler_params=params(),
        cost_estimate=cost(
            flops=4 * count * ROWS_AT_ONCE * cols * width * width * (2 * pair_channels + seqs),
            bytes_accessed=4 * count * ROWS_AT_ONCE * cols * pair_channels,
            transcendentals=0,
        ),
        name="pair_update",
    )(*operands)


def projection_grad_kernel(place_ref, features_ref, gain_ref, offset_ref, grads_ref, out_ref):
    seqs = features_ref.shape[0]
    total = None
    for s in range(seqs):
        rescaled = norm_rows(features_ref[s])
        normed = (rescaled * gain_ref[...] + offset_ref[...]).astype(BF16)
        term = dot(grads_ref[s], normed, ((1,), (0,)))
        total = term if total is None else total + term
    out_ref[...] = total


def projection_grad_part(x, low_y, features, gain, offset, grads):
    _, residues, channels = features.shape
    quarter, both_widths, _ = grads.shape
    eighth = quarter // 2
    place = jnp.stack([x * 2 + low_y, low_y])
    return pl.pallas_call(
        projection_grad_kernel,
        grid_spec=pltpu.PrefetchScalarGridSpec(
            num_scalar_prefetch=1,
            grid=(1,),
            in_specs=[
                pl.BlockSpec((eighth, residues, channels), lambda n, ref: (ref[0], 0, 0)),
                whole((1, channels)),
                whole((1, channels)),
                pl.BlockSpec((eighth, both_widths, residues), lambda n, ref: (ref[1], 0, 0)),
            ],
            out_specs=whole((both_widths, channels)),
        ),
        out_shape=jax.ShapeDtypeStruct((both_widths, channels), F32),
        compiler_params=params(),
        name="projection_grad",
    )(place, features, gain, offset, grads)


def norm_grad_kernel(count, first_ref, features_ref, gain_ref, weight_ref, *refs):
    piece_refs, (out_ref, token_ref, grads_ref) = refs[:count], refs[-3:]
    token_ref[...] = jnp.zeros_like(token_ref)
    step = pl.program_id(0)
    seqs, residues, channels = features_ref.shape
    steps = piece_refs[0].shape[0] // seqs
    for t in range(len(piece_refs)):

        @pl.when(step // steps == t)
        def _(t=t):
            grads_ref[...] = piece_refs[t][pl.ds(lax.rem(step, steps) * seqs, seqs)]

    at_once = 4
    for s in range(0, seqs, at_once):
        features = features_ref[s : s + at_once].reshape(at_once * residues, channels)
        rescaled, inverse_deviation = norm_block(features)
        grad = [dot(grads_ref[s + n], weight_ref[...], ((0,), (0,))) for n in range(at_once)]
        grad = jnp.concatenate(grad, axis=0) * gain_ref[...]
        grad = inverse_deviation * (grad - row_mean(grad) - rescaled * row_mean(grad * rescaled))
        out_ref[s : s + at_once] = grad.astype(BF16).reshape(at_once, residues, channels)


def norm_grad(first, pieces, features, gain, weight, before=None, after=()):
    _, residues, channels = features.shape
    quarter, both_widths, _ = pieces[0].shape
    seqs = quarter
    steps = 1

    def place(n, first_ref):
        return (lax.rem(n // steps + first_ref[0], RING) * steps + lax.rem(n, steps), 0, 0)

    operands = [first.reshape(1), features, gain, weight, *pieces, *after]
    in_specs = [
        pl.BlockSpec((seqs, residues, channels), place),
        whole((1, channels)),
        whole(weight.shape),
    ]
    in_specs += [whole(piece.shape) for piece in pieces] + [ANYWHERE] * len(after)
    aliases = {}
    if before is not None:
        aliases = {len(operands): 0}
        operands.append(before)
        in_specs.append(ANYWHERE)
    return pl.pallas_call(
        functools.partial(norm_grad_kernel, len(pieces)),
        grid_spec=pltpu.PrefetchScalarGridSpec(
            num_scalar_prefetch=1,
            grid=(len(pieces) * steps,),
            in_specs=in_specs,
            out_specs=[pl.BlockSpec((seqs, residues, channels), place), whole((8, 128))],
            scratch_shapes=[pltpu.VMEM((seqs, both_widths, residues), BF16)],
        ),
        out_shape=[
            jax.ShapeDtypeStruct(features.shape, BF16),
            jax.ShapeDtypeStruct((8, 128), F32),
        ],
        input_output_aliases=aliases,
        compiler_params=params(),
        cost_estimate=cost(
            flops=4 * len(pieces) * quarter * residues * channels * both_widths,
            bytes_accessed=4 * len(pieces) * quarter * residues * channels,
            transcendentals=0,
        ),
        name="norm_grad",
    )(*operands)


def share_kernel(scale, terms_ref, *refs):
    share_ref, spread_ref = refs[-2:]
    total = terms_ref[0].astype(F32)
    for n in range(1, terms_ref.shape[0]):
        total = total + terms_ref[n].astype(F32)
    total = total * scale
    share_ref[...] = total
    spread_ref[...] = jnp.broadcast_to(total.astype(BF16), spread_ref.shape)


def add_terms(terms, scale, after=()):
    return pl.pallas_call(
        functools.partial(share_kernel, scale),
        in_specs=[pl.BlockSpec(memory_space=pltpu.VMEM)] + [ANYWHERE] * len(after),
        out_specs=[pl.BlockSpec(memory_space=pltpu.VMEM)] * 2,
        out_shape=[
            jax.ShapeDtypeStruct(terms.shape[1:], F32),
            jax.ShapeDtypeStruct(terms.shape, BF16),
        ],
        compiler_params=pltpu.CompilerParams(vmem_limit_bytes=VMEM_LIMIT),
        name="add_terms",
    )(terms, *after)


def terms_kernel(weight_ref, projection_ref, bias_ref, *refs):
    out_ref, token_ref = refs[-2:]
    token_ref[...] = jnp.zeros_like(token_ref)
    devices, rows, lanes = out_ref.shape
    weight_rows = weight_ref.shape[0] // devices
    bias = jnp.sum(bias_ref[...], axis=0, keepdims=True)
    bias_high = bias.astype(BF16).astype(F32)
    tail = jnp.concatenate(
        [bias_high, bias - bias_high, jnp.zeros((rows - weight_rows - 3, lanes), F32)], axis=0
    )
    for n in range(devices):
        block = [
            weight_ref[n * weight_rows : (n + 1) * weight_rows, :],
            projection_ref[n : n + 1, :],
            tail,
        ]
        out_ref[n] = jnp.concatenate(block, axis=0).astype(BF16)


def gather_terms(devices, weight_part, projection_part, bias_part, after=()):
    lanes = weight_part.shape[1]
    return pl.pallas_call(
        terms_kernel,
        in_specs=[pl.BlockSpec(memory_space=pltpu.VMEM)] * 3 + [ANYWHERE] * len(after),
        out_specs=[pl.BlockSpec(memory_space=pltpu.VMEM)] * 2,
        out_shape=[
            jax.ShapeDtypeStruct((devices, 16, lanes), BF16),
            jax.ShapeDtypeStruct((8, lanes), F32),
        ],
        compiler_params=pltpu.CompilerParams(vmem_limit_bytes=VMEM_LIMIT),
        name="gather_terms",
    )(weight_part, projection_part.reshape(devices, lanes), bias_part, *after)


def torus_permute(value, move):
    pairs = []
    for z in range(RING):
        for y in range(RING):
            for x in range(RING):
                for s in range(2):
                    tx, ty, tz, ts = move(x, y, z, s)
                    tx, ty, tz = tx % RING, ty % RING, tz % RING
                    source = ((z * 2 + y // 2) * 8 + x * 2 + y % 2) * 2 + s
                    target = ((tz * 2 + ty // 2) * 8 + tx * 2 + ty % 2) * 2 + ts
                    pairs.append((source, target))
    return lax.ppermute(value, AXES, pairs)


def swap_cores(value):
    return torus_permute(value, lambda x, y, z, s: (x, y, z, 1 - s))


def swap_low_y(value):
    return torus_permute(value, lambda x, y, z, s: (x, y ^ 1, z, s))


def swap_both(value):
    return torus_permute(value, lambda x, y, z, s: (x, y ^ 1, z, 1 - s))


def shift_z(value, steps):
    return torus_permute(value, lambda x, y, z, s: (x, y, z + steps, s))


def shift_x(value, steps):
    return torus_permute(value, lambda x, y, z, s: (x + steps, y, z, s))


def transpose_xz(value):
    return torus_permute(value, lambda x, y, z, s: (z, SWAP_Y[y], x, s))


def body(
    alignment_features,
    norm_gain_vector,
    norm_offset_vector,
    projection_weight,
    output_weight,
    output_bias,
    pair_update_cotangent,
):
    half, residues, channels = alignment_features.shape
    width = projection_weight.shape[1] // 2
    pair_channels = output_weight.shape[1]
    rows, cols, _ = pair_update_cotangent.shape
    rows_total = residues * lax.axis_size("ia")
    quarter = half // RING
    inv_seqs = 1.0 / (half * 2)
    x = lax.axis_index("ja") // 2
    low_y = lax.axis_index("ja") % 2
    z = lax.axis_index("ia") // 2
    core = lax.axis_index("sa")
    features = pltpu.with_memory_space_constraint(alignment_features, pltpu.HBM)
    cotangent = pair_update_cotangent
    gain_row = norm_gain_vector.reshape(1, -1)
    offset_row = norm_offset_vector.reshape(1, -1)
    weight_rows = projection_weight.T

    right_piece = project(
        x,
        quarter,
        x * 0,
        residues,
        features,
        pltpu.with_memory_space_constraint(gain_row, pltpu.HBM),
        pltpu.with_memory_space_constraint(offset_row, pltpu.HBM),
        weight_rows[width:],
    )
    arrived = transpose_xz(right_piece.reshape(quarter, width * residues))

    def left_rows(part):
        return project(
            z,
            half,
            part,
            rows,
            alignment_features,
            gain_row,
            offset_row,
            weight_rows[:width],
            after=(right_piece,),
        )

    left_came = swap_cores(left_rows(1 - core)).transpose(2, 1, 0)
    left_kept = left_rows(core).transpose(2, 1, 0)
    own_left = jnp.concatenate([left_kept, left_came], axis=2).reshape(rows * width, 2 * half)

    arrived = add_up([arrived], after=(own_left,))
    right_pieces = [arrived] + [shift_z(arrived, -t) for t in range(1, RING)]
    right_cols = right_pieces + [swap_cores(piece) for piece in right_pieces]

    weight_dc = (
        output_weight.reshape(width, width, pair_channels)
        .transpose(1, 0, 2)
        .reshape(width * width, pair_channels)
    )
    blocks = rows // ROWS_AT_ONCE
    part = right_grad_part(
        0, blocks // 2, cotangent, weight_dc, own_left, None, after=(arrived,)
    )
    right_partial, _, bias_partial = right_grad_part(
        blocks // 2,
        blocks // 2,
        cotangent,
        weight_dc,
        own_left,
        part,
        after=tuple(right_pieces[1:]),
    )

    right_sum = add_up([right_partial[:half], swap_cores(right_partial[half:])])
    pieces = [right_sum[t * quarter : (t + 1) * quarter] for t in range(RING)]
    right_came = [shift_z(pieces[t], t) for t in range(1, RING)]
    left_partial = left_grad_part(
        lax.rem(z - x + RING, RING),
        right_cols,
        cotangent,
        weight_dc,
        after=(right_sum,),
    )

    left_came = [shift_x(left_partial[t], t) for t in range(1, RING)]
    right_sum = transpose_xz(add_up([pieces[0], *right_came], after=(left_partial,)))

    def pair_part(first, count, before, after):
        return pair_and_weight_grad(
            first,
            count,
            right_cols,
            own_left,
            weight_dc.T,
            output_bias,
            cotangent,
            before,
            after,
        )

    pair = pair_part(0, blocks // 2, None, (left_partial,))
    left_sum = add_up([left_partial[0], *left_came], after=(pair[1], right_sum))

    left_own, left_other = left_sum[:quarter], left_sum[quarter:]
    own_beside, right_beside = swap_low_y(left_own), swap_low_y(right_sum)
    other_here, other_beside = swap_cores(left_other), swap_both(left_other)
    pair = pair_part(blocks // 2, blocks // 4, pair, (left_sum,))
    left_own = add_up([left_own, own_beside], inv_seqs, after=(pair[1],))
    left_came = add_up([other_here, other_beside], inv_seqs, after=(pair[1],))
    right_grad = add_up([right_sum, right_beside], inv_seqs, after=(pair[1],))

    left_low = jnp.where(core == 0, left_own, left_came).reshape(quarter, rows, width)
    left_high = jnp.where(core == 0, left_came, left_own).reshape(quarter, rows, width)
    left_grad = jnp.concatenate(
        [left_low.transpose(0, 2, 1), left_high.transpose(0, 2, 1)], axis=2
    )
    grads = jnp.concatenate([left_grad, right_grad.reshape(quarter, width, residues)], axis=1)
    grad_pieces = [grads] + [shift_x(grads, -t) for t in range(1, RING)]

    pair_update_result, weight_partial = pair_part(blocks - blocks // 4, blocks // 4, pair, (grads,))
    projection_part = projection_grad_part(x, low_y, features, gain_row, offset_row, grads)
    devices = 128
    terms, token = gather_terms(
        devices, weight_partial, projection_part, bias_partial, after=tuple(grad_pieces[1:])
    )

    came = lax.all_to_all(terms, AXES, 0, 0, tiled=True)

    def norm_part(first, before, after):
        pieces = grad_pieces[first : first + 2]
        place = lax.rem(x + first, RING)
        return norm_grad(
            place, pieces, features, gain_row, weight_rows, before, after
        )

    alignment_gradient, token = norm_part(0, None, (token,))
    share, spread = add_terms(came, 1.0 / rows_total, after=(token,))
    bias_sum = share[9] + share[10]
    everything = lax.all_to_all(spread, AXES, 0, 0, tiled=True).astype(F32)
    alignment_gradient, _ = norm_part(2, alignment_gradient, (share,))
    weight_sum = (
        everything[:, :8]
        .reshape(width, width, pair_channels)
        .transpose(1, 0, 2)
        .reshape(width * width, pair_channels)
    )
    projection_sum = everything[:, 8].reshape(2 * width, channels).T

    return (
        pair_update_result,
        alignment_gradient,
        projection_sum,
        weight_sum,
        bias_sum,
    )


def solution(mesh):
    in_specs = (P("sa", "ia", None), P(), P(), P(), P(), P(), P(("ia", "sa"), "ja", None))
    out_specs = (P(("ia", "sa"), "ja", None), P("sa", "ia", None), P(), P(), P())
    return jax.shard_map(body, mesh=mesh, in_specs=in_specs, out_specs=out_specs, check_vma=False)
```

```python
import functools

import jax
import jax.numpy as jnp
from jax import lax
from jax.experimental import pallas as pl
from jax.experimental.pallas import tpu as pltpu
from jax.sharding import PartitionSpec as P

epsilon = 1e-05
AXES = ("ia", "ja", "sa")
RING = 4
SWAP_Y = (0, 2, 1, 3)
ROWS_AT_ONCE = 16
BF16 = jnp.bfloat16
F32 = jnp.float32
VMEM_LIMIT = 20 * 1024 * 1024


def dot(a, b, contract):
    return lax.dot_general(a, b, (contract, ((), ())), preferred_element_type=F32)


def params(limit=VMEM_LIMIT):
    return pltpu.CompilerParams(dimension_semantics=("arbitrary",), vmem_limit_bytes=limit)


ANYWHERE = pl.BlockSpec(memory_space=pl.ANY)


def cost(flops, bytes_accessed, transcendentals):
    return pl.CostEstimate(
        flops=flops, bytes_accessed=bytes_accessed, transcendentals=transcendentals
    )


def whole(shape):
    return pl.BlockSpec(shape, lambda *_: (0,) * len(shape))


def row_mean(values):
    channels = values.shape[-1]
    ones = jnp.full((channels, 128), 1.0 / channels, BF16)
    mean = dot(values.astype(BF16), ones, ((1,), (0,)))
    return jnp.concatenate([mean] * (channels // 128), axis=1)


def norm_block(features):
    centred = features.astype(F32) - row_mean(features)
    inverse_deviation = lax.rsqrt(row_mean(centred * centred) + epsilon)
    return centred * inverse_deviation, inverse_deviation


def norm_rows(features):
    values = features.astype(F32)
    scale = 1.0 / values.shape[-1]
    centred = values - jnp.sum(values, axis=-1, keepdims=True) * scale
    variance = jnp.sum(centred * centred, axis=-1, keepdims=True) * scale
    return centred * lax.rsqrt(variance + epsilon)


def project_kernel(place_ref, features_ref, gain_ref, offset_ref, weight_ref, *refs):
    out_ref = refs[-1]
    seqs, residues, channels = features_ref.shape
    at_once = 256 // residues
    for s in range(0, seqs, at_once):
        normed = [
            (norm_rows(features_ref[n, r : r + 64]) * gain_ref[...] + offset_ref[...]).astype(BF16)
            for n in range(s, s + at_once)
            for r in range(0, residues, 64)
        ]
        normed = jnp.concatenate(normed, axis=0)
        several = dot(weight_ref[...], normed, ((1,), (1,))).astype(BF16)
        for n in range(at_once):
            out_ref[s + n] = several[:, n * residues : (n + 1) * residues]


def project(first, count, part, residues, features, gain, offset, weight, after=()):
    total, _, channels = features.shape
    width = weight.shape[0]
    seqs = min(2048 // residues, 16)
    steps = total // seqs

    def place(n, place_ref):
        return (lax.rem(place_ref[0] + n, steps), place_ref[1], 0)

    return pl.pallas_call(
        project_kernel,
        grid_spec=pltpu.PrefetchScalarGridSpec(
            num_scalar_prefetch=1,
            grid=(count // seqs,),
            in_specs=[
                pl.BlockSpec((seqs, residues, channels), place),
                whole((1, channels)),
                whole((1, channels)),
                whole((width, channels)),
            ]
            + [ANYWHERE] * len(after),
            out_specs=pl.BlockSpec((seqs, width, residues), lambda n, place_ref: (n, 0, 0)),
        ),
        out_shape=jax.ShapeDtypeStruct((count, width, residues), BF16),
        compiler_params=params(),
        cost_estimate=cost(
            flops=4 * count * residues * channels * width,
            bytes_accessed=2 * count * residues * (channels + width),
            transcendentals=count * residues,
        ),
        name="project",
    )(jnp.stack([first, part]), features, gain, offset, weight, *after)


def outer_grad_block(cot_ref, weight_ref, grad_ref):
    rows, cols, pair_channels = cot_ref.shape
    width = grad_ref.shape[0]
    for i in range(0, rows, 2):
        cot = cot_ref[i : i + 2].reshape(2 * cols, pair_channels)
        grad = dot(weight_ref[...], cot, ((1,), (1,))).astype(BF16)
        grad = grad.reshape(width, width, 2 * cols)
        grad_ref[:, i * width : (i + 1) * width, :] = grad[:, :, :cols]
        grad_ref[:, (i + 1) * width : (i + 2) * width, :] = grad[:, :, cols:]


def right_grad_kernel(fresh, cot_ref, weight_ref, left_ref, total_in_ref, bias_in_ref, *refs):
    right_ref, total_ref, bias_ref, grad_ref = refs[-4:]
    step = pl.program_id(0)
    rows, cols, pair_channels = cot_ref.shape
    width = grad_ref.shape[0]

    @pl.when(step == 0)
    def _():
        if fresh:
            total_ref[...] = jnp.zeros_like(total_ref)
            bias_ref[...] = jnp.zeros_like(bias_ref)
        else:
            total_ref[...] = total_in_ref[...]
            bias_ref[...] = bias_in_ref[...]

    bias_ref[...] += jnp.sum(
        cot_ref[...].astype(F32).reshape(rows * cols // 8, 8, pair_channels), axis=0
    )
    outer_grad_block(cot_ref, weight_ref, grad_ref)
    left = left_ref[...].T
    for d in range(0, width, 2):
        both = jnp.concatenate([grad_ref[d], grad_ref[d + 1]], axis=1)
        total_ref[:, d * cols : (d + 2) * cols] += dot(left, both, ((1,), (0,)))

    if not fresh:

        @pl.when(step == pl.num_programs(0) - 1)
        def _():
            right_ref[...] = total_ref[...].astype(BF16)


def right_grad_part(first, count, cotangent, weight, left, before, after=()):
    rows, cols, pair_channels = cotangent.shape
    seqs = left.shape[1]
    width = left.shape[0] // rows
    block = ROWS_AT_ONCE * width
    fresh = before is None
    if fresh:
        before = (None, jnp.zeros((8, pair_channels), F32), jnp.zeros((8, pair_channels), F32))
    right_shape = (8, pair_channels) if fresh else (seqs, width * cols)
    return pl.pallas_call(
        functools.partial(right_grad_kernel, fresh),
        grid=(count,),
        in_specs=[
            pl.BlockSpec((ROWS_AT_ONCE, cols, pair_channels), lambda n: (first + n, 0, 0)),
            whole((width * width, pair_channels)),
            pl.BlockSpec((block, seqs), lambda n: (first + n, 0)),
            whole(before[1].shape),
            whole(before[2].shape),
        ]
        + [ANYWHERE] * len(after),
        out_specs=[
            whole(right_shape),
            whole((seqs, width * cols)),
            whole((8, pair_channels)),
        ],
        out_shape=[
            jax.ShapeDtypeStruct(right_shape, BF16),
            jax.ShapeDtypeStruct((seqs, width * cols), F32),
            jax.ShapeDtypeStruct((8, pair_channels), F32),
        ],
        scratch_shapes=[pltpu.VMEM((width, block, cols), BF16)],
        compiler_params=params(),
        cost_estimate=cost(
            flops=4 * count * ROWS_AT_ONCE * cols * width * width * pair_channels,
            bytes_accessed=2 * count * ROWS_AT_ONCE * cols * pair_channels,
            transcendentals=0,
        ),
        name="right_grad",
    )(cotangent, weight, left, before[1], before[2], *after)


def left_grad_kernel(turn_ref, *refs):
    piece_refs, (cot_ref, weight_ref, out_ref, cols_ref, grad_ref) = refs[: 2 * RING], refs[-5:]
    width, _, cols = grad_ref.shape
    quarter = piece_refs[0].shape[0]

    @pl.when(pl.program_id(0) == 0)
    def _():
        for d in range(width):
            here = slice(d * cols, (d + 1) * cols)
            part = jnp.concatenate([piece[:, here] for piece in piece_refs], axis=0)
            cols_ref[here, :] = part.T

    outer_grad_block(cot_ref, weight_ref, grad_ref)
    block = 8 * width
    for first_row in range(0, grad_ref.shape[1], block):
        here = slice(first_row, first_row + block)
        total = None
        for d in range(0, width, 2):
            both = jnp.concatenate([grad_ref[d, here], grad_ref[d + 1, here]], axis=1)
            term = dot(both, cols_ref[d * cols : (d + 2) * cols, :], ((1,), (0,)))
            total = term if total is None else total + term
        total = total.T.astype(BF16)
        for p in range(RING):
            place = lax.rem(turn_ref[0] + p, RING)
            for h in range(2):
                first = (h * RING + p) * quarter
                out_ref[place, h * quarter : (h + 1) * quarter, here] = total[
                    first : first + quarter
                ]


def left_grad_part(turn, pieces, cotangent, weight, after=()):
    rows, cols, pair_channels = cotangent.shape
    quarter = pieces[0].shape[0]
    width = pieces[0].shape[1] // cols
    blocks, block = rows // ROWS_AT_ONCE, ROWS_AT_ONCE * width
    seqs = 2 * RING * quarter
    return pl.pallas_call(
        left_grad_kernel,
        grid_spec=pltpu.PrefetchScalarGridSpec(
            num_scalar_prefetch=1,
            grid=(blocks,),
            in_specs=[whole(piece.shape) for piece in pieces]
            + [ANYWHERE] * len(after)
            + [
                pl.BlockSpec((ROWS_AT_ONCE, cols, pair_channels), lambda n, turn_ref: (n, 0, 0)),
                whole((width * width, pair_channels)),
            ],
            out_specs=pl.BlockSpec((RING, 2 * quarter, block), lambda n, turn_ref: (0, 0, n)),
            scratch_shapes=[
                pltpu.VMEM((width * cols, seqs), BF16),
                pltpu.VMEM((width, block, cols), BF16),
            ],
        ),
        out_shape=jax.ShapeDtypeStruct((RING, 2 * quarter, blocks * block), BF16),
        compiler_params=params(),
        cost_estimate=cost(
            flops=4 * blocks * width * block * cols * (seqs + pair_channels),
            bytes_accessed=4 * seqs * width * cols,
            transcendentals=0,
        ),
        name="left_grad",
    )(
        turn.reshape(1),
        *pieces,
        *after,
        cotangent,
        weight,
    )


def add_kernel(count, scale, *refs):
    total = refs[0][...].astype(F32)
    for ref in refs[1:count]:
        total = total + ref[...].astype(F32)
    refs[-1][...] = (total * scale).astype(BF16)


def add_up(parts, scale=1.0, after=()):
    return pl.pallas_call(
        lambda *refs: add_kernel(len(parts), scale, *refs),
        in_specs=[pl.BlockSpec(memory_space=pltpu.VMEM)] * len(parts) + [ANYWHERE] * len(after),
        out_specs=pl.BlockSpec(memory_space=pltpu.VMEM),
        out_shape=jax.ShapeDtypeStruct(parts[0].shape, BF16),
        compiler_params=pltpu.CompilerParams(vmem_limit_bytes=VMEM_LIMIT),
        name="add_up",
    )(*parts, *after)


def pair_kernel(fresh, *refs):
    piece_refs, refs = refs[: 2 * RING], refs[2 * RING :]
    left_ref, weight_ref, bias_ref, cot_ref, before_ref = refs[:5]
    pair_ref, total_ref, cols_ref, outer_ref = refs[-4:]
    rows, cols, pair_channels = cot_ref.shape
    width = outer_ref.shape[0]
    inv_seqs = 1.0 / cols_ref.shape[0]

    @pl.when(pl.program_id(0) == 0)
    def _():
        first = 0
        for piece in piece_refs:
            cols_ref[first : first + piece.shape[0], :] = piece[...]
            first += piece.shape[0]
        total_ref[...] = jnp.zeros_like(total_ref) if fresh else before_ref[...]

    for d in range(0, width, 2):
        both = dot(left_ref[...], cols_ref[:, d * cols : (d + 2) * cols], ((1,), (0,)))
        both = (both * inv_seqs).astype(BF16)
        outer_ref[d] = both[:, :cols]
        outer_ref[d + 1] = both[:, cols:]
    for i in range(0, rows, 2):
        outer = jnp.concatenate(
            [
                outer_ref[:, n * width : (n + 1) * width, :].reshape(width * width, cols)
                for n in (i, i + 1)
            ],
            axis=1,
        )
        cot = cot_ref[i : i + 2].reshape(2 * cols, pair_channels)
        total_ref[...] += dot(outer, cot, ((1,), (0,)))
        pair = dot(weight_ref[...], outer, ((1,), (0,))).T + bias_ref[...]
        pair_ref[i : i + 2] = pair.astype(BF16).reshape(2, cols, pair_channels)


def pair_and_weight_grad(first, count, pieces, left, weight, bias, cotangent, before, after=()):
    rows, cols, pair_channels = cotangent.shape
    seqs = left.shape[1]
    width = left.shape[0] // rows
    block = ROWS_AT_ONCE * width
    fresh = before is None
    if fresh:
        before = (None, jnp.zeros((8, pair_channels), F32))
    operands = [*pieces, left, weight, bias.reshape(1, -1), cotangent, before[1], *after]
    in_specs = [whole(piece.shape) for piece in pieces] + [
        pl.BlockSpec((block, seqs), lambda n: (first + n, 0)),
        whole((pair_channels, width * width)),
        whole((1, pair_channels)),
        pl.BlockSpec((ROWS_AT_ONCE, cols, pair_channels), lambda n: (first + n, 0, 0)),
        whole(before[1].shape),
    ]
    in_specs += [ANYWHERE] * len(after)
    aliases = {}
    if not fresh:
        aliases = {len(operands): 0}
        operands.append(before[0])
        in_specs.append(ANYWHERE)
    return pl.pallas_call(
        functools.partial(pair_kernel, fresh),
        grid=(count,),
        in_specs=in_specs,
        out_specs=[
            pl.BlockSpec((ROWS_AT_ONCE, cols, pair_channels), lambda n: (first + n, 0, 0)),
            whole((width * width, pair_channels)),
        ],
        out_shape=[
            jax.ShapeDtypeStruct((rows, cols, pair_channels), BF16),
            jax.ShapeDtypeStruct((width * width, pair_channels), F32),
        ],
        scratch_shapes=[
            pltpu.VMEM((seqs, width * cols), BF16),
            pltpu.VMEM((width, block, cols), BF16),
        ],
        input_output_aliases=aliases,
        compiler_params=params(),
        cost_estimate=cost(
            flops=4 * count * ROWS_AT_ONCE * cols * width * width * (2 * pair_channels + seqs),
            bytes_accessed=4 * count * ROWS_AT_ONCE * cols * pair_channels,
            transcendentals=0,
        ),
        name="pair_update",
    )(*operands)


def projection_grad_kernel(place_ref, features_ref, gain_ref, offset_ref, grads_ref, out_ref):
    seqs = features_ref.shape[0]
    total = None
    for s in range(seqs):
        rescaled = norm_rows(features_ref[s])
        normed = (rescaled * gain_ref[...] + offset_ref[...]).astype(BF16)
        term = dot(grads_ref[s], normed, ((1,), (0,)))
        total = term if total is None else total + term
    out_ref[...] = total


def projection_grad_part(x, low_y, features, gain, offset, grads):
    _, residues, channels = features.shape
    quarter, both_widths, _ = grads.shape
    eighth = quarter // 2
    place = jnp.stack([x * 2 + low_y, low_y])
    return pl.pallas_call(
        projection_grad_kernel,
        grid_spec=pltpu.PrefetchScalarGridSpec(
            num_scalar_prefetch=1,
            grid=(1,),
            in_specs=[
                pl.BlockSpec((eighth, residues, channels), lambda n, ref: (ref[0], 0, 0)),
                whole((1, channels)),
                whole((1, channels)),
                pl.BlockSpec((eighth, both_widths, residues), lambda n, ref: (ref[1], 0, 0)),
            ],
            out_specs=whole((both_widths, channels)),
        ),
        out_shape=jax.ShapeDtypeStruct((both_widths, channels), F32),
        compiler_params=params(),
        name="projection_grad",
    )(place, features, gain, offset, grads)


def norm_grad_kernel(count, first_ref, features_ref, gain_ref, weight_ref, *refs):
    piece_refs, (out_ref, token_ref, grads_ref) = refs[:count], refs[-3:]
    token_ref[...] = jnp.zeros_like(token_ref)
    step = pl.program_id(0)
    seqs, residues, channels = features_ref.shape
    steps = piece_refs[0].shape[0] // seqs
    for t in range(len(piece_refs)):

        @pl.when(step // steps == t)
        def _(t=t):
            grads_ref[...] = piece_refs[t][pl.ds(lax.rem(step, steps) * seqs, seqs)]

    at_once = 4
    for s in range(0, seqs, at_once):
        features = features_ref[s : s + at_once].reshape(at_once * residues, channels)
        rescaled, inverse_deviation = norm_block(features)
        grad = [dot(grads_ref[s + n], weight_ref[...], ((0,), (0,))) for n in range(at_once)]
        grad = jnp.concatenate(grad, axis=0) * gain_ref[...]
        grad = inverse_deviation * (grad - row_mean(grad) - rescaled * row_mean(grad * rescaled))
        out_ref[s : s + at_once] = grad.astype(BF16).reshape(at_once, residues, channels)


def norm_grad(first, pieces, features, gain, weight, before=None, after=()):
    _, residues, channels = features.shape
    quarter, both_widths, _ = pieces[0].shape
    seqs = quarter
    steps = 1

    def place(n, first_ref):
        return (lax.rem(n // steps + first_ref[0], RING) * steps + lax.rem(n, steps), 0, 0)

    operands = [first.reshape(1), features, gain, weight, *pieces, *after]
    in_specs = [
        pl.BlockSpec((seqs, residues, channels), place),
        whole((1, channels)),
        whole(weight.shape),
    ]
    in_specs += [whole(piece.shape) for piece in pieces] + [ANYWHERE] * len(after)
    aliases = {}
    if before is not None:
        aliases = {len(operands): 0}
        operands.append(before)
        in_specs.append(ANYWHERE)
    return pl.pallas_call(
        functools.partial(norm_grad_kernel, len(pieces)),
        grid_spec=pltpu.PrefetchScalarGridSpec(
            num_scalar_prefetch=1,
            grid=(len(pieces) * steps,),
            in_specs=in_specs,
            out_specs=[pl.BlockSpec((seqs, residues, channels), place), whole((8, 128))],
            scratch_shapes=[pltpu.VMEM((seqs, both_widths, residues), BF16)],
        ),
        out_shape=[
            jax.ShapeDtypeStruct(features.shape, BF16),
            jax.ShapeDtypeStruct((8, 128), F32),
        ],
        input_output_aliases=aliases,
        compiler_params=params(),
        cost_estimate=cost(
            flops=4 * len(pieces) * quarter * residues * channels * both_widths,
            bytes_accessed=4 * len(pieces) * quarter * residues * channels,
            transcendentals=0,
        ),
        name="norm_grad",
    )(*operands)


def share_kernel(scale, terms_ref, *refs):
    share_ref, spread_ref = refs[-2:]
    total = terms_ref[0].astype(F32)
    for n in range(1, terms_ref.shape[0]):
        total = total + terms_ref[n].astype(F32)
    total = total * scale
    share_ref[...] = total
    spread_ref[...] = jnp.broadcast_to(total.astype(BF16), spread_ref.shape)


def add_terms(terms, scale, after=()):
    return pl.pallas_call(
        functools.partial(share_kernel, scale),
        in_specs=[pl.BlockSpec(memory_space=pltpu.VMEM)] + [ANYWHERE] * len(after),
        out_specs=[pl.BlockSpec(memory_space=pltpu.VMEM)] * 2,
        out_shape=[
            jax.ShapeDtypeStruct(terms.shape[1:], F32),
            jax.ShapeDtypeStruct(terms.shape, BF16),
        ],
        compiler_params=pltpu.CompilerParams(vmem_limit_bytes=VMEM_LIMIT),
        name="add_terms",
    )(terms, *after)


def terms_kernel(weight_ref, projection_ref, bias_ref, *refs):
    out_ref, token_ref = refs[-2:]
    token_ref[...] = jnp.zeros_like(token_ref)
    devices, rows, lanes = out_ref.shape
    weight_rows = weight_ref.shape[0] // devices
    bias = jnp.sum(bias_ref[...], axis=0, keepdims=True)
    bias_high = bias.astype(BF16).astype(F32)
    tail = jnp.concatenate(
        [bias_high, bias - bias_high, jnp.zeros((rows - weight_rows - 3, lanes), F32)], axis=0
    )
    for n in range(devices):
        block = [
            weight_ref[n * weight_rows : (n + 1) * weight_rows, :],
            projection_ref[n : n + 1, :],
            tail,
        ]
        out_ref[n] = jnp.concatenate(block, axis=0).astype(BF16)


def gather_terms(devices, weight_part, projection_part, bias_part, after=()):
    lanes = weight_part.shape[1]
    return pl.pallas_call(
        terms_kernel,
        in_specs=[pl.BlockSpec(memory_space=pltpu.VMEM)] * 3 + [ANYWHERE] * len(after),
        out_specs=[pl.BlockSpec(memory_space=pltpu.VMEM)] * 2,
        out_shape=[
            jax.ShapeDtypeStruct((devices, 16, lanes), BF16),
            jax.ShapeDtypeStruct((8, lanes), F32),
        ],
        compiler_params=pltpu.CompilerParams(vmem_limit_bytes=VMEM_LIMIT),
        name="gather_terms",
    )(weight_part, projection_part.reshape(devices, lanes), bias_part, *after)


def torus_permute(value, move):
    pairs = []
    for z in range(RING):
        for y in range(RING):
            for x in range(RING):
                for s in range(2):
                    tx, ty, tz, ts = move(x, y, z, s)
                    tx, ty, tz = tx % RING, ty % RING, tz % RING
                    source = ((z * 2 + y // 2) * 8 + x * 2 + y % 2) * 2 + s
                    target = ((tz * 2 + ty // 2) * 8 + tx * 2 + ty % 2) * 2 + ts
                    pairs.append((source, target))
    return lax.ppermute(value, AXES, pairs)


def swap_cores(value):
    return torus_permute(value, lambda x, y, z, s: (x, y, z, 1 - s))


def swap_low_y(value):
    return torus_permute(value, lambda x, y, z, s: (x, y ^ 1, z, s))


def swap_both(value):
    return torus_permute(value, lambda x, y, z, s: (x, y ^ 1, z, 1 - s))


def shift_z(value, steps):
    return torus_permute(value, lambda x, y, z, s: (x, y, z + steps, s))


def shift_x(value, steps):
    return torus_permute(value, lambda x, y, z, s: (x + steps, y, z, s))


def transpose_xz(value):
    return torus_permute(value, lambda x, y, z, s: (z, SWAP_Y[y], x, s))


def body(
    alignment_features,
    norm_gain_vector,
    norm_offset_vector,
    projection_weight,
    output_weight,
    output_bias,
    pair_update_cotangent,
):
    half, residues, channels = alignment_features.shape
    width = projection_weight.shape[1] // 2
    pair_channels = output_weight.shape[1]
    rows, cols, _ = pair_update_cotangent.shape
    rows_total = residues * lax.axis_size("ia")
    quarter = half // RING
    inv_seqs = 1.0 / (half * 2)
    x = lax.axis_index("ja") // 2
    low_y = lax.axis_index("ja") % 2
    z = lax.axis_index("ia") // 2
    core = lax.axis_index("sa")
    features = pltpu.with_memory_space_constraint(alignment_features, pltpu.HBM)
    cotangent = pair_update_cotangent
    gain_row = norm_gain_vector.reshape(1, -1)
    offset_row = norm_offset_vector.reshape(1, -1)
    weight_rows = projection_weight.T

    right_piece = project(
        x,
        quarter,
        x * 0,
        residues,
        features,
        pltpu.with_memory_space_constraint(gain_row, pltpu.HBM),
        pltpu.with_memory_space_constraint(offset_row, pltpu.HBM),
        weight_rows[width:],
    )
    arrived = transpose_xz(right_piece.reshape(quarter, width * residues))

    def left_rows(part):
        return project(
            z,
            half,
            part,
            rows,
            alignment_features,
            gain_row,
            offset_row,
            weight_rows[:width],
            after=(right_piece,),
        )

    left_came = swap_cores(left_rows(1 - core)).transpose(2, 1, 0)
    left_kept = left_rows(core).transpose(2, 1, 0)
    own_left = jnp.concatenate([left_kept, left_came], axis=2).reshape(rows * width, 2 * half)

    arrived = add_up([arrived], after=(own_left,))
    right_pieces = [arrived] + [shift_z(arrived, -t) for t in range(1, RING)]
    right_cols = right_pieces + [swap_cores(piece) for piece in right_pieces]

    weight_dc = (
        output_weight.reshape(width, width, pair_channels)
        .transpose(1, 0, 2)
        .reshape(width * width, pair_channels)
    )
    blocks = rows // ROWS_AT_ONCE
    part = right_grad_part(
        0, blocks // 2, cotangent, weight_dc, own_left, None, after=(arrived,)
    )
    right_partial, _, bias_partial = right_grad_part(
        blocks // 2,
        blocks // 2,
        cotangent,
        weight_dc,
        own_left,
        part,
        after=tuple(right_pieces[1:]),
    )

    right_sum = add_up([right_partial[:half], swap_cores(right_partial[half:])])
    pieces = [right_sum[t * quarter : (t + 1) * quarter] for t in range(RING)]
    right_came = [shift_z(pieces[t], t) for t in range(1, RING)]
    left_partial = left_grad_part(
        lax.rem(z - x + RING, RING),
        right_cols,
        cotangent,
        weight_dc,
        after=(right_sum,),
    )

    left_came = [shift_x(left_partial[t], t) for t in range(1, RING)]
    right_sum = transpose_xz(add_up([pieces[0], *right_came], after=(left_partial,)))

    def pair_part(first, count, before, after):
        return pair_and_weight_grad(
            first,
            count,
            right_cols,
            own_left,
            weight_dc.T,
            output_bias,
            cotangent,
            before,
            after,
        )

    pair = pair_part(0, blocks // 2, None, (left_partial,))
    left_sum = add_up([left_partial[0], *left_came], after=(pair[1], right_sum))

    left_own, left_other = left_sum[:quarter], left_sum[quarter:]
    own_beside, right_beside = swap_low_y(left_own), swap_low_y(right_sum)
    other_here, other_beside = swap_cores(left_other), swap_both(left_other)
    pair = pair_part(blocks // 2, blocks // 4, pair, (left_sum,))
    left_own = add_up([left_own, own_beside], inv_seqs, after=(pair[1],))
    left_came = add_up([other_here, other_beside], inv_seqs, after=(pair[1],))
    right_grad = add_up([right_sum, right_beside], inv_seqs, after=(pair[1],))

    left_low = jnp.where(core == 0, left_own, left_came).reshape(quarter, rows, width)
    left_high = jnp.where(core == 0, left_came, left_own).reshape(quarter, rows, width)
    left_grad = jnp.concatenate(
        [left_low.transpose(0, 2, 1), left_high.transpose(0, 2, 1)], axis=2
    )
    grads = jnp.concatenate([left_grad, right_grad.reshape(quarter, width, residues)], axis=1)
    grad_pieces = [grads] + [shift_x(grads, -t) for t in range(1, RING)]

    pair_update_result, weight_partial = pair_part(blocks - blocks // 4, blocks // 4, pair, (grads,))
    projection_part = projection_grad_part(x, low_y, features, gain_row, offset_row, grads)
    devices = 128
    terms, token = gather_terms(
        devices, weight_partial, projection_part, bias_partial, after=tuple(grad_pieces[1:])
    )

    came = lax.all_to_all(terms, AXES, 0, 0, tiled=True)

    def norm_part(first, before, after):
        pieces = grad_pieces[first : first + 2]
        place = lax.rem(x + first, RING)
        return norm_grad(
            place, pieces, features, gain_row, weight_rows, before, after
        )

    alignment_gradient, token = norm_part(0, None, (token,))
    share, spread = add_terms(came, 1.0 / rows_total, after=(token,))
    bias_sum = share[9] + share[10]
    everything = lax.all_to_all(spread, AXES, 0, 0, tiled=True).astype(F32)
    alignment_gradient, _ = norm_part(2, alignment_gradient, (share,))
    weight_sum = (
        everything[:, :8]
        .reshape(width, width, pair_channels)
        .transpose(1, 0, 2)
        .reshape(width * width, pair_channels)
    )
    projection_sum = everything[:, 8].reshape(2 * width, channels).T

    return (
        pair_update_result,
        alignment_gradient,
        projection_sum,
        weight_sum,
        bias_sum,
    )


def solution(mesh):
    in_specs = (P("sa", "ia", None), P(), P(), P(), P(), P(), P(("ia", "sa"), "ja", None))
    out_specs = (P(("ia", "sa"), "ja", None), P("sa", "ia", None), P(), P(), P())
    return jax.shard_map(body, mesh=mesh, in_specs=in_specs, out_specs=out_specs, check_vma=False)
```

```python
import functools

import jax
import jax.numpy as jnp
from jax import lax
from jax.experimental import pallas as pl
from jax.experimental.pallas import tpu as pltpu
from jax.sharding import PartitionSpec as P

epsilon = 1e-05
AXES = ("ia", "ja", "sa")
RING = 4
SWAP_Y = (0, 2, 1, 3)
ROWS_AT_ONCE = 16
BF16 = jnp.bfloat16
F32 = jnp.float32
VMEM_LIMIT = 20 * 1024 * 1024


def dot(a, b, contract):
    return lax.dot_general(a, b, (contract, ((), ())), preferred_element_type=F32)


def params(limit=VMEM_LIMIT):
    return pltpu.CompilerParams(dimension_semantics=("arbitrary",), vmem_limit_bytes=limit)


ANYWHERE = pl.BlockSpec(memory_space=pl.ANY)


def cost(flops, bytes_accessed, transcendentals):
    return pl.CostEstimate(
        flops=flops, bytes_accessed=bytes_accessed, transcendentals=transcendentals
    )


def whole(shape):
    return pl.BlockSpec(shape, lambda *_: (0,) * len(shape))


def row_mean(values):
    channels = values.shape[-1]
    ones = jnp.full((channels, 128), 1.0 / channels, BF16)
    mean = dot(values.astype(BF16), ones, ((1,), (0,)))
    return jnp.concatenate([mean] * (channels // 128), axis=1)


def norm_block(features):
    centred = features.astype(F32) - row_mean(features)
    inverse_deviation = lax.rsqrt(row_mean(centred * centred) + epsilon)
    return centred * inverse_deviation, inverse_deviation


def norm_rows(features):
    values = features.astype(F32)
    scale = 1.0 / values.shape[-1]
    centred = values - jnp.sum(values, axis=-1, keepdims=True) * scale
    variance = jnp.sum(centred * centred, axis=-1, keepdims=True) * scale
    return centred * lax.rsqrt(variance + epsilon)


def project_kernel(place_ref, features_ref, gain_ref, offset_ref, weight_ref, *refs):
    out_ref = refs[-1]
    seqs, residues, channels = features_ref.shape
    at_once = 256 // residues
    for s in range(0, seqs, at_once):
        normed = [
            (norm_rows(features_ref[n, r : r + 64]) * gain_ref[...] + offset_ref[...]).astype(BF16)
            for n in range(s, s + at_once)
            for r in range(0, residues, 64)
        ]
        normed = jnp.concatenate(normed, axis=0)
        several = dot(normed, weight_ref[...], ((1,), (0,))).T.astype(BF16)
        for n in range(at_once):
            out_ref[s + n] = several[:, n * residues : (n + 1) * residues]


def project(first, count, part, residues, features, gain, offset, weight, after=()):
    total, _, channels = features.shape
    width = weight.shape[1]
    seqs = min(2048 // residues, 16)
    steps = total // seqs

    def place(n, place_ref):
        return (lax.rem(place_ref[0] + n, steps), place_ref[1], 0)

    return pl.pallas_call(
        project_kernel,
        grid_spec=pltpu.PrefetchScalarGridSpec(
            num_scalar_prefetch=1,
            grid=(count // seqs,),
            in_specs=[
                pl.BlockSpec((seqs, residues, channels), place),
                whole((1, channels)),
                whole((1, channels)),
                whole((channels, width)),
            ]
            + [ANYWHERE] * len(after),
            out_specs=pl.BlockSpec((seqs, width, residues), lambda n, place_ref: (n, 0, 0)),
        ),
        out_shape=jax.ShapeDtypeStruct((count, width, residues), BF16),
        compiler_params=params(),
        cost_estimate=cost(
            flops=4 * count * residues * channels * width,
            bytes_accessed=2 * count * residues * (channels + width),
            transcendentals=count * residues,
        ),
        name="project",
    )(jnp.stack([first, part]), features, gain, offset, weight, *after)


def outer_grad_block(cot_ref, weight_ref, grad_ref):
    rows, cols, pair_channels = cot_ref.shape
    width = grad_ref.shape[0]
    for i in range(0, rows, 2):
        cot = cot_ref[i : i + 2].reshape(2 * cols, pair_channels)
        grad = dot(weight_ref[...], cot, ((1,), (1,))).astype(BF16)
        grad = grad.reshape(width, width, 2 * cols)
        grad_ref[:, i * width : (i + 1) * width, :] = grad[:, :, :cols]
        grad_ref[:, (i + 1) * width : (i + 2) * width, :] = grad[:, :, cols:]


def right_grad_kernel(fresh, cot_ref, weight_ref, left_ref, total_in_ref, bias_in_ref, *refs):
    right_ref, total_ref, bias_ref, grad_ref = refs[-4:]
    step = pl.program_id(0)
    rows, cols, pair_channels = cot_ref.shape
    width = grad_ref.shape[0]

    @pl.when(step == 0)
    def _():
        if fresh:
            total_ref[...] = jnp.zeros_like(total_ref)
            bias_ref[...] = jnp.zeros_like(bias_ref)
        else:
            total_ref[...] = total_in_ref[...]
            bias_ref[...] = bias_in_ref[...]

    bias_ref[...] += jnp.sum(
        cot_ref[...].astype(F32).reshape(rows * cols // 8, 8, pair_channels), axis=0
    )
    outer_grad_block(cot_ref, weight_ref, grad_ref)
    left = left_ref[...].T
    for d in range(0, width, 2):
        both = jnp.concatenate([grad_ref[d], grad_ref[d + 1]], axis=1)
        total_ref[:, d * cols : (d + 2) * cols] += dot(left, both, ((1,), (0,)))

    if not fresh:

        @pl.when(step == pl.num_programs(0) - 1)
        def _():
            right_ref[...] = total_ref[...].astype(BF16)


def right_grad_part(first, count, cotangent, weight, left, before, after=()):
    rows, cols, pair_channels = cotangent.shape
    seqs = left.shape[1]
    width = left.shape[0] // rows
    block = ROWS_AT_ONCE * width
    fresh = before is None
    if fresh:
        before = (None, jnp.zeros((8, pair_channels), F32), jnp.zeros((8, pair_channels), F32))
    right_shape = (8, pair_channels) if fresh else (seqs, width * cols)
    return pl.pallas_call(
        functools.partial(right_grad_kernel, fresh),
        grid=(count,),
        in_specs=[
            pl.BlockSpec((ROWS_AT_ONCE, cols, pair_channels), lambda n: (first + n, 0, 0)),
            whole((width * width, pair_channels)),
            pl.BlockSpec((block, seqs), lambda n: (first + n, 0)),
            whole(before[1].shape),
            whole(before[2].shape),
        ]
        + [ANYWHERE] * len(after),
        out_specs=[
            whole(right_shape),
            whole((seqs, width * cols)),
            whole((8, pair_channels)),
        ],
        out_shape=[
            jax.ShapeDtypeStruct(right_shape, BF16),
            jax.ShapeDtypeStruct((seqs, width * cols), F32),
            jax.ShapeDtypeStruct((8, pair_channels), F32),
        ],
        scratch_shapes=[pltpu.VMEM((width, block, cols), BF16)],
        compiler_params=params(),
        cost_estimate=cost(
            flops=4 * count * ROWS_AT_ONCE * cols * width * width * pair_channels,
            bytes_accessed=2 * count * ROWS_AT_ONCE * cols * pair_channels,
            transcendentals=0,
        ),
        name="right_grad",
    )(cotangent, weight, left, before[1], before[2], *after)


def left_grad_kernel(turn_ref, *refs):
    piece_refs, (cot_ref, weight_ref, out_ref, cols_ref, grad_ref) = refs[: 2 * RING], refs[-5:]
    width, _, cols = grad_ref.shape
    quarter = piece_refs[0].shape[0]

    @pl.when(pl.program_id(0) == 0)
    def _():
        for d in range(width):
            here = slice(d * cols, (d + 1) * cols)
            part = jnp.concatenate([piece[:, here] for piece in piece_refs], axis=0)
            cols_ref[here, :] = part.T

    outer_grad_block(cot_ref, weight_ref, grad_ref)
    block = 8 * width
    for first_row in range(0, grad_ref.shape[1], block):
        here = slice(first_row, first_row + block)
        total = None
        for d in range(0, width, 2):
            both = jnp.concatenate([grad_ref[d, here], grad_ref[d + 1, here]], axis=1)
            term = dot(both, cols_ref[d * cols : (d + 2) * cols, :], ((1,), (0,)))
            total = term if total is None else total + term
        total = total.T.astype(BF16)
        for p in range(RING):
            place = lax.rem(turn_ref[0] + p, RING)
            for h in range(2):
                first = (h * RING + p) * quarter
                out_ref[place, h * quarter : (h + 1) * quarter, here] = total[
                    first : first + quarter
                ]


def left_grad_part(turn, pieces, cotangent, weight, after=()):
    rows, cols, pair_channels = cotangent.shape
    quarter = pieces[0].shape[0]
    width = pieces[0].shape[1] // cols
    blocks, block = rows // ROWS_AT_ONCE, ROWS_AT_ONCE * width
    seqs = 2 * RING * quarter
    return pl.pallas_call(
        left_grad_kernel,
        grid_spec=pltpu.PrefetchScalarGridSpec(
            num_scalar_prefetch=1,
            grid=(blocks,),
            in_specs=[whole(piece.shape) for piece in pieces]
            + [ANYWHERE] * len(after)
            + [
                pl.BlockSpec((ROWS_AT_ONCE, cols, pair_channels), lambda n, turn_ref: (n, 0, 0)),
                whole((width * width, pair_channels)),
            ],
            out_specs=pl.BlockSpec((RING, 2 * quarter, block), lambda n, turn_ref: (0, 0, n)),
            scratch_shapes=[
                pltpu.VMEM((width * cols, seqs), BF16),
                pltpu.VMEM((width, block, cols), BF16),
            ],
        ),
        out_shape=jax.ShapeDtypeStruct((RING, 2 * quarter, blocks * block), BF16),
        compiler_params=params(),
        cost_estimate=cost(
            flops=4 * blocks * width * block * cols * (seqs + pair_channels),
            bytes_accessed=4 * seqs * width * cols,
            transcendentals=0,
        ),
        name="left_grad",
    )(
        turn.reshape(1),
        *pieces,
        *after,
        cotangent,
        weight,
    )


def add_kernel(count, scale, *refs):
    total = refs[0][...].astype(F32)
    for ref in refs[1:count]:
        total = total + ref[...].astype(F32)
    refs[-1][...] = (total * scale).astype(BF16)


def add_up(parts, scale=1.0, after=()):
    return pl.pallas_call(
        lambda *refs: add_kernel(len(parts), scale, *refs),
        in_specs=[pl.BlockSpec(memory_space=pltpu.VMEM)] * len(parts) + [ANYWHERE] * len(after),
        out_specs=pl.BlockSpec(memory_space=pltpu.VMEM),
        out_shape=jax.ShapeDtypeStruct(parts[0].shape, BF16),
        compiler_params=pltpu.CompilerParams(vmem_limit_bytes=VMEM_LIMIT),
        name="add_up",
    )(*parts, *after)


def pair_kernel(fresh, *refs):
    piece_refs, refs = refs[: 2 * RING], refs[2 * RING :]
    left_ref, weight_ref, bias_ref, cot_ref, before_ref = refs[:5]
    pair_ref, total_ref, cols_ref, outer_ref = refs[-4:]
    rows, cols, pair_channels = cot_ref.shape
    width = outer_ref.shape[0]
    inv_seqs = 1.0 / cols_ref.shape[0]

    @pl.when(pl.program_id(0) == 0)
    def _():
        first = 0
        for piece in piece_refs:
            cols_ref[first : first + piece.shape[0], :] = piece[...]
            first += piece.shape[0]
        total_ref[...] = jnp.zeros_like(total_ref) if fresh else before_ref[...]

    for d in range(0, width, 2):
        both = dot(left_ref[...], cols_ref[:, d * cols : (d + 2) * cols], ((1,), (0,)))
        both = (both * inv_seqs).astype(BF16)
        outer_ref[d] = both[:, :cols]
        outer_ref[d + 1] = both[:, cols:]
    for i in range(0, rows, 2):
        outer = jnp.concatenate(
            [
                outer_ref[:, n * width : (n + 1) * width, :].reshape(width * width, cols)
                for n in (i, i + 1)
            ],
            axis=1,
        )
        cot = cot_ref[i : i + 2].reshape(2 * cols, pair_channels)
        total_ref[...] += dot(outer, cot, ((1,), (0,)))
        pair = dot(weight_ref[...], outer, ((1,), (0,))).T + bias_ref[...]
        pair_ref[i : i + 2] = pair.astype(BF16).reshape(2, cols, pair_channels)


def pair_and_weight_grad(first, count, pieces, left, weight, bias, cotangent, before, after=()):
    rows, cols, pair_channels = cotangent.shape
    seqs = left.shape[1]
    width = left.shape[0] // rows
    block = ROWS_AT_ONCE * width
    fresh = before is None
    if fresh:
        before = (None, jnp.zeros((8, pair_channels), F32))
    operands = [*pieces, left, weight, bias.reshape(1, -1), cotangent, before[1], *after]
    in_specs = [whole(piece.shape) for piece in pieces] + [
        pl.BlockSpec((block, seqs), lambda n: (first + n, 0)),
        whole((pair_channels, width * width)),
        whole((1, pair_channels)),
        pl.BlockSpec((ROWS_AT_ONCE, cols, pair_channels), lambda n: (first + n, 0, 0)),
        whole(before[1].shape),
    ]
    in_specs += [ANYWHERE] * len(after)
    aliases = {}
    if not fresh:
        aliases = {len(operands): 0}
        operands.append(before[0])
        in_specs.append(ANYWHERE)
    return pl.pallas_call(
        functools.partial(pair_kernel, fresh),
        grid=(count,),
        in_specs=in_specs,
        out_specs=[
            pl.BlockSpec((ROWS_AT_ONCE, cols, pair_channels), lambda n: (first + n, 0, 0)),
            whole((width * width, pair_channels)),
        ],
        out_shape=[
            jax.ShapeDtypeStruct((rows, cols, pair_channels), BF16),
            jax.ShapeDtypeStruct((width * width, pair_channels), F32),
        ],
        scratch_shapes=[
            pltpu.VMEM((seqs, width * cols), BF16),
            pltpu.VMEM((width, block, cols), BF16),
        ],
        input_output_aliases=aliases,
        compiler_params=params(),
        cost_estimate=cost(
            flops=4 * count * ROWS_AT_ONCE * cols * width * width * (2 * pair_channels + seqs),
            bytes_accessed=4 * count * ROWS_AT_ONCE * cols * pair_channels,
            transcendentals=0,
        ),
        name="pair_update",
    )(*operands)


def projection_grad_kernel(place_ref, features_ref, gain_ref, offset_ref, grads_ref, out_ref):
    seqs = features_ref.shape[0]
    total = None
    for s in range(seqs):
        rescaled = norm_rows(features_ref[s])
        normed = (rescaled * gain_ref[...] + offset_ref[...]).astype(BF16)
        term = dot(grads_ref[s], normed, ((1,), (0,)))
        total = term if total is None else total + term
    out_ref[...] = total


def projection_grad_part(x, low_y, features, gain, offset, grads):
    _, residues, channels = features.shape
    quarter, both_widths, _ = grads.shape
    eighth = quarter // 2
    place = jnp.stack([x * 2 + low_y, low_y])
    return pl.pallas_call(
        projection_grad_kernel,
        grid_spec=pltpu.PrefetchScalarGridSpec(
            num_scalar_prefetch=1,
            grid=(1,),
            in_specs=[
                pl.BlockSpec((eighth, residues, channels), lambda n, ref: (ref[0], 0, 0)),
                whole((1, channels)),
                whole((1, channels)),
                pl.BlockSpec((eighth, both_widths, residues), lambda n, ref: (ref[1], 0, 0)),
            ],
            out_specs=whole((both_widths, channels)),
        ),
        out_shape=jax.ShapeDtypeStruct((both_widths, channels), F32),
        compiler_params=params(),
        name="projection_grad",
    )(place, features, gain, offset, grads)


def norm_grad_kernel(count, first_ref, features_ref, gain_ref, weight_ref, *refs):
    piece_refs, (out_ref, token_ref, grads_ref) = refs[:count], refs[-3:]
    token_ref[...] = jnp.zeros_like(token_ref)
    step = pl.program_id(0)
    seqs, residues, channels = features_ref.shape
    steps = piece_refs[0].shape[0] // seqs
    for t in range(len(piece_refs)):

        @pl.when(step // steps == t)
        def _(t=t):
            grads_ref[...] = piece_refs[t][pl.ds(lax.rem(step, steps) * seqs, seqs)]

    at_once = 4
    for s in range(0, seqs, at_once):
        features = features_ref[s : s + at_once].reshape(at_once * residues, channels)
        rescaled, inverse_deviation = norm_block(features)
        grad = [dot(grads_ref[s + n], weight_ref[...], ((0,), (0,))) for n in range(at_once)]
        grad = jnp.concatenate(grad, axis=0) * gain_ref[...]
        grad = inverse_deviation * (grad - row_mean(grad) - rescaled * row_mean(grad * rescaled))
        out_ref[s : s + at_once] = grad.astype(BF16).reshape(at_once, residues, channels)


def norm_grad(first, pieces, features, gain, weight, before=None, after=()):
    _, residues, channels = features.shape
    quarter, both_widths, _ = pieces[0].shape
    seqs = quarter
    steps = 1

    def place(n, first_ref):
        return (lax.rem(n // steps + first_ref[0], RING) * steps + lax.rem(n, steps), 0, 0)

    operands = [first.reshape(1), features, gain, weight, *pieces, *after]
    in_specs = [
        pl.BlockSpec((seqs, residues, channels), place),
        whole((1, channels)),
        whole(weight.shape),
    ]
    in_specs += [whole(piece.shape) for piece in pieces] + [ANYWHERE] * len(after)
    aliases = {}
    if before is not None:
        aliases = {len(operands): 0}
        operands.append(before)
        in_specs.append(ANYWHERE)
    return pl.pallas_call(
        functools.partial(norm_grad_kernel, len(pieces)),
        grid_spec=pltpu.PrefetchScalarGridSpec(
            num_scalar_prefetch=1,
            grid=(len(pieces) * steps,),
            in_specs=in_specs,
            out_specs=[pl.BlockSpec((seqs, residues, channels), place), whole((8, 128))],
            scratch_shapes=[pltpu.VMEM((seqs, both_widths, residues), BF16)],
        ),
        out_shape=[
            jax.ShapeDtypeStruct(features.shape, BF16),
            jax.ShapeDtypeStruct((8, 128), F32),
        ],
        input_output_aliases=aliases,
        compiler_params=params(),
        cost_estimate=cost(
            flops=4 * len(pieces) * quarter * residues * channels * both_widths,
            bytes_accessed=4 * len(pieces) * quarter * residues * channels,
            transcendentals=0,
        ),
        name="norm_grad",
    )(*operands)


def share_kernel(scale, terms_ref, *refs):
    share_ref, spread_ref = refs[-2:]
    total = terms_ref[0].astype(F32)
    for n in range(1, terms_ref.shape[0]):
        total = total + terms_ref[n].astype(F32)
    total = total * scale
    share_ref[...] = total
    spread_ref[...] = jnp.broadcast_to(total.astype(BF16), spread_ref.shape)


def add_terms(terms, scale, after=()):
    return pl.pallas_call(
        functools.partial(share_kernel, scale),
        in_specs=[pl.BlockSpec(memory_space=pltpu.VMEM)] + [ANYWHERE] * len(after),
        out_specs=[pl.BlockSpec(memory_space=pltpu.VMEM)] * 2,
        out_shape=[
            jax.ShapeDtypeStruct(terms.shape[1:], F32),
            jax.ShapeDtypeStruct(terms.shape, BF16),
        ],
        compiler_params=pltpu.CompilerParams(vmem_limit_bytes=VMEM_LIMIT),
        name="add_terms",
    )(terms, *after)


def terms_kernel(weight_ref, projection_ref, bias_ref, *refs):
    out_ref, token_ref = refs[-2:]
    token_ref[...] = jnp.zeros_like(token_ref)
    devices, rows, lanes = out_ref.shape
    weight_rows = weight_ref.shape[0] // devices
    bias = jnp.sum(bias_ref[...], axis=0, keepdims=True)
    bias_high = bias.astype(BF16).astype(F32)
    tail = jnp.concatenate(
        [bias_high, bias - bias_high, jnp.zeros((rows - weight_rows - 3, lanes), F32)], axis=0
    )
    for n in range(devices):
        block = [
            weight_ref[n * weight_rows : (n + 1) * weight_rows, :],
            projection_ref[n : n + 1, :],
            tail,
        ]
        out_ref[n] = jnp.concatenate(block, axis=0).astype(BF16)


def gather_terms(devices, weight_part, projection_part, bias_part, after=()):
    lanes = weight_part.shape[1]
    return pl.pallas_call(
        terms_kernel,
        in_specs=[pl.BlockSpec(memory_space=pltpu.VMEM)] * 3 + [ANYWHERE] * len(after),
        out_specs=[pl.BlockSpec(memory_space=pltpu.VMEM)] * 2,
        out_shape=[
            jax.ShapeDtypeStruct((devices, 16, lanes), BF16),
            jax.ShapeDtypeStruct((8, lanes), F32),
        ],
        compiler_params=pltpu.CompilerParams(vmem_limit_bytes=VMEM_LIMIT),
        name="gather_terms",
    )(weight_part, projection_part.reshape(devices, lanes), bias_part, *after)


def torus_permute(value, move):
    pairs = []
    for z in range(RING):
        for y in range(RING):
            for x in range(RING):
                for s in range(2):
                    tx, ty, tz, ts = move(x, y, z, s)
                    tx, ty, tz = tx % RING, ty % RING, tz % RING
                    source = ((z * 2 + y // 2) * 8 + x * 2 + y % 2) * 2 + s
                    target = ((tz * 2 + ty // 2) * 8 + tx * 2 + ty % 2) * 2 + ts
                    pairs.append((source, target))
    return lax.ppermute(value, AXES, pairs)


def swap_cores(value):
    return torus_permute(value, lambda x, y, z, s: (x, y, z, 1 - s))


def swap_low_y(value):
    return torus_permute(value, lambda x, y, z, s: (x, y ^ 1, z, s))


def swap_both(value):
    return torus_permute(value, lambda x, y, z, s: (x, y ^ 1, z, 1 - s))


def shift_z(value, steps):
    return torus_permute(value, lambda x, y, z, s: (x, y, z + steps, s))


def shift_x(value, steps):
    return torus_permute(value, lambda x, y, z, s: (x + steps, y, z, s))


def transpose_xz(value):
    return torus_permute(value, lambda x, y, z, s: (z, SWAP_Y[y], x, s))


def body(
    alignment_features,
    norm_gain_vector,
    norm_offset_vector,
    projection_weight,
    output_weight,
    output_bias,
    pair_update_cotangent,
):
    half, residues, channels = alignment_features.shape
    width = projection_weight.shape[1] // 2
    pair_channels = output_weight.shape[1]
    rows, cols, _ = pair_update_cotangent.shape
    rows_total = residues * lax.axis_size("ia")
    quarter = half // RING
    inv_seqs = 1.0 / (half * 2)
    x = lax.axis_index("ja") // 2
    low_y = lax.axis_index("ja") % 2
    z = lax.axis_index("ia") // 2
    core = lax.axis_index("sa")
    features = pltpu.with_memory_space_constraint(alignment_features, pltpu.HBM)
    cotangent = pair_update_cotangent
    gain_row = norm_gain_vector.reshape(1, -1)
    offset_row = norm_offset_vector.reshape(1, -1)
    weight_rows = projection_weight.T

    right_piece = project(
        x,
        quarter,
        x * 0,
        residues,
        features,
        pltpu.with_memory_space_constraint(gain_row, pltpu.HBM),
        pltpu.with_memory_space_constraint(offset_row, pltpu.HBM),
        projection_weight[:, width:],
    )
    arrived = transpose_xz(right_piece.reshape(quarter, width * residues))

    def left_rows(part):
        return project(
            z,
            half,
            part,
            rows,
            alignment_features,
            gain_row,
            offset_row,
            projection_weight[:, :width],
            after=(right_piece,),
        )

    left_came = swap_cores(left_rows(1 - core)).transpose(2, 1, 0)
    left_kept = left_rows(core).transpose(2, 1, 0)
    own_left = jnp.concatenate([left_kept, left_came], axis=2).reshape(rows * width, 2 * half)

    arrived = add_up([arrived], after=(own_left,))
    right_pieces = [arrived] + [shift_z(arrived, -t) for t in range(1, RING)]
    right_cols = right_pieces + [swap_cores(piece) for piece in right_pieces]

    weight_dc = (
        output_weight.reshape(width, width, pair_channels)
        .transpose(1, 0, 2)
        .reshape(width * width, pair_channels)
    )
    blocks = rows // ROWS_AT_ONCE
    part = right_grad_part(
        0, blocks // 2, cotangent, weight_dc, own_left, None, after=(arrived,)
    )
    right_partial, _, bias_partial = right_grad_part(
        blocks // 2,
        blocks // 2,
        cotangent,
        weight_dc,
        own_left,
        part,
        after=tuple(right_pieces[1:]),
    )

    right_sum = add_up([right_partial[:half], swap_cores(right_partial[half:])])
    pieces = [right_sum[t * quarter : (t + 1) * quarter] for t in range(RING)]
    right_came = [shift_z(pieces[t], t) for t in range(1, RING)]
    left_partial = left_grad_part(
        lax.rem(z - x + RING, RING),
        right_cols,
        cotangent,
        weight_dc,
        after=(right_sum,),
    )

    left_came = [shift_x(left_partial[t], t) for t in range(1, RING)]
    right_sum = transpose_xz(add_up([pieces[0], *right_came], after=(left_partial,)))

    def pair_part(first, count, before, after, cotangent=cotangent):
        return pair_and_weight_grad(
            first,
            count,
            right_cols,
            own_left,
            weight_dc.T,
            output_bias,
            cotangent,
            before,
            after,
        )

    pair = pair_part(0, blocks // 2, None, (left_partial,))
    left_sum = add_up([left_partial[0], *left_came], after=(pair[1], right_sum))

    left_own, left_other = left_sum[:quarter], left_sum[quarter:]
    own_beside, right_beside = swap_low_y(left_own), swap_low_y(right_sum)
    other_here, other_beside = swap_cores(left_other), swap_both(left_other)
    pair = pair_part(blocks // 2, blocks // 4, pair, (left_sum,))
    left_own = add_up([left_own, own_beside], inv_seqs, after=(pair[1],))
    left_came = add_up([other_here, other_beside], inv_seqs, after=(pair[1],))
    right_grad = add_up([right_sum, right_beside], inv_seqs, after=(pair[1],))

    left_low = jnp.where(core == 0, left_own, left_came).reshape(quarter, rows, width)
    left_high = jnp.where(core == 0, left_came, left_own).reshape(quarter, rows, width)
    left_grad = jnp.concatenate(
        [left_low.transpose(0, 2, 1), left_high.transpose(0, 2, 1)], axis=2
    )
    grads = jnp.concatenate([left_grad, right_grad.reshape(quarter, width, residues)], axis=1)
    grad_pieces = [grads] + [shift_x(grads, -t) for t in range(1, RING)]

    pair_update_result, weight_partial = pair_part(
        blocks - blocks // 4,
        blocks // 4,
        pair,
        (grads,),
        pltpu.with_memory_space_constraint(cotangent, pltpu.HBM),
    )
    projection_part = projection_grad_part(x, low_y, features, gain_row, offset_row, grads)
    devices = 128
    terms, token = gather_terms(
        devices, weight_partial, projection_part, bias_partial, after=tuple(grad_pieces[1:])
    )

    came = lax.all_to_all(terms, AXES, 0, 0, tiled=True)

    def norm_part(first, before, after):
        pieces = grad_pieces[first : first + 2]
        place = lax.rem(x + first, RING)
        return norm_grad(
            place, pieces, features, gain_row, weight_rows, before, after
        )

    alignment_gradient, token = norm_part(0, None, (token,))
    share, spread = add_terms(came, 1.0 / rows_total, after=(token,))
    bias_sum = share[9] + share[10]
    everything = lax.all_to_all(spread, AXES, 0, 0, tiled=True).astype(F32)
    alignment_gradient, _ = norm_part(2, alignment_gradient, (share,))
    weight_sum = (
        everything[:, :8]
        .reshape(width, width, pair_channels)
        .transpose(1, 0, 2)
        .reshape(width * width, pair_channels)
    )
    projection_sum = everything[:, 8].reshape(2 * width, channels).T

    return (
        pair_update_result,
        alignment_gradient,
        projection_sum,
        weight_sum,
        bias_sum,
    )


def solution(mesh):
    in_specs = (P("sa", "ia", None), P(), P(), P(), P(), P(), P(("ia", "sa"), "ja", None))
    out_specs = (P(("ia", "sa"), "ja", None), P("sa", "ia", None), P(), P(), P())
    return jax.shard_map(body, mesh=mesh, in_specs=in_specs, out_specs=out_specs, check_vma=False)
```

```python
import functools

import jax
import jax.numpy as jnp
from jax import lax
from jax.experimental import pallas as pl
from jax.experimental.pallas import tpu as pltpu
from jax.sharding import PartitionSpec as P

epsilon = 1e-05
AXES = ("ia", "ja", "sa")
RING = 4
SWAP_Y = (0, 2, 1, 3)
ROWS_AT_ONCE = 16
BF16 = jnp.bfloat16
F32 = jnp.float32
VMEM_LIMIT = 20 * 1024 * 1024


def dot(a, b, contract):
    return lax.dot_general(a, b, (contract, ((), ())), preferred_element_type=F32)


def params(limit=VMEM_LIMIT):
    return pltpu.CompilerParams(dimension_semantics=("arbitrary",), vmem_limit_bytes=limit)


ANYWHERE = pl.BlockSpec(memory_space=pl.ANY)


def cost(flops, bytes_accessed, transcendentals):
    return pl.CostEstimate(
        flops=flops, bytes_accessed=bytes_accessed, transcendentals=transcendentals
    )


def whole(shape):
    return pl.BlockSpec(shape, lambda *_: (0,) * len(shape))


def row_mean(values):
    channels = values.shape[-1]
    ones = jnp.full((channels, 128), 1.0 / channels, BF16)
    mean = dot(values.astype(BF16), ones, ((1,), (0,)))
    return jnp.concatenate([mean] * (channels // 128), axis=1)


def norm_block(features):
    centred = features.astype(F32) - row_mean(features)
    inverse_deviation = lax.rsqrt(row_mean(centred * centred) + epsilon)
    return centred * inverse_deviation, inverse_deviation


def norm_rows(features):
    values = features.astype(F32)
    scale = 1.0 / values.shape[-1]
    centred = values - jnp.sum(values, axis=-1, keepdims=True) * scale
    variance = jnp.sum(centred * centred, axis=-1, keepdims=True) * scale
    return centred * lax.rsqrt(variance + epsilon)


def project_kernel(place_ref, features_ref, gain_ref, offset_ref, weight_ref, *refs):
    out_ref = refs[-1]
    seqs, residues, channels = features_ref.shape
    at_once = 256 // residues
    for s in range(0, seqs, at_once):
        normed = [
            (norm_rows(features_ref[n, r : r + 64]) * gain_ref[...] + offset_ref[...]).astype(BF16)
            for n in range(s, s + at_once)
            for r in range(0, residues, 64)
        ]
        normed = jnp.concatenate(normed, axis=0)
        several = dot(weight_ref[...], normed, ((1,), (1,))).astype(BF16)
        for n in range(at_once):
            out_ref[s + n] = several[:, n * residues : (n + 1) * residues]


def project(first, count, part, residues, features, gain, offset, weight, after=()):
    total, _, channels = features.shape
    width = weight.shape[0]
    seqs = min(2048 // residues, 16)
    steps = total // seqs

    def place(n, place_ref):
        return (lax.rem(place_ref[0] + n, steps), place_ref[1], 0)

    return pl.pallas_call(
        project_kernel,
        grid_spec=pltpu.PrefetchScalarGridSpec(
            num_scalar_prefetch=1,
            grid=(count // seqs,),
            in_specs=[
                pl.BlockSpec((seqs, residues, channels), place),
                whole((1, channels)),
                whole((1, channels)),
                whole((width, channels)),
            ]
            + [ANYWHERE] * len(after),
            out_specs=pl.BlockSpec((seqs, width, residues), lambda n, place_ref: (n, 0, 0)),
        ),
        out_shape=jax.ShapeDtypeStruct((count, width, residues), BF16),
        compiler_params=params(),
        cost_estimate=cost(
            flops=4 * count * residues * channels * width,
            bytes_accessed=2 * count * residues * (channels + width),
            transcendentals=count * residues,
        ),
        name="project",
    )(jnp.stack([first, part]), features, gain, offset, weight, *after)


def outer_grad_block(cot_ref, weight_ref, grad_ref):
    rows, cols, pair_channels = cot_ref.shape
    width = grad_ref.shape[0]
    for i in range(0, rows, 2):
        cot = cot_ref[i : i + 2].reshape(2 * cols, pair_channels)
        grad = dot(weight_ref[...], cot, ((1,), (1,))).astype(BF16)
        grad = grad.reshape(width, width, 2 * cols)
        grad_ref[:, i * width : (i + 1) * width, :] = grad[:, :, :cols]
        grad_ref[:, (i + 1) * width : (i + 2) * width, :] = grad[:, :, cols:]


def right_grad_kernel(fresh, cot_ref, weight_ref, left_ref, total_in_ref, bias_in_ref, *refs):
    right_ref, total_ref, bias_ref, grad_ref = refs[-4:]
    step = pl.program_id(0)
    rows, cols, pair_channels = cot_ref.shape
    width = grad_ref.shape[0]

    @pl.when(step == 0)
    def _():
        if fresh:
            total_ref[...] = jnp.zeros_like(total_ref)
            bias_ref[...] = jnp.zeros_like(bias_ref)
        else:
            total_ref[...] = total_in_ref[...]
            bias_ref[...] = bias_in_ref[...]

    bias_ref[...] += jnp.sum(
        cot_ref[...].astype(F32).reshape(rows * cols // 8, 8, pair_channels), axis=0
    )
    outer_grad_block(cot_ref, weight_ref, grad_ref)
    left = left_ref[...].T
    for d in range(0, width, 2):
        both = jnp.concatenate([grad_ref[d], grad_ref[d + 1]], axis=1)
        total_ref[:, d * cols : (d + 2) * cols] += dot(left, both, ((1,), (0,)))

    if not fresh:

        @pl.when(step == pl.num_programs(0) - 1)
        def _():
            right_ref[...] = total_ref[...].astype(BF16)


def right_grad_part(first, count, cotangent, weight, left, before, after=()):
    rows, cols, pair_channels = cotangent.shape
    seqs = left.shape[1]
    width = left.shape[0] // rows
    block = ROWS_AT_ONCE * width
    fresh = before is None
    if fresh:
        before = (None, jnp.zeros((8, pair_channels), F32), jnp.zeros((8, pair_channels), F32))
    right_shape = (8, pair_channels) if fresh else (seqs, width * cols)
    return pl.pallas_call(
        functools.partial(right_grad_kernel, fresh),
        grid=(count,),
        in_specs=[
            pl.BlockSpec((ROWS_AT_ONCE, cols, pair_channels), lambda n: (first + n, 0, 0)),
            whole((width * width, pair_channels)),
            pl.BlockSpec((block, seqs), lambda n: (first + n, 0)),
            whole(before[1].shape),
            whole(before[2].shape),
        ]
        + [ANYWHERE] * len(after),
        out_specs=[
            whole(right_shape),
            whole((seqs, width * cols)),
            whole((8, pair_channels)),
        ],
        out_shape=[
            jax.ShapeDtypeStruct(right_shape, BF16),
            jax.ShapeDtypeStruct((seqs, width * cols), F32),
            jax.ShapeDtypeStruct((8, pair_channels), F32),
        ],
        scratch_shapes=[pltpu.VMEM((width, block, cols), BF16)],
        compiler_params=params(),
        cost_estimate=cost(
            flops=4 * count * ROWS_AT_ONCE * cols * width * width * pair_channels,
            bytes_accessed=2 * count * ROWS_AT_ONCE * cols * pair_channels,
            transcendentals=0,
        ),
        name="right_grad",
    )(cotangent, weight, left, before[1], before[2], *after)


def left_grad_kernel(turn_ref, *refs):
    piece_refs, (cot_ref, weight_ref, out_ref, cols_ref, grad_ref) = refs[: 2 * RING], refs[-5:]
    width, _, cols = grad_ref.shape
    quarter = piece_refs[0].shape[0]

    @pl.when(pl.program_id(0) == 0)
    def _():
        for d in range(width):
            here = slice(d * cols, (d + 1) * cols)
            part = jnp.concatenate([piece[:, here] for piece in piece_refs], axis=0)
            cols_ref[here, :] = part.T

    outer_grad_block(cot_ref, weight_ref, grad_ref)
    block = 8 * width
    for first_row in range(0, grad_ref.shape[1], block):
        here = slice(first_row, first_row + block)
        total = None
        for d in range(0, width, 2):
            both = jnp.concatenate([grad_ref[d, here], grad_ref[d + 1, here]], axis=1)
            term = dot(both, cols_ref[d * cols : (d + 2) * cols, :], ((1,), (0,)))
            total = term if total is None else total + term
        total = total.T.astype(BF16)
        for p in range(RING):
            place = lax.rem(turn_ref[0] + p, RING)
            for h in range(2):
                first = (h * RING + p) * quarter
                out_ref[place, h * quarter : (h + 1) * quarter, here] = total[
                    first : first + quarter
                ]


def left_grad_part(turn, pieces, cotangent, weight, after=()):
    rows, cols, pair_channels = cotangent.shape
    quarter = pieces[0].shape[0]
    width = pieces[0].shape[1] // cols
    blocks, block = rows // ROWS_AT_ONCE, ROWS_AT_ONCE * width
    seqs = 2 * RING * quarter
    return pl.pallas_call(
        left_grad_kernel,
        grid_spec=pltpu.PrefetchScalarGridSpec(
            num_scalar_prefetch=1,
            grid=(blocks,),
            in_specs=[whole(piece.shape) for piece in pieces]
            + [ANYWHERE] * len(after)
            + [
                pl.BlockSpec((ROWS_AT_ONCE, cols, pair_channels), lambda n, turn_ref: (n, 0, 0)),
                whole((width * width, pair_channels)),
            ],
            out_specs=pl.BlockSpec((RING, 2 * quarter, block), lambda n, turn_ref: (0, 0, n)),
            scratch_shapes=[
                pltpu.VMEM((width * cols, seqs), BF16),
                pltpu.VMEM((width, block, cols), BF16),
            ],
        ),
        out_shape=jax.ShapeDtypeStruct((RING, 2 * quarter, blocks * block), BF16),
        compiler_params=params(),
        cost_estimate=cost(
            flops=4 * blocks * width * block * cols * (seqs + pair_channels),
            bytes_accessed=4 * seqs * width * cols,
            transcendentals=0,
        ),
        name="left_grad",
    )(
        turn.reshape(1),
        *pieces,
        *after,
        cotangent,
        weight,
    )


def add_kernel(count, scale, *refs):
    total = refs[0][...].astype(F32)
    for ref in refs[1:count]:
        total = total + ref[...].astype(F32)
    refs[-1][...] = (total * scale).astype(BF16)


def add_up(parts, scale=1.0, after=()):
    return pl.pallas_call(
        lambda *refs: add_kernel(len(parts), scale, *refs),
        in_specs=[pl.BlockSpec(memory_space=pltpu.VMEM)] * len(parts) + [ANYWHERE] * len(after),
        out_specs=pl.BlockSpec(memory_space=pltpu.VMEM),
        out_shape=jax.ShapeDtypeStruct(parts[0].shape, BF16),
        compiler_params=pltpu.CompilerParams(vmem_limit_bytes=VMEM_LIMIT),
        name="add_up",
    )(*parts, *after)


def pair_kernel(fresh, *refs):
    piece_refs, refs = refs[: 2 * RING], refs[2 * RING :]
    left_ref, weight_ref, bias_ref, cot_ref, before_ref = refs[:5]
    pair_ref, total_ref, cols_ref, outer_ref = refs[-4:]
    rows, cols, pair_channels = cot_ref.shape
    width = outer_ref.shape[0]
    inv_seqs = 1.0 / cols_ref.shape[0]

    @pl.when(pl.program_id(0) == 0)
    def _():
        first = 0
        for piece in piece_refs:
            cols_ref[first : first + piece.shape[0], :] = piece[...]
            first += piece.shape[0]
        total_ref[...] = jnp.zeros_like(total_ref) if fresh else before_ref[...]

    for d in range(0, width, 2):
        both = dot(left_ref[...], cols_ref[:, d * cols : (d + 2) * cols], ((1,), (0,)))
        both = (both * inv_seqs).astype(BF16)
        outer_ref[d] = both[:, :cols]
        outer_ref[d + 1] = both[:, cols:]
    for i in range(0, rows, 2):
        outer = jnp.concatenate(
            [
                outer_ref[:, n * width : (n + 1) * width, :].reshape(width * width, cols)
                for n in (i, i + 1)
            ],
            axis=1,
        )
        cot = cot_ref[i : i + 2].reshape(2 * cols, pair_channels)
        total_ref[...] += dot(outer, cot, ((1,), (0,)))
        pair = dot(weight_ref[...], outer, ((1,), (0,))).T + bias_ref[...]
        pair_ref[i : i + 2] = pair.astype(BF16).reshape(2, cols, pair_channels)


def pair_and_weight_grad(first, count, pieces, left, weight, bias, cotangent, before, after=()):
    rows, cols, pair_channels = cotangent.shape
    seqs = left.shape[1]
    width = left.shape[0] // rows
    block = ROWS_AT_ONCE * width
    fresh = before is None
    if fresh:
        before = (None, jnp.zeros((8, pair_channels), F32))
    operands = [*pieces, left, weight, bias.reshape(1, -1), cotangent, before[1], *after]
    in_specs = [whole(piece.shape) for piece in pieces] + [
        pl.BlockSpec((block, seqs), lambda n: (first + n, 0)),
        whole((pair_channels, width * width)),
        whole((1, pair_channels)),
        pl.BlockSpec((ROWS_AT_ONCE, cols, pair_channels), lambda n: (first + n, 0, 0)),
        whole(before[1].shape),
    ]
    in_specs += [ANYWHERE] * len(after)
    aliases = {}
    if not fresh:
        aliases = {len(operands): 0}
        operands.append(before[0])
        in_specs.append(ANYWHERE)
    return pl.pallas_call(
        functools.partial(pair_kernel, fresh),
        grid=(count,),
        in_specs=in_specs,
        out_specs=[
            pl.BlockSpec((ROWS_AT_ONCE, cols, pair_channels), lambda n: (first + n, 0, 0)),
            whole((width * width, pair_channels)),
        ],
        out_shape=[
            jax.ShapeDtypeStruct((rows, cols, pair_channels), BF16),
            jax.ShapeDtypeStruct((width * width, pair_channels), F32),
        ],
        scratch_shapes=[
            pltpu.VMEM((seqs, width * cols), BF16),
            pltpu.VMEM((width, block, cols), BF16),
        ],
        input_output_aliases=aliases,
        compiler_params=params(),
        cost_estimate=cost(
            flops=4 * count * ROWS_AT_ONCE * cols * width * width * (2 * pair_channels + seqs),
            bytes_accessed=4 * count * ROWS_AT_ONCE * cols * pair_channels,
            transcendentals=0,
        ),
        name="pair_update",
    )(*operands)


def projection_grad_kernel(place_ref, features_ref, gain_ref, offset_ref, grads_ref, out_ref):
    seqs = features_ref.shape[0]
    total = None
    for s in range(seqs):
        rescaled = norm_rows(features_ref[s])
        normed = (rescaled * gain_ref[...] + offset_ref[...]).astype(BF16)
        term = dot(grads_ref[s], normed, ((1,), (0,)))
        total = term if total is None else total + term
    out_ref[...] = total


def projection_grad_part(x, low_y, features, gain, offset, grads):
    _, residues, channels = features.shape
    quarter, both_widths, _ = grads.shape
    eighth = quarter // 2
    place = jnp.stack([x * 2 + low_y, low_y])
    return pl.pallas_call(
        projection_grad_kernel,
        grid_spec=pltpu.PrefetchScalarGridSpec(
            num_scalar_prefetch=1,
            grid=(1,),
            in_specs=[
                pl.BlockSpec((eighth, residues, channels), lambda n, ref: (ref[0], 0, 0)),
                whole((1, channels)),
                whole((1, channels)),
                pl.BlockSpec((eighth, both_widths, residues), lambda n, ref: (ref[1], 0, 0)),
            ],
            out_specs=whole((both_widths, channels)),
        ),
        out_shape=jax.ShapeDtypeStruct((both_widths, channels), F32),
        compiler_params=params(),
        name="projection_grad",
    )(place, features, gain, offset, grads)


def norm_grad_kernel(count, first_ref, features_ref, gain_ref, weight_ref, *refs):
    piece_refs, (out_ref, token_ref, grads_ref) = refs[:count], refs[-3:]
    token_ref[...] = jnp.zeros_like(token_ref)
    step = pl.program_id(0)
    seqs, residues, channels = features_ref.shape
    steps = piece_refs[0].shape[0] // seqs
    for t in range(len(piece_refs)):

        @pl.when(step // steps == t)
        def _(t=t):
            grads_ref[...] = piece_refs[t][pl.ds(lax.rem(step, steps) * seqs, seqs)]

    at_once = 4
    for s in range(0, seqs, at_once):
        features = features_ref[s : s + at_once].reshape(at_once * residues, channels)
        rescaled, inverse_deviation = norm_block(features)
        grad = [dot(grads_ref[s + n], weight_ref[...], ((0,), (0,))) for n in range(at_once)]
        grad = jnp.concatenate(grad, axis=0) * gain_ref[...]
        grad = inverse_deviation * (grad - row_mean(grad) - rescaled * row_mean(grad * rescaled))
        out_ref[s : s + at_once] = grad.astype(BF16).reshape(at_once, residues, channels)


def norm_grad(first, pieces, features, gain, weight, before=None, after=()):
    _, residues, channels = features.shape
    quarter, both_widths, _ = pieces[0].shape
    seqs = quarter
    steps = 1

    def place(n, first_ref):
        return (lax.rem(n // steps + first_ref[0], RING) * steps + lax.rem(n, steps), 0, 0)

    operands = [first.reshape(1), features, gain, weight, *pieces, *after]
    in_specs = [
        pl.BlockSpec((seqs, residues, channels), place),
        whole((1, channels)),
        whole(weight.shape),
    ]
    in_specs += [whole(piece.shape) for piece in pieces] + [ANYWHERE] * len(after)
    aliases = {}
    if before is not None:
        aliases = {len(operands): 0}
        operands.append(before)
        in_specs.append(ANYWHERE)
    return pl.pallas_call(
        functools.partial(norm_grad_kernel, len(pieces)),
        grid_spec=pltpu.PrefetchScalarGridSpec(
            num_scalar_prefetch=1,
            grid=(len(pieces) * steps,),
            in_specs=in_specs,
            out_specs=[pl.BlockSpec((seqs, residues, channels), place), whole((8, 128))],
            scratch_shapes=[pltpu.VMEM((seqs, both_widths, residues), BF16)],
        ),
        out_shape=[
            jax.ShapeDtypeStruct(features.shape, BF16),
            jax.ShapeDtypeStruct((8, 128), F32),
        ],
        input_output_aliases=aliases,
        compiler_params=params(),
        cost_estimate=cost(
            flops=4 * len(pieces) * quarter * residues * channels * both_widths,
            bytes_accessed=4 * len(pieces) * quarter * residues * channels,
            transcendentals=0,
        ),
        name="norm_grad",
    )(*operands)


def share_kernel(scale, terms_ref, *refs):
    share_ref, spread_ref = refs[-2:]
    total = terms_ref[0].astype(F32)
    for n in range(1, terms_ref.shape[0]):
        total = total + terms_ref[n].astype(F32)
    total = total * scale
    share_ref[...] = total
    spread_ref[...] = jnp.broadcast_to(total.astype(BF16), spread_ref.shape)


def add_terms(terms, scale, after=()):
    return pl.pallas_call(
        functools.partial(share_kernel, scale),
        in_specs=[pl.BlockSpec(memory_space=pltpu.VMEM)] + [ANYWHERE] * len(after),
        out_specs=[pl.BlockSpec(memory_space=pltpu.VMEM)] * 2,
        out_shape=[
            jax.ShapeDtypeStruct(terms.shape[1:], F32),
            jax.ShapeDtypeStruct(terms.shape, BF16),
        ],
        compiler_params=pltpu.CompilerParams(vmem_limit_bytes=VMEM_LIMIT),
        name="add_terms",
    )(terms, *after)


def terms_kernel(weight_ref, projection_ref, bias_ref, *refs):
    out_ref, token_ref = refs[-2:]
    token_ref[...] = jnp.zeros_like(token_ref)
    devices, rows, lanes = out_ref.shape
    weight_rows = weight_ref.shape[0] // devices
    bias = jnp.sum(bias_ref[...], axis=0, keepdims=True)
    bias_high = bias.astype(BF16).astype(F32)
    tail = jnp.concatenate(
        [bias_high, bias - bias_high, jnp.zeros((rows - weight_rows - 3, lanes), F32)], axis=0
    )
    for n in range(devices):
        block = [
            weight_ref[n * weight_rows : (n + 1) * weight_rows, :],
            projection_ref[n : n + 1, :],
            tail,
        ]
        out_ref[n] = jnp.concatenate(block, axis=0).astype(BF16)


def gather_terms(devices, weight_part, projection_part, bias_part, after=()):
    lanes = weight_part.shape[1]
    return pl.pallas_call(
        terms_kernel,
        in_specs=[pl.BlockSpec(memory_space=pltpu.VMEM)] * 3 + [ANYWHERE] * len(after),
        out_specs=[pl.BlockSpec(memory_space=pltpu.VMEM)] * 2,
        out_shape=[
            jax.ShapeDtypeStruct((devices, 16, lanes), BF16),
            jax.ShapeDtypeStruct((8, lanes), F32),
        ],
        compiler_params=pltpu.CompilerParams(vmem_limit_bytes=VMEM_LIMIT),
        name="gather_terms",
    )(weight_part, projection_part.reshape(devices, lanes), bias_part, *after)


def torus_permute(value, move):
    pairs = []
    for z in range(RING):
        for y in range(RING):
            for x in range(RING):
                for s in range(2):
                    tx, ty, tz, ts = move(x, y, z, s)
                    tx, ty, tz = tx % RING, ty % RING, tz % RING
                    source = ((z * 2 + y // 2) * 8 + x * 2 + y % 2) * 2 + s
                    target = ((tz * 2 + ty // 2) * 8 + tx * 2 + ty % 2) * 2 + ts
                    pairs.append((source, target))
    return lax.ppermute(value, AXES, pairs)


def swap_cores(value):
    return torus_permute(value, lambda x, y, z, s: (x, y, z, 1 - s))


def swap_low_y(value):
    return torus_permute(value, lambda x, y, z, s: (x, y ^ 1, z, s))


def swap_both(value):
    return torus_permute(value, lambda x, y, z, s: (x, y ^ 1, z, 1 - s))


def shift_z(value, steps):
    return torus_permute(value, lambda x, y, z, s: (x, y, z + steps, s))


def shift_x(value, steps):
    return torus_permute(value, lambda x, y, z, s: (x + steps, y, z, s))


def transpose_xz(value):
    return torus_permute(value, lambda x, y, z, s: (z, SWAP_Y[y], x, s))


def body(
    alignment_features,
    norm_gain_vector,
    norm_offset_vector,
    projection_weight,
    output_weight,
    output_bias,
    pair_update_cotangent,
):
    half, residues, channels = alignment_features.shape
    width = projection_weight.shape[1] // 2
    pair_channels = output_weight.shape[1]
    rows, cols, _ = pair_update_cotangent.shape
    rows_total = residues * lax.axis_size("ia")
    quarter = half // RING
    inv_seqs = 1.0 / (half * 2)
    x = lax.axis_index("ja") // 2
    low_y = lax.axis_index("ja") % 2
    z = lax.axis_index("ia") // 2
    core = lax.axis_index("sa")
    features = pltpu.with_memory_space_constraint(alignment_features, pltpu.HBM)
    cotangent = pair_update_cotangent
    gain_row = norm_gain_vector.reshape(1, -1)
    offset_row = norm_offset_vector.reshape(1, -1)
    weight_rows = projection_weight.T

    right_piece = project(
        x,
        quarter,
        x * 0,
        residues,
        features,
        pltpu.with_memory_space_constraint(gain_row, pltpu.HBM),
        pltpu.with_memory_space_constraint(offset_row, pltpu.HBM),
        weight_rows[width:],
    )
    arrived = transpose_xz(right_piece.reshape(quarter, width * residues))

    def left_rows(part):
        return project(
            z,
            half,
            part,
            rows,
            alignment_features,
            gain_row,
            offset_row,
            weight_rows[:width],
            after=(right_piece,),
        )

    left_came = swap_cores(left_rows(1 - core)).transpose(2, 1, 0)
    left_kept = left_rows(core).transpose(2, 1, 0)
    own_left = jnp.concatenate([left_kept, left_came], axis=2).reshape(rows * width, 2 * half)

    arrived = add_up([arrived], after=(own_left,))
    right_pieces = [arrived] + [shift_z(arrived, -t) for t in range(1, RING)]
    right_cols = right_pieces + [swap_cores(piece) for piece in right_pieces]

    weight_dc = (
        output_weight.reshape(width, width, pair_channels)
        .transpose(1, 0, 2)
        .reshape(width * width, pair_channels)
    )
    blocks = rows // ROWS_AT_ONCE
    part = right_grad_part(
        0, blocks // 2, cotangent, weight_dc, own_left, None, after=(arrived,)
    )
    right_partial, _, bias_partial = right_grad_part(
        blocks // 2,
        blocks // 2,
        cotangent,
        weight_dc,
        own_left,
        part,
        after=tuple(right_pieces[1:]),
    )

    right_sum = add_up([right_partial[:half], swap_cores(right_partial[half:])])
    pieces = [right_sum[t * quarter : (t + 1) * quarter] for t in range(RING)]
    right_came = [shift_z(pieces[t], t) for t in range(1, RING)]
    left_partial = left_grad_part(
        lax.rem(z - x + RING, RING),
        right_cols,
        cotangent,
        weight_dc,
        after=(right_sum,),
    )

    left_came = [shift_x(left_partial[t], t) for t in range(1, RING)]
    right_sum = transpose_xz(add_up([pieces[0], *right_came], after=(left_partial,)))

    def pair_part(first, count, before, after, cotangent=cotangent):
        return pair_and_weight_grad(
            first,
            count,
            right_cols,
            own_left,
            weight_dc.T,
            output_bias,
            cotangent,
            before,
            after,
        )

    pair = pair_part(0, blocks // 2, None, (left_partial,))
    left_sum = add_up([left_partial[0], *left_came], after=(pair[1],))

    left_own, left_other = left_sum[:quarter], left_sum[quarter:]
    own_beside, right_beside = swap_low_y(left_own), swap_low_y(right_sum)
    other_here, other_beside = swap_cores(left_other), swap_both(left_other)
    pair = pair_part(blocks // 2, blocks // 4, pair, (left_sum,))
    left_own = add_up([left_own, own_beside], inv_seqs, after=(pair[1],))
    left_came = add_up([other_here, other_beside], inv_seqs, after=(pair[1],))
    right_grad = add_up([right_sum, right_beside], inv_seqs, after=(pair[1],))

    left_low = jnp.where(core == 0, left_own, left_came).reshape(quarter, rows, width)
    left_high = jnp.where(core == 0, left_came, left_own).reshape(quarter, rows, width)
    left_grad = jnp.concatenate(
        [left_low.transpose(0, 2, 1), left_high.transpose(0, 2, 1)], axis=2
    )
    grads = jnp.concatenate([left_grad, right_grad.reshape(quarter, width, residues)], axis=1)
    grad_pieces = [grads] + [shift_x(grads, -t) for t in range(1, RING)]

    pair_update_result, weight_partial = pair_part(
        blocks - blocks // 4,
        blocks // 4,
        pair,
        (grads,),
        pltpu.with_memory_space_constraint(cotangent, pltpu.HBM),
    )
    projection_part = projection_grad_part(x, low_y, features, gain_row, offset_row, grads)
    devices = 128
    terms, token = gather_terms(
        devices, weight_partial, projection_part, bias_partial, after=tuple(grad_pieces[1:])
    )

    came = lax.all_to_all(terms, AXES, 0, 0, tiled=True)

    def norm_part(first, before, after):
        pieces = grad_pieces[first : first + 2]
        place = lax.rem(x + first, RING)
        return norm_grad(
            place, pieces, features, gain_row, weight_rows, before, after
        )

    alignment_gradient, token = norm_part(0, None, (token,))
    share, spread = add_terms(came, 1.0 / rows_total, after=(token,))
    bias_sum = share[9] + share[10]
    everything = lax.all_to_all(spread, AXES, 0, 0, tiled=True).astype(F32)
    alignment_gradient, _ = norm_part(2, alignment_gradient, (share,))
    weight_sum = (
        everything[:, :8]
        .reshape(width, width, pair_channels)
        .transpose(1, 0, 2)
        .reshape(width * width, pair_channels)
    )
    projection_sum = everything[:, 8].reshape(2 * width, channels).T

    return (
        pair_update_result,
        alignment_gradient,
        projection_sum,
        weight_sum,
        bias_sum,
    )


def solution(mesh):
    in_specs = (P("sa", "ia", None), P(), P(), P(), P(), P(), P(("ia", "sa"), "ja", None))
    out_specs = (P(("ia", "sa"), "ja", None), P("sa", "ia", None), P(), P(), P())
    return jax.shard_map(body, mesh=mesh, in_specs=in_specs, out_specs=out_specs, check_vma=False)
```
